32 devices in a mesh: dp: 4 (over x, core), fsdp: 8 (over z, y).
Axes of the slice: x: 2, y: 2, z: 4, core: 2. Of those that a mesh axis runs over, the one named last changes fastest.
Arguments:
- prompt_ids: int32 [64, 192], P(('dp', 'fsdp')), may hold values from 0 to 32127
- prompt_lengths: int32 [64], P(('dp', 'fsdp')), may hold values from 1 to 192, 9216 in all
- response_ids: int32 [128, 32], P(('dp', 'fsdp')), may hold values from 0 to 32127
- response_lengths: int32 [128], P(('dp', 'fsdp')), may hold values from 1 to 32
- sequence_pair: int32 [128], P(('dp', 'fsdp')), may hold values from 0 to 63, as said below
- chosen_flag: int32 [128], P(('dp', 'fsdp')), may hold values from 0 to 1, as said below
- pair_microbatch: int32 [64], P(('dp', 'fsdp')), may hold values from 0 to 1
- policy_embed: float32 [32128, 1024], P(('dp', 'fsdp')), may hold values from -6 to 6
- policy_layers: float32 [1024, 28672], P(('dp', 'fsdp')), may hold values from -0.1875 to 0.1875
- policy_gains: float32 [7, 1024], replicated, may hold values from 0.5 to 1.5
- momentum_embed: float32 [32128, 1024], P(('dp', 'fsdp')), may hold values from -7.6293945e-06 to 7.6293945e-06
- momentum_layers: float32 [1024, 28672], P(('dp', 'fsdp')), may hold values from -0.00015258789 to 0.00015258789
- momentum_gains: float32 [7, 1024], replicated, may hold values from -0.00015258789 to 0.00015258789
- average_embed: float32 [32128, 1024], P(('dp', 'fsdp')), may hold values from -6 to 6
- average_layers: float32 [1024, 28672], P(('dp', 'fsdp')), may hold values from -0.1875 to 0.1875
- average_gains: float32 [7, 1024], replicated, may hold values from 0.5 to 1.5
- frozen_embed: bfloat16 [32128, 1024], P(('dp', 'fsdp')), may hold values from -6 to 6
- frozen_layers: bfloat16 [1024, 28672], P(('dp', 'fsdp')), may hold values from -0.1875 to 0.1875
- frozen_gains: float32 [7, 1024], replicated, may hold values from 0.5 to 1.5
Outputs:
- loss: float32 [], replicated
- grad_norm: float32 [], replicated
- micro_counts: float32 [2, 2], replicated
- frozen_mean: float32 [128], P(('dp', 'fsdp'))
- step_embed: float32 [32128, 1024], P(('dp', 'fsdp'))
- next_layers: float32 [1024, 28672], P(('dp', 'fsdp'))
- next_gains: float32 [7, 1024], replicated
- moment_embed: float32 [32128, 1024], P(('dp', 'fsdp'))
- moment_layers: float32 [1024, 28672], P(('dp', 'fsdp'))
- moment_gains: float32 [7, 1024], replicated
- smooth_embed: float32 [32128, 1024], P(('dp', 'fsdp'))
- smooth_layers: float32 [1024, 28672], P(('dp', 'fsdp'))
- smooth_gains: float32 [7, 1024], replicated
The draws below stay inside these ranges and needn't reach their ends.
Inputs may be any that keep to these rules, and one draw needn't show every extreme that they name: `sequence_pair`: each pair id names exactly two sequences; the sequences of pairs 2 * i to 2 * i + 1 are the rows 2 * 2 * i to 2 * 2 * i + 2 * 2 - 1. `chosen_flag`: of the two sequences of a pair exactly one has flag 1.
All inputs are finite; a program needn't handle non-finite values. No bound on the sum of `prompt_lengths` on one device may be relied on, other than what follows from the above.
Results may differ from the reference program's by a relative error of at most 0.008.
Values may be sent and summed in bfloat16 or wider, within the bound.
A program may use at most 704 MiB of HBM per device.

```python
import math
import jax
import jax.numpy as jnp
import numpy as np
from jax import lax

D = 1024
HEADS = 16
HEAD = 64
FF = 4096
VOCAB = 32128
PAIRS_DEV = 2
P_MAX = 192
R_MAX = 32
MICRO = 2
LAYER_COLS = 28672
PAIRS = 64
SEQS = 128


def pairing(key):
    device_groups = PAIRS // PAIRS_DEV
    seat_count = 2 * PAIRS_DEV
    base_bits = jax.random.randint(jax.random.fold_in(key, 7), (device_groups, seat_count), 0, 1 << 20)
    scores = base_bits * seat_count + jnp.arange(seat_count)[None, :]
    ordering = jnp.argsort(scores, axis=1, stable=True)
    ranking = jnp.argsort(ordering, axis=1, stable=True)
    flips = jax.random.randint(jax.random.fold_in(key, 11), (device_groups, PAIRS_DEV), 0, 2)
    pair_local = ranking // 2
    owners = jnp.arange(device_groups)[:, None] * PAIRS_DEV + pair_local
    flags = (ranking % 2 + jnp.take_along_axis(flips, pair_local, axis=1)) % 2
    return (owners.reshape(-1).astype(jnp.int32), flags.reshape(-1).astype(jnp.int32))


def draw_sequence_pair(key, part):
    return pairing(key)[0]


def draw_chosen_flag(key, part):
    return pairing(key)[1]


def draw_response_lengths(key, part):
    device_groups = PAIRS // PAIRS_DEV
    seat_count = 2 * PAIRS_DEV
    group_index = jnp.arange(SEQS, dtype=jnp.int32) // seat_count
    base_cap = R_MAX // 4
    caps = base_cap + (R_MAX - base_cap) * group_index // max(device_groups - 1, 1)
    bits = jax.random.randint(jax.random.fold_in(key, 23), (SEQS,), 0, 1 << 20)
    lengths = bits % caps + 1
    last_first = (device_groups - 1) * seat_count
    lengths = jnp.where(jnp.arange(SEQS) == last_first, R_MAX, lengths)
    return lengths.astype(jnp.int32)


def shared_table(key):
    hub_total = min(64, VOCAB // 4)
    signs = jnp.where(jax.random.randint(jax.random.fold_in(key, 1), (D,), 0, 2) == 1, 1.0, -1.0).astype(jnp.float32)
    order = jax.random.permutation(jax.random.fold_in(key, 2), VOCAB)
    marked = (order < hub_total).astype(jnp.float32)
    noise = jax.random.normal(jax.random.fold_in(key, 3), (VOCAB, D), jnp.float32)
    lift = 1.0 + 2.0 * marked
    return jnp.clip(noise + lift[:, None] * signs[None, :], -6.0, 6.0)


def draw_policy_embed(key, part):
    key = jax.random.fold_in(key, 31)
    return shared_table(key)


def draw_frozen_embed(key, part):
    key = jax.random.fold_in(key, 37)
    return shared_table(key).astype(jnp.bfloat16)


def place_ends(values, own_key, smallest, largest):
    dims = values.shape
    spot = [jax.random.randint(jax.random.fold_in(own_key, axis), (), 0, dims[axis]) for axis in range(len(dims))]
    values = values.at[tuple(spot)].set(smallest)
    longest = dims.index(max(dims))
    spot[longest] = (spot[longest] + 1) % dims[longest]
    return values.at[tuple(spot)].set(largest)


def level_of(rng, dims, pieces, smallest, largest):
    level = 1.0
    for dim, blocks in pieces:
        steps = jax.random.uniform(jax.random.fold_in(jax.random.fold_in(rng, 6), dim), (blocks,), jnp.float32, smallest / len(pieces), largest / len(pieces))
        level = level * jnp.repeat(jnp.exp(steps), dims[dim] // blocks).reshape((-1,) + (1,) * (len(dims) - 1 - dim))
    return level


def rank_bounds(number_of, slope):
    loads = [(1 << 20) // math.isqrt(rank ** slope) + 1 for rank in range(1, number_of + 1)]
    spread = 1 + sum(loads) // (1 << 30)
    return np.cumsum(np.array([max(1, weight // spread) for weight in loads]))


def skewed_ids(key, shape, count, lean):
    listing = rank_bounds(count, lean)
    ticket = jax.random.randint(jax.random.fold_in(key, 1), shape, 0, int(listing[count - 1]))
    rank = jnp.searchsorted(jnp.asarray(listing, jnp.int32), ticket, side="right")
    return jax.random.permutation(jax.random.fold_in(key, 2), count)[rank].astype(jnp.int32)


def length_profile(count, total, reach, skew):
    portions = [(1 << 20) // math.isqrt(grade ** skew) + 1 for grade in range(2, count + 1)]
    surplus, holding = total - reach - (count - 1), [1] * (count - 1)
    while surplus > 0:
        movable = [i for i in range(count - 1) if holding[i] < reach]
        pool, remaining = sum([portions[i] for i in movable]), surplus
        for i in movable:
            more = min(reach - holding[i], max(1, remaining * portions[i] // pool), surplus)
            holding[i] = holding[i] + more
            surplus = surplus - more
    return np.array([reach] + holding)


def ragged(own_key, number_of, total, most, lean):
    if number_of == 2:
        one = jax.random.randint(own_key, (), max(1, total - most), min(most, total - 1) + 1)
        return jnp.stack([one, total - one])
    tallies = jnp.asarray(length_profile(number_of, total, most, lean), jnp.int32)
    pairs = (number_of - 1) // 2
    donor, taker = tallies[1:1 + 2 * pairs:2], tallies[2:2 + 2 * pairs:2]
    slack = jnp.minimum(donor - 1, most - taker)
    shifted = jax.random.randint(jax.random.fold_in(own_key, 1), (pairs,), 0, 1 << 20) % (slack + 1)
    tallies = tallies.at[1:1 + 2 * pairs:2].set(donor - shifted).at[2:2 + 2 * pairs:2].set(taker + shifted)
    return tallies[jax.random.permutation(jax.random.fold_in(own_key, 2), number_of)]


def bell_draw(own_key, shape, deviation, limit, split=(), held_as=jnp.bfloat16):
    array = deviation * jax.random.normal(own_key, shape, jnp.float32)
    if split:
        array = array * level_of(own_key, shape, split, -0.22, 0.18)
    return jnp.clip(array, -limit, limit).astype(held_as)


def setup_inputs(seed: int = 0) -> dict:
    splits = jax.random.split(jax.random.key(seed), 20)
    prompt_ids = place_ends(skewed_ids(splits[0], (PAIRS, P_MAX), VOCAB, 2), jax.random.fold_in(splits[0], 3), 0, VOCAB - 1).astype(jnp.int32)
    prompt_lengths = ragged(splits[1], PAIRS, 3 * PAIRS * P_MAX // 4, P_MAX, 2).astype(jnp.int32)
    response_ids = place_ends(skewed_ids(splits[2], (SEQS, R_MAX), VOCAB, 2), jax.random.fold_in(splits[2], 3), 0, VOCAB - 1).astype(jnp.int32)
    response_lengths = draw_response_lengths(jax.random.fold_in(splits[19], 71), 0)
    sequence_pair = draw_sequence_pair(jax.random.fold_in(splits[19], 71), 0)
    chosen_flag = draw_chosen_flag(jax.random.fold_in(splits[19], 71), 0)
    pair_microbatch = place_ends(jax.random.randint(splits[6], (PAIRS,), 0, MICRO), jax.random.fold_in(splits[6], 1), 0, MICRO - 1).astype(jnp.int32)
    policy_embed = draw_policy_embed(jax.random.fold_in(splits[19], 71), 0)
    policy_layers = bell_draw(splits[8], (D, LAYER_COLS), D ** -0.5, 0.1875, ((0, 32),), jnp.float32)
    policy_gains = jnp.clip(1.0 + 0.1 * jax.random.normal(splits[9], (7, D), jnp.float32), 0.5, 1.5)
    momentum_embed = bell_draw(splits[10], (VOCAB, D), 0.0000005, 7.62939453125e-06, ((0, 32),), jnp.float32)
    momentum_layers = bell_draw(splits[11], (D, LAYER_COLS), 0.00001, 0.00015258789, ((0, 32),), jnp.float32)
    momentum_gains = bell_draw(splits[12], (7, D), 0.00001, 0.00015258789, (), jnp.float32)
    average_embed = bell_draw(splits[13], (VOCAB, D), 1.0, 6.0, ((0, 32),), jnp.float32)
    average_layers = bell_draw(splits[14], (D, LAYER_COLS), D ** -0.5, 0.1875, ((0, 32),), jnp.float32)
    average_gains = jnp.clip(1.0 + 0.1 * jax.random.normal(splits[15], (7, D), jnp.float32), 0.5, 1.5)
    frozen_embed = draw_frozen_embed(jax.random.fold_in(splits[19], 71), 0)
    frozen_layers = bell_draw(splits[17], (D, LAYER_COLS), D ** -0.5, 0.1875, ((0, 32),))
    frozen_gains = jnp.clip(1.0 + 0.1 * jax.random.normal(splits[18], (7, D), jnp.float32), 0.5, 1.5)
    return dict(prompt_ids=prompt_ids, prompt_lengths=prompt_lengths, response_ids=response_ids, response_lengths=response_lengths, sequence_pair=sequence_pair, chosen_flag=chosen_flag, pair_microbatch=pair_microbatch, policy_embed=policy_embed, policy_layers=policy_layers, policy_gains=policy_gains, momentum_embed=momentum_embed, momentum_layers=momentum_layers, momentum_gains=momentum_gains, average_embed=average_embed, average_layers=average_layers, average_gains=average_gains, frozen_embed=frozen_embed, frozen_layers=frozen_layers, frozen_gains=frozen_gains)


EPSILON = 1e-06
SCORE_SCALE = 0.125
PREFERENCE_BETA = 0.1
CHOSEN_WEIGHT = 1.0
MOMENTUM = 0.9
LEARN_RATE = 2000.0
AVERAGE_DECAY = 0.5
CLIP_NORM = 0.04
MASK_FILL = -1000000000.0
HIGHEST = lax.Precision.HIGHEST

@jax.custom_vjp
def low(v):
    return lax.optimization_barrier(v.astype(jnp.bfloat16)).astype(jnp.float32)

@jax.custom_vjp
def low_back(v):
    return v

def low_keep(v):
    return (low(v), None)

def low_pass(kept, grad):
    return (grad,)

def back_keep(v):
    return (v, None)

def back_low(kept, grad):
    return (low(grad),)
low.defvjp(low_keep, low_pass)
low_back.defvjp(back_keep, back_low)

def rms_norm(values, gain_row):
    return values * lax.rsqrt(lax.optimization_barrier(jnp.mean(values * values, axis=-1, keepdims=True)) + EPSILON) * gain_row

def project(inputs, weight):
    return jnp.einsum('...d,de->...e', inputs, weight, precision=HIGHEST)

def attend(queries, key_rows, values, allowed):
    batches, query_rows = (queries.shape[0], queries.shape[1])
    q_heads = low(queries).reshape(batches, query_rows, HEADS, HEAD)
    k_heads = low(key_rows).reshape(batches, key_rows.shape[1], HEADS, HEAD)
    v_heads = low(values).reshape(batches, values.shape[1], HEADS, HEAD)
    scores = low_back(SCORE_SCALE * jnp.einsum('bqhe,bkhe->bhqk', q_heads, k_heads, precision=HIGHEST))
    scores = jnp.where(allowed[:, None], scores, MASK_FILL)
    softmax_out = jax.nn.softmax(scores, axis=-1)
    mixed_out = jnp.einsum('bhqk,bkhe->bqhe', low(softmax_out), v_heads, precision=HIGHEST)
    return low_back(mixed_out.reshape(batches, query_rows, HEADS * HEAD))

def feed_forward(residual, gain_row, weight_in, weight_out):
    normed = low(rms_norm(residual, gain_row))
    before = low_back(project(normed, weight_in))
    active = low(jax.nn.relu(before))
    return low_back(jnp.einsum('...f,df->...d', active, weight_out, precision=HIGHEST))

def model_pi(embed, layers, gain_rows, prompt_ids, prompt_lengths, decoder_input, targets, response_lengths, pair_local):
    table_low = low(embed)
    weights = low(layers)

    def column_block(first_column, column_count):
        return weights[:, first_column:first_column + column_count]
    pairs_here, seat_count = (prompt_ids.shape[0], decoder_input.shape[0])
    prompt_pos = jnp.arange(P_MAX)
    reply_pos = jnp.arange(R_MAX)
    prompt_keys = prompt_pos[None, :] < prompt_lengths[:, None]
    valid = reply_pos[None, :] < response_lengths[:, None]
    encoder_input = table_low[prompt_ids]
    normed = low(rms_norm(encoder_input, gain_rows[0]))
    triple = low_back(project(normed, column_block(0, 3 * D)))
    enc_allowed = jnp.broadcast_to(prompt_keys[:, None, :], (pairs_here, P_MAX, P_MAX))
    attended = attend(triple[..., :D], triple[..., D:2 * D], triple[..., 2 * D:], enc_allowed)
    encoder_one = encoder_input + low_back(project(low(attended), column_block(3 * D, D)))
    encoder_two = encoder_one + feed_forward(encoder_one, gain_rows[1], column_block(12 * D, FF), column_block(12 * D + FF, FF))
    encoder_final = low(rms_norm(encoder_two, gain_rows[2]))
    cross_memory = low_back(project(encoder_final, column_block(9 * D, 2 * D)))
    decoder_zero = table_low[decoder_input]
    normed = low(rms_norm(decoder_zero, gain_rows[3]))
    triple = low_back(project(normed, column_block(4 * D, 3 * D)))
    self_allowed = (reply_pos[:, None] >= reply_pos[None, :])[None] & valid[:, None, :]
    attended = attend(triple[..., :D], triple[..., D:2 * D], triple[..., 2 * D:], self_allowed)
    decoder_one = decoder_zero + low_back(project(low(attended), column_block(7 * D, D)))
    normed = low(rms_norm(decoder_one, gain_rows[4]))
    cross_query = low_back(project(normed, column_block(8 * D, D)))
    seat_memory = cross_memory[pair_local]
    cross_allowed = jnp.broadcast_to(prompt_keys[pair_local][:, None, :], (seat_count, R_MAX, P_MAX))
    attended = attend(cross_query, seat_memory[..., :D], seat_memory[..., D:], cross_allowed)
    decoder_two = decoder_one + low_back(project(low(attended), column_block(11 * D, D)))
    decoder_three = decoder_two + feed_forward(decoder_two, gain_rows[5], column_block(12 * D + 2 * FF, FF), column_block(12 * D + 3 * FF, FF))
    final_rows = low(rms_norm(decoder_three, gain_rows[6]) * D ** (-0.5))
    logits = low_back(jnp.einsum('srd,vd->srv', final_rows, table_low, precision=HIGHEST))
    picked = jnp.take_along_axis(logits, targets[..., None], axis=-1)[..., 0]
    token_logp = picked - jax.nn.logsumexp(logits, axis=-1)
    return lax.optimization_barrier(jnp.sum(jnp.where(valid, token_logp, 0.0), axis=-1))

def group_loss(embed, layers, gain_rows, inputs_group, frozen_logp, pair_divisor, sequence_divisor, chosen_float):
    policy_logp = model_pi(embed, layers, gain_rows, *inputs_group)
    select = (inputs_group[5][:, None] == jnp.arange(PAIRS_DEV)[None, :]).astype(jnp.float32)
    sign_value = 2.0 * chosen_float - 1.0
    margin = PREFERENCE_BETA * lax.optimization_barrier(jnp.sum(select * (sign_value * (policy_logp - frozen_logp))[:, None], axis=0))
    return (jnp.sum(jax.nn.softplus(-margin) / pair_divisor) - CHOSEN_WEIGHT * jnp.sum(chosen_float * policy_logp / sequence_divisor)) / MICRO

def apply_update(weight, moment, average, gradient, factor):
    clipped = gradient * factor
    moment_new = MOMENTUM * moment + clipped
    step_size = -LEARN_RATE * (clipped + MOMENTUM * moment_new)
    weight_new = weight + step_size
    return (weight_new, moment_new, AVERAGE_DECAY * average + (1.0 - AVERAGE_DECAY) * weight_new, step_size)

def reference(prompt_ids, prompt_lengths, response_ids, response_lengths, sequence_pair, chosen_flag, pair_microbatch, policy_embed, policy_layers, policy_gains, momentum_embed, momentum_layers, momentum_gains, average_embed, average_layers, average_gains, frozen_embed, frozen_layers, frozen_gains):
    groups = PAIRS // PAIRS_DEV
    seat_count = 2 * PAIRS_DEV
    decoder_input = jnp.concatenate([jnp.zeros((SEQS, 1), jnp.int32), response_ids[:, :-1]], axis=1)
    pair_local = sequence_pair - jnp.arange(SEQS, dtype=jnp.int32) // seat_count * PAIRS_DEV
    grouped = (prompt_ids.reshape(groups, PAIRS_DEV, P_MAX), prompt_lengths.reshape(groups, PAIRS_DEV), decoder_input.reshape(groups, seat_count, R_MAX), response_ids.reshape(groups, seat_count, R_MAX), response_lengths.reshape(groups, seat_count), pair_local.reshape(groups, seat_count))
    frozen_table = frozen_embed.astype(jnp.float32)
    frozen_weights = frozen_layers.astype(jnp.float32)

    def frozen_group(inputs_group):
        return model_pi(frozen_table, frozen_weights, frozen_gains, *inputs_group)
    frozen_logp = lax.map(frozen_group, grouped)
    frozen_mean = frozen_logp.reshape(-1) / response_lengths.astype(jnp.float32)
    micro_range = jnp.arange(MICRO)
    sequence_micro = pair_microbatch[sequence_pair]
    pair_count = lax.optimization_barrier(jnp.sum((pair_microbatch[:, None] == micro_range[None, :]).astype(jnp.float32), axis=0))
    chosen_tokens = (chosen_flag * response_lengths).astype(jnp.float32)
    token_count = lax.optimization_barrier(jnp.sum((sequence_micro[:, None] == micro_range[None, :]).astype(jnp.float32) * chosen_tokens[:, None], axis=0))
    micro_counts = jnp.stack([pair_count, token_count])
    pair_divisor = pair_count[pair_microbatch].reshape(groups, PAIRS_DEV)
    sequence_divisor = token_count[sequence_micro].reshape(groups, seat_count)
    chosen_float = chosen_flag.astype(jnp.float32).reshape(groups, seat_count)
    extras = (grouped, frozen_logp, pair_divisor, sequence_divisor, chosen_float)

    def accumulate(running, extra_slice):

        def local_loss(embed, layers, gain_rows):
            return group_loss(embed, layers, gain_rows, *extra_slice)
        group_value, pullback = jax.vjp(local_loss, policy_embed, policy_layers, policy_gains)
        group_grads = pullback(jnp.ones_like(group_value))
        return ((running[0] + group_value, jax.tree.map(jnp.add, running[1], group_grads)), None)
    initial = (jnp.zeros((), jnp.float32), (jnp.zeros_like(policy_embed), jnp.zeros_like(policy_layers), jnp.zeros_like(policy_gains)))
    (loss, gradients), unused = lax.scan(accumulate, initial, extras)
    squares = jnp.sum(gradients[0] * gradients[0]) + jnp.sum(gradients[1] * gradients[1]) + jnp.sum(gradients[2] * gradients[2])
    grad_norm = jnp.sqrt(squares)
    factor = jnp.minimum(1.0, CLIP_NORM / grad_norm)
    embed_new = apply_update(policy_embed, momentum_embed, average_embed, gradients[0], factor)
    layers_new = apply_update(policy_layers, momentum_layers, average_layers, gradients[1], factor)
    gains_new = apply_update(policy_gains, momentum_gains, average_gains, gradients[2], factor)
    return (loss, grad_norm, micro_counts, frozen_mean, embed_new[3], layers_new[0], gains_new[0], embed_new[1], layers_new[1], gains_new[1], embed_new[2], layers_new[2], gains_new[2])
```

```python
import functools

import jax
import jax.numpy as jnp
from jax import lax
from jax.experimental import pallas as pl
from jax.experimental.pallas import tpu as pltpu
from jax.sharding import PartitionSpec as P

D = 1024
HEADS = 16
HEAD = 64
FF = 4096
P_MAX = 192
R_MAX = 32
MICRO = 2


EPSILON = 1e-06
SCORE_SCALE = 0.125
PREFERENCE_BETA = 0.1
CHOSEN_WEIGHT = 1.0
MOMENTUM = 0.9
LEARN_RATE = 2000.0
AVERAGE_DECAY = 0.5
CLIP_NORM = 0.04
MASK_FILL = -1000000000.0
HIGHEST = lax.Precision.HIGHEST


def rms_norm(values, gain_row):
    return (
        values * lax.rsqrt(jnp.mean(values * values, axis=-1, keepdims=True) + EPSILON) * gain_row
    )


def final_norm(values, gain_row):
    return rms_norm(values, gain_row) * D ** (-0.5)


def to_low(values):
    return values.astype(jnp.bfloat16)


def matmul(left_side, right_side):
    return jnp.dot(left_side, right_side, preferred_element_type=jnp.float32)


def matmul_back(grad_low, weight):
    return jnp.einsum("re,de->rd", grad_low, weight, preferred_element_type=jnp.float32)


def split_heads(values):
    return values.reshape(values.shape[0], values.shape[1], HEADS, HEAD)


def scores_of(queries, key_rows, allowed):
    raw_scores = (
        jnp.einsum(
            "bqhe,bkhe->bhqk",
            split_heads(queries),
            split_heads(key_rows),
            preferred_element_type=jnp.float32,
        )
        * SCORE_SCALE
    )
    return jnp.where(allowed[:, None], raw_scores, MASK_FILL)


def attend_forward(queries, key_rows, values, allowed):
    scores = scores_of(queries, key_rows, allowed)
    log_total = jax.nn.logsumexp(scores, axis=-1, keepdims=True)
    softmax_out = to_low(jnp.exp(scores - log_total))
    mixed_out = jnp.einsum(
        "bhqk,bkhe->bqhe", softmax_out, split_heads(values), preferred_element_type=jnp.float32
    )
    return (to_low(mixed_out.reshape(queries.shape)), log_total)


def attend_backward(queries, key_rows, values, allowed, log_total, grad_mixed):
    softmax_out = jnp.exp(scores_of(queries, key_rows, allowed) - log_total)
    grad_heads = split_heads(to_low(grad_mixed))
    grad_values = jnp.einsum(
        "bhqk,bqhe->bkhe", to_low(softmax_out), grad_heads, preferred_element_type=jnp.float32
    )
    grad_probs = jnp.einsum(
        "bqhe,bkhe->bhqk", grad_heads, split_heads(values), preferred_element_type=jnp.float32
    )
    grad_scores = to_low(
        softmax_out * (grad_probs - jnp.sum(grad_probs * softmax_out, axis=-1, keepdims=True))
    )
    grad_query = (
        jnp.einsum(
            "bhqk,bkhe->bqhe",
            grad_scores,
            split_heads(key_rows),
            preferred_element_type=jnp.float32,
        )
        * SCORE_SCALE
    )
    grad_keys = (
        jnp.einsum(
            "bhqk,bqhe->bkhe", grad_scores, split_heads(queries), preferred_element_type=jnp.float32
        )
        * SCORE_SCALE
    )
    return (
        grad_query.reshape(queries.shape),
        grad_keys.reshape(key_rows.shape),
        grad_values.reshape(values.shape),
    )


def self_forward(residual, gain_row, weight_three, weight_out, allowed, shape_pair):
    normed = to_low(rms_norm(residual, gain_row))
    triple = to_low(matmul(normed, weight_three)).reshape(shape_pair[0], shape_pair[1], 3 * D)
    mixed_out, log_total = attend_forward(
        triple[..., :D], triple[..., D : 2 * D], triple[..., 2 * D :], allowed
    )
    flat_mixed = mixed_out.reshape(-1, D)
    return (residual + matmul(flat_mixed, weight_out), (normed, triple, log_total, flat_mixed))


def self_backward(residual, gain_row, weight_three, weight_out, allowed, stored, grad_out):
    normed, triple, log_total, flat_mixed = stored
    grad_low = to_low(grad_out)
    grad_mixed = matmul_back(grad_low, weight_out)
    queries = triple[..., :D]
    grad_query, grad_keys, grad_values = attend_backward(
        queries,
        triple[..., D : 2 * D],
        triple[..., 2 * D :],
        allowed,
        log_total,
        grad_mixed.reshape(queries.shape),
    )
    grad_triple = to_low(
        jnp.concatenate([grad_query, grad_keys, grad_values], axis=-1).reshape(-1, 3 * D)
    )
    grad_normed = matmul_back(grad_triple, weight_three)
    grad_residual, grad_gain = jax.vjp(rms_norm, residual, gain_row)[1](grad_normed)
    return (grad_out + grad_residual, grad_gain, ((normed, grad_triple), (flat_mixed, grad_low)))


def cross_forward(
    residual, gain_row, weight_query, weight_out, cross_memory, select_low, allowed, shape_pair
):
    normed = to_low(rms_norm(residual, gain_row))
    queries = to_low(matmul(normed, weight_query)).reshape(shape_pair[0], shape_pair[1], D)
    seat_memory = to_low(
        jnp.einsum("sp,pkd->skd", select_low, cross_memory, preferred_element_type=jnp.float32)
    )
    mixed_out, log_total = attend_forward(
        queries, seat_memory[..., :D], seat_memory[..., D:], allowed
    )
    flat_mixed = mixed_out.reshape(-1, D)
    return (
        residual + matmul(flat_mixed, weight_out),
        (normed, queries, seat_memory, log_total, flat_mixed),
    )


def cross_backward(
    residual, gain_row, weight_query, weight_out, select_low, allowed, stored, grad_out
):
    normed, queries, seat_memory, log_total, flat_mixed = stored
    grad_low = to_low(grad_out)
    grad_mixed = matmul_back(grad_low, weight_out)
    grad_query, grad_keys, grad_values = attend_backward(
        queries,
        seat_memory[..., :D],
        seat_memory[..., D:],
        allowed,
        log_total,
        grad_mixed.reshape(queries.shape),
    )
    grad_memory = to_low(
        jnp.einsum(
            "sp,skd->pkd",
            select_low.astype(jnp.float32),
            jnp.concatenate([grad_keys, grad_values], axis=-1),
            precision=HIGHEST,
        )
    )
    query_low = to_low(grad_query.reshape(-1, D))
    grad_normed = matmul_back(query_low, weight_query)
    grad_residual, grad_gain = jax.vjp(rms_norm, residual, gain_row)[1](grad_normed)
    return (
        grad_out + grad_residual,
        grad_gain,
        grad_memory,
        ((normed, query_low), (flat_mixed, grad_low)),
    )


def feed_forward(residual, gain_row, weight_in, weight_out):
    normed = to_low(rms_norm(residual, gain_row))
    before = matmul(normed, weight_in)
    active = to_low(jax.nn.relu(before))
    return (
        residual + jnp.einsum("rf,df->rd", active, weight_out, preferred_element_type=jnp.float32),
        (normed, before, active),
    )


def feed_backward(residual, gain_row, weight_in, weight_out, stored, grad_out):
    normed, before, active = stored
    grad_low = to_low(grad_out)
    grad_active = matmul(grad_low, weight_out)
    grad_before = to_low(jnp.where(before > 0, grad_active, 0.0))
    grad_normed = matmul_back(grad_before, weight_in)
    grad_residual, grad_gain = jax.vjp(rms_norm, residual, gain_row)[1](grad_normed)
    return (grad_out + grad_residual, grad_gain, ((normed, grad_before), (grad_low, active)))


AXES = ("dp", "fsdp")
SLOTS = 24
MESH = pl.DeviceIdType.MESH
WAVE_STEP = 512


def device_bits():
    bits = []
    for axis in AXES:
        mask = lax.axis_size(axis) // 2
        while mask:
            bits.append((axis, mask))
            mask //= 2
    return bits


def scatter_orders():
    core, across = (("dp", 1), ("dp", 2))
    inner = [bit for bit in reversed(device_bits()) if bit[0] == "fsdp"]
    first, rest = inner[:1], inner[1:]
    return (
        [core, across] + rest + first,
        [core] + inner + [across],
        [core, across] + first + rest,
        [core] + first + [across] + rest,
    )


def wave_orders(wave):
    orders = scatter_orders()
    return orders[2:] if wave % 3 == 1 else orders[:2]


def bit_of(bit):
    axis, mask = bit
    return (lax.axis_index(axis) // mask) % 2


def partner(bit):
    axis, mask = bit
    return {axis: lax.axis_index(axis) + mask * (1 - 2 * bit_of(bit))}


def greet(bits):
    barrier = pltpu.get_barrier_semaphore()
    for bit in bits:
        pl.semaphore_signal(barrier, inc=1, device_id=partner(bit), device_id_type=MESH)
    pl.semaphore_wait(barrier, len(bits))


def gather_kernel(bits, waves, x_ref, *refs):
    outs, (own_sem, send_sem, recv_sem) = (refs[:-3], refs[-3:])
    mine = {bit: bit_of(bit) for bit in bits}
    depth = len(bits)

    def held(order, low, width):
        lead = tuple(pl.ds(0, 2) if bit in order else pl.ds(mine[bit], 1) for bit in bits)
        return lead + (slice(None), pl.ds(low, width))

    def source(start, width):
        return x_ref.at[(slice(None),) * (depth + 1) + (pl.ds(start, width),)]

    greet(bits)
    number, index = (0, {})
    for wave, pieces in enumerate(waves):
        for lane in range(len(pieces)):
            index[wave, lane] = number
            number += 1
    sent, kept = ({}, {})
    for turn in range(len(waves) + depth):
        for step in range(depth + 1):
            wave = turn - step
            if not 0 <= wave < len(waves):
                continue
            for lane, (start, which, low, width, order) in enumerate(waves[wave]):
                slot = index[wave, lane]
                out = outs[which]
                place = out.at[held(order[:step], low, width)]
                if step == 0:
                    kept[slot] = pltpu.make_async_copy(source(start, width), place, own_sem.at[slot])
                    kept[slot].start()
                elif step == 1:
                    kept[slot].wait()
                if step > 0:
                    sent[slot, step - 1].wait_recv()
                if step < depth:
                    sent[slot, step] = pltpu.make_async_remote_copy(
                        src_ref=source(start, width) if step == 0 else place,
                        dst_ref=place,
                        send_sem=send_sem.at[slot, step],
                        recv_sem=recv_sem.at[slot, step],
                        device_id=partner(order[step]),
                        device_id_type=MESH,
                    )
                    sent[slot, step].start()
    for copy in sent.values():
        copy.wait_send()


def tree_gather(shard, blocks, step, collective_id):
    bits = device_bits()
    pieces = []
    for which, (start, width) in enumerate(blocks):
        for low in range(0, width, step):
            pieces.append((start + low, which, low, min(step, width - low)))
    waves = []
    for wave in range(-(-len(pieces) // 2)):
        waves.append(
            [
                piece + (tuple(reversed(order)),)
                for piece, order in zip(pieces[2 * wave : 2 * wave + 2], wave_orders(wave))
            ]
        )
    rows = shard.shape[0]
    gathered = pl.pallas_call(
        functools.partial(gather_kernel, bits, waves),
        out_shape=[
            jax.ShapeDtypeStruct((2,) * len(bits) + (rows, width), shard.dtype)
            for _, width in blocks
        ],
        in_specs=[pl.BlockSpec(memory_space=pl.ANY)],
        out_specs=[pl.BlockSpec(memory_space=pl.ANY)] * len(blocks),
        scratch_shapes=[
            pltpu.SemaphoreType.DMA((len(pieces),)),
            pltpu.SemaphoreType.DMA((len(pieces), len(bits))),
            pltpu.SemaphoreType.DMA((len(pieces), len(bits))),
        ],
        compiler_params=pltpu.CompilerParams(collective_id=collective_id, has_side_effects=True),
    )(shard.reshape((1,) * len(bits) + shard.shape))
    return [value.reshape(-1, width) for value, (_, width) in zip(gathered, blocks)]


def gather_whole(values, step, collective_id):
    full = tree_gather(values, [(0, values.shape[1])], step, collective_id)[0]
    return full.reshape((-1,) + values.shape)


def scatter_kernel(bits, plan, produce, *refs):
    n_waves, slots, width = (plan["waves"], plan["slots"], plan["step"])
    ins, (out_ref, send_core, total, from_core, arrived) = (refs[:-8], refs[-8:-3])
    send_sem, recv_sem, free_sem = refs[-3:]
    depth = len(bits)
    mine = {bit: bit_of(bit) for bit in bits}
    core = scatter_orders()[0][0]
    rest = [bit for bit in bits if bit != core]

    def half(order, step, kept):
        bit_at = {bit: pl.ds(mine[bit], 1) for bit in order[1:step]}
        last = mine[order[step]] if kept else 1 - mine[order[step]]
        bit_at[order[step]] = pl.ds(last, 1)
        return tuple(bit_at.get(bit, pl.ds(0, 2)) for bit in rest)

    def copy(slot, step, order):
        if step == 0:
            source, target = (send_core.at[slot], from_core.at[slot])
        else:
            source = total.at[(slot,) + half(order, step, False)]
            target = arrived.at[(slot,) + half(order, step, True)]
        return pltpu.make_async_remote_copy(
            src_ref=source,
            dst_ref=target,
            send_sem=send_sem.at[slot, step],
            recv_sem=recv_sem.at[slot, step],
            device_id=partner(order[step]),
            device_id_type=MESH,
        )

    def kept_entries(order, step):
        left = [bit for bit in rest if bit not in order[: step + 1]]
        for number in range(2 ** len(left)):
            chosen = {bit: (number >> place) % 2 for place, bit in enumerate(reversed(left))}
            here = tuple(chosen.get(bit, mine[bit]) for bit in rest)
            came = tuple(1 - mine[bit] if bit == order[step] else at for bit, at in zip(rest, here))
            yield here, came

    def put(ref, slot, at, value):
        ref[(slot,) + at] = value.astype(ref.dtype)

    def visit(wave, lane, step, order):
        piece = wave * 2 + lane
        slot = lax.rem(piece, slots)
        reuse = wave >= slots // 2
        if step == 0:

            @pl.when(reuse)
            def _():
                for old in range(depth):
                    copy(slot, old, order).wait_send()

            produce(ins, piece, 1 - mine[core], lambda at, value: put(send_core, slot, at, value))
        else:
            copy(slot, step - 1, order).wait_recv()
            if step == 1:

                def add(at, value):
                    put(total, slot, at, value + from_core[(slot,) + at].astype(jnp.float32))

                produce(ins, piece, mine[core], add)
            else:
                for here, came in kept_entries(order, step - 1):
                    value = total[(slot,) + here].astype(jnp.float32)
                    value = value + arrived[(slot,) + came].astype(jnp.float32)
                    if step == depth:
                        out_ref[:, pl.ds(pl.multiple_of(piece * width, width), width)] = value
                    else:
                        put(total, slot, here, value)

            @pl.when(wave + slots // 2 < n_waves)
            def _():
                pl.semaphore_signal(
                    free_sem.at[slot, step - 1],
                    inc=1,
                    device_id=partner(order[step - 1]),
                    device_id_type=MESH,
                )

        if step < depth:

            @pl.when(reuse)
            def _():
                pl.semaphore_wait(free_sem.at[slot, step], 1)

            copy(slot, step, order).start()

    def group(first, carry):
        for phase in range(3):
            for step in range(depth + 1):
                wave = first * 3 + phase - step

                @pl.when((wave >= 0) & (wave < n_waves))
                def _():
                    for lane, order in enumerate(wave_orders(phase - step)):
                        visit(wave, lane, step, order)

        return carry

    greet(bits)
    lax.fori_loop(0, -(-(n_waves + depth) // 3), group, 0)
    for wave in range(max(0, n_waves - slots // 2), n_waves):
        for lane, order in enumerate(wave_orders(wave)):
            for step in range(depth):
                copy((wave * 2 + lane) % slots, step, order).wait_send()


def tree_scatter(operands, produce, plan, collective_id):
    bits = device_bits()
    slots, width, rows = (plan["slots"], plan["step"], plan["rows"])
    entries = pltpu.VMEM((slots,) + (2,) * (len(bits) - 1) + (rows, width), jnp.bfloat16)
    in_vmem = pl.BlockSpec(memory_space=pltpu.VMEM)
    return pl.pallas_call(
        functools.partial(scatter_kernel, bits, plan, produce),
        out_shape=jax.ShapeDtypeStruct((rows, 2 * plan["waves"] * width), jnp.float32),
        in_specs=[in_vmem] * len(operands),
        out_specs=in_vmem,
        scratch_shapes=[entries] * 4
        + [
            pltpu.SemaphoreType.DMA((slots, len(bits))),
            pltpu.SemaphoreType.DMA((slots, len(bits))),
            pltpu.SemaphoreType.REGULAR((slots, len(bits))),
        ],
        compiler_params=pltpu.CompilerParams(
            collective_id=collective_id, has_side_effects=True, vmem_limit_bytes=60 * 2**20
        ),
    )(*operands)


def unit_of(block, blocks):
    edges, most = ([], sum(blocks))
    for count in blocks[:-1]:
        edges.append(count + (edges[-1] if edges else 0))
    return sum(lax.div(block + (most - edge), most) for edge in edges)


def put_rows(value, lead, rest_count, rows, put):
    for number in range(2**rest_count):
        at = tuple((number >> place) % 2 for place in reversed(range(rest_count)))
        put(lead + at, value[number * rows : (number + 1) * rows])


def layer_products(dec_blocks, enc_blocks, step, rows, ins, piece, core, put):
    dec_left, dec_right, enc_left, enc_right = ins
    dec_pieces = dec_right.shape[1] // step
    rest_count = (D // 4 // rows).bit_length() - 1

    def product(left, right, blocks, number):
        unit = unit_of(lax.div(number * step, D), blocks)
        sides = right[:, pl.ds(pl.multiple_of(number * step, step), step)]
        for across in range(2):
            value = jnp.dot(left[unit, across, core], sides, preferred_element_type=jnp.float32)
            put_rows(value, (across,), rest_count, rows, put)

    @pl.when(piece < dec_pieces)
    def _():
        product(dec_left, dec_right, dec_blocks, piece)

    @pl.when(piece >= dec_pieces)
    def _():
        product(enc_left, enc_right, enc_blocks, piece - dec_pieces)


def scatter_layers(dec_pairs, enc_pairs, rows, collective_id):
    operands, counts = ([], [])
    for pairs in (dec_pairs, enc_pairs):
        left = jnp.stack([left_side.T.reshape(2, 2, D // 4, -1) for left_side, _ in pairs])
        operands += [left, jnp.concatenate([right_side for _, right_side in pairs], axis=1)]
        counts.append([right_side.shape[1] // D for _, right_side in pairs])
    columns_all = operands[1].shape[1] + operands[3].shape[1]
    plan = {"waves": columns_all // (2 * WAVE_STEP), "slots": 12, "step": WAVE_STEP, "rows": rows}
    produce = functools.partial(layer_products, counts[0], counts[1], WAVE_STEP, rows)
    return tree_scatter(operands, produce, plan, collective_id)


def final_entries(step, rows, ins, piece, core, put):
    part = ins[0]
    rest_count = len(part.shape) - 4
    columns_here = pl.ds(pl.multiple_of(piece * step, step), step)
    for number in range(2 ** (rest_count + 1)):
        at = tuple((number >> place) % 2 for place in reversed(range(rest_count + 1)))
        put(at, part[at[:1] + (core,) + at[1:] + (slice(None), columns_here)].astype(jnp.float32))


def scatter_final(part, collective_id):
    bits = device_bits()
    n_dev, step, width = (2 ** len(bits), 128, part.shape[1])
    rows_all = part.shape[0] // n_dev
    turns = max(1, n_dev // 32)
    rows = rows_all // turns
    plan = {"waves": width // (2 * step), "slots": width // step, "step": step, "rows": rows}
    sums = []
    for turn in range(turns):
        some = part.reshape(n_dev, rows_all, width)[:, turn * rows : (turn + 1) * rows]
        operand = some.reshape((2,) * len(bits) + (rows, width))
        produce = functools.partial(final_entries, step, rows)
        sums.append(tree_scatter([operand], produce, plan, collective_id + turn))
    return jnp.concatenate(sums, axis=0)


def lookup_plan(ids, live, rows_here):
    count = ids.shape[0]
    owner = ids // rows_here
    same = (ids[:, None] == ids[None, :]) & live[None, :]
    earlier = jnp.arange(count)[None, :] < jnp.arange(count)[:, None]
    first = live & ~jnp.any(same & earlier, axis=1)
    below = first[None, :] & (owner[:, None] == owner[None, :]) & (ids[None, :] < ids[:, None])
    rank = jnp.sum(below.astype(jnp.int32), axis=1)
    rounds = jnp.max(jnp.where(live, rank, 0)) // SLOTS + 1
    return (owner, ids - owner * rows_here, first, live, rank, rounds)


def round_flat(plan, turn):
    owner, _, _, live, rank, _ = plan
    slot = rank - turn * SLOTS
    return jnp.where(live & (slot >= 0) & (slot < SLOTS), owner * SLOTS + slot, -1)


def round_requests(plan, turn, n_dev):
    flat = round_flat(plan, turn)
    hit = (flat[:, None] == jnp.arange(n_dev * SLOTS)[None, :]) & plan[2][:, None]
    return jnp.sum(jnp.where(hit, plan[1][:, None] + 1, 0), axis=0) - 1


def picking(plan, turn, n_dev):
    return (
        round_flat(plan, turn)[:, None] == jnp.arange(n_dev * SLOTS)[None, :]
    ).astype(jnp.bfloat16)


def asked_hot(asked, rows_here):
    return (asked.reshape(-1)[:, None] == jnp.arange(rows_here)[None, :]).astype(jnp.bfloat16)


def mine_of(table):
    return lax.dynamic_slice_in_dim(table, lax.axis_index(AXES) * SLOTS, SLOTS, axis=1)


def swap(rows, n_dev):
    wide = rows.shape[-1]
    return lax.all_to_all(
        rows.reshape(n_dev, SLOTS, wide), AXES, 0, 0, tiled=True
    ).reshape(n_dev * SLOTS, wide)


def deliver(asked, pick, tables, n_dev):
    hot = asked_hot(asked, tables[0].shape[0])
    rows = jnp.concatenate([to_low(matmul(hot, table)) for table in tables], axis=1)
    return matmul(pick, swap(rows, n_dev))


def fetch_rows(plan, asked, rounds, tables, n_dev):
    rows = deliver(asked, picking(plan, 0, n_dev), tables, n_dev)

    def more(state):
        turn, rows = state
        asked = mine_of(lax.all_gather(round_requests(plan, turn, n_dev), AXES, axis=0))
        return (turn + 1, rows + deliver(asked, picking(plan, turn, n_dev), tables, n_dev))

    return lax.while_loop(lambda state: state[0] < rounds, more, (jnp.int32(1), rows))[1]


def collect(asked, pick, gradient, rows_here, n_dev):
    sums = to_low(jnp.einsum("nk,nd->kd", pick, gradient, preferred_element_type=jnp.float32))
    return jnp.einsum(
        "kc,kd->cd",
        asked_hot(asked, rows_here),
        swap(sums, n_dev),
        preferred_element_type=jnp.float32,
    )


def return_rows(plan, asked, rounds, gradient, rows_here, n_dev):
    gradient = to_low(gradient)
    sums = collect(asked, picking(plan, 0, n_dev), gradient, rows_here, n_dev)

    def more(state):
        turn, sums = state
        asked = mine_of(lax.all_gather(round_requests(plan, turn, n_dev), AXES, axis=0))
        pick = picking(plan, turn, n_dev)
        return (turn + 1, sums + collect(asked, pick, gradient, rows_here, n_dev))

    return lax.while_loop(lambda state: state[0] < rounds, more, (jnp.int32(1), sums))[1]


ENC_BLOCKS = ((0, 3 * D), (3 * D, D), (9 * D, 2 * D), (12 * D, FF), (12 * D + FF, FF))
DEC_BLOCKS = (
    (4 * D, 3 * D),
    (7 * D, D),
    (8 * D, D),
    (11 * D, D),
    (12 * D + 2 * FF, FF),
    (12 * D + 3 * FF, FF),
)


def gather_offloaded(shard, blocks):
    part = jnp.concatenate([shard[:, low : low + width] for low, width in blocks], axis=1)
    part = lax.all_gather(part, AXES, axis=0, tiled=True)
    gathered, at = ([], 0)
    for _, width in blocks:
        gathered.append(part[:, at : at + width])
        at += width
    return gathered


def after(values, *others):
    return lax.optimization_barrier((values,) + others)[0]


def columns(layer_full, first_column, column_count):
    assert layer_full[first_column].shape[1] == column_count
    return layer_full[first_column]


def by_column(blocks, gathered):
    return {low: value for (low, _), value in zip(blocks, gathered)}


def shard_stats(final_rows, table_shard, targets, collective_ids):
    all_rows = gather_whole(final_rows, 128, collective_ids[0]).reshape(-1, D)
    logits = jnp.einsum("rd,vd->rv", all_rows, table_shard, preferred_element_type=jnp.float32)
    low = lax.axis_index(AXES) * table_shard.shape[0]
    hot = (targets - low)[:, None] == jnp.arange(table_shard.shape[0])[None, :]
    largest = jnp.max(logits, axis=1)
    total = jnp.sum(jnp.exp(logits - largest[:, None]), axis=1)
    picked = jnp.sum(jnp.where(hot, logits, 0.0), axis=1)
    stats = jnp.stack([largest, total, picked, picked]).reshape(8, -1)
    stats = gather_whole(stats, stats.shape[1], collective_ids[1]).reshape(-1, 4, largest.shape[0])
    peak = jnp.max(stats[:, 0], axis=0)
    log_own = peak + jnp.log(jnp.sum(stats[:, 1] * jnp.exp(stats[:, 0] - peak), axis=0))
    return (jnp.sum(stats[:, 2], axis=0) - log_own, log_own, logits, hot, all_rows)


def forward(token_rows, layer_full, gain_rows, batch_data):
    (
        prompt_ids,
        decoder_input,
        targets,
        enc_allowed,
        self_allowed,
        cross_allowed,
        select_low,
        valid,
    ) = batch_data
    pairs_here, seat_count = (prompt_ids.shape[0], decoder_input.shape[0])
    prompt_count = prompt_ids.size
    encoder_input = token_rows[:prompt_count]
    encoder_one, encoder_attn = self_forward(
        encoder_input,
        gain_rows[0],
        columns(layer_full, 0, 3 * D),
        columns(layer_full, 3 * D, D),
        enc_allowed,
        (pairs_here, P_MAX),
    )
    encoder_two, encoder_ffn = feed_forward(
        encoder_one,
        gain_rows[1],
        columns(layer_full, 12 * D, FF),
        columns(layer_full, 12 * D + FF, FF),
    )
    encoder_final = to_low(rms_norm(encoder_two, gain_rows[2]))
    cross_memory = to_low(matmul(encoder_final, columns(layer_full, 9 * D, 2 * D))).reshape(
        pairs_here, P_MAX, 2 * D
    )
    decoder_zero = token_rows[prompt_count:]
    decoder_one, decoder_attn = self_forward(
        decoder_zero,
        gain_rows[3],
        columns(layer_full, 4 * D, 3 * D),
        columns(layer_full, 7 * D, D),
        self_allowed,
        (seat_count, R_MAX),
    )
    decoder_two, decoder_cross = cross_forward(
        decoder_one,
        gain_rows[4],
        columns(layer_full, 8 * D, D),
        columns(layer_full, 11 * D, D),
        cross_memory,
        select_low,
        cross_allowed,
        (seat_count, R_MAX),
    )
    decoder_three, decoder_ffn = feed_forward(
        decoder_two,
        gain_rows[5],
        columns(layer_full, 12 * D + 2 * FF, FF),
        columns(layer_full, 12 * D + 3 * FF, FF),
    )
    final_rows = to_low(final_norm(decoder_three, gain_rows[6]))
    stored = (
        encoder_input,
        encoder_one,
        encoder_two,
        encoder_attn,
        encoder_ffn,
        encoder_final,
        decoder_zero,
        decoder_one,
        decoder_two,
        decoder_three,
        decoder_attn,
        decoder_cross,
        decoder_ffn,
    )
    return (final_rows, stored)


def backward(layer_full, gain_rows, batch_data, stored, grad_final):
    (
        prompt_ids,
        decoder_input,
        targets,
        enc_allowed,
        self_allowed,
        cross_allowed,
        select_low,
        valid,
    ) = batch_data
    (
        encoder_input,
        encoder_one,
        encoder_two,
        encoder_attn,
        encoder_ffn,
        encoder_final,
        decoder_zero,
        decoder_one,
        decoder_two,
        decoder_three,
        decoder_attn,
        decoder_cross,
        decoder_ffn,
    ) = stored
    grad_three, gain_six = jax.vjp(final_norm, decoder_three, gain_rows[6])[1](grad_final)
    grad_two, gain_five, dec_ffn_pairs = feed_backward(
        decoder_two,
        gain_rows[5],
        columns(layer_full, 12 * D + 2 * FF, FF),
        columns(layer_full, 12 * D + 3 * FF, FF),
        decoder_ffn,
        grad_three,
    )
    grad_one, gain_four, grad_memory, cross_pairs = cross_backward(
        decoder_one,
        gain_rows[4],
        columns(layer_full, 8 * D, D),
        columns(layer_full, 11 * D, D),
        select_low,
        cross_allowed,
        decoder_cross,
        grad_two,
    )
    grad_zero, gain_three, dec_self_pairs = self_backward(
        decoder_zero,
        gain_rows[3],
        columns(layer_full, 4 * D, 3 * D),
        columns(layer_full, 7 * D, D),
        self_allowed,
        decoder_attn,
        grad_one,
    )
    memory_low = grad_memory.reshape(-1, 2 * D)
    grad_encoder_final = matmul_back(memory_low, columns(layer_full, 9 * D, 2 * D))
    grad_encoder_two, gain_two = jax.vjp(rms_norm, encoder_two, gain_rows[2])[1](grad_encoder_final)
    grad_encoder_one, gain_one, enc_ffn_pairs = feed_backward(
        encoder_one,
        gain_rows[1],
        columns(layer_full, 12 * D, FF),
        columns(layer_full, 12 * D + FF, FF),
        encoder_ffn,
        grad_encoder_two,
    )
    grad_encoder_input, gain_zero, enc_self_pairs = self_backward(
        encoder_input,
        gain_rows[0],
        columns(layer_full, 0, 3 * D),
        columns(layer_full, 3 * D, D),
        enc_allowed,
        encoder_attn,
        grad_encoder_one,
    )
    gain_grads = jnp.stack(
        [gain_zero, gain_one, gain_two, gain_three, gain_four, gain_five, gain_six]
    )
    layer_pairs = (
        enc_self_pairs[0],
        enc_self_pairs[1],
        dec_self_pairs[0],
        dec_self_pairs[1],
        cross_pairs[0],
        (encoder_final, memory_low),
        cross_pairs[1],
        enc_ffn_pairs[0],
        enc_ffn_pairs[1],
        dec_ffn_pairs[0],
        dec_ffn_pairs[1],
    )
    return (gain_grads, layer_pairs, grad_encoder_input, grad_zero)


def apply_update(weight, moment, average, gradient, factor):
    clipped = gradient * factor
    moment_new = MOMENTUM * moment + clipped
    step_size = -LEARN_RATE * (clipped + MOMENTUM * moment_new)
    weight_new = weight + step_size
    return (
        weight_new,
        moment_new,
        AVERAGE_DECAY * average + (1.0 - AVERAGE_DECAY) * weight_new,
        step_size,
    )


def body(
    prompt_ids,
    prompt_lengths,
    response_ids,
    response_lengths,
    sequence_pair,
    chosen_flag,
    pair_microbatch,
    policy_embed,
    policy_layers,
    policy_gains,
    momentum_embed,
    momentum_layers,
    momentum_gains,
    average_embed,
    average_layers,
    average_gains,
    frozen_embed,
    frozen_layers,
    frozen_gains,
):
    n_dev = lax.axis_size(AXES)
    me = lax.axis_index(AXES)
    rows_here = policy_embed.shape[0]
    pairs_here = prompt_ids.shape[0]
    seat_count = response_ids.shape[0]
    decoder_input = jnp.concatenate(
        [jnp.zeros((seat_count, 1), jnp.int32), response_ids[:, :-1]], axis=1
    )
    pair_local = sequence_pair - me * pairs_here
    select_float = (pair_local[:, None] == jnp.arange(pairs_here)[None, :]).astype(jnp.float32)
    prompt_pos = jnp.arange(P_MAX)
    reply_pos = jnp.arange(R_MAX)
    prompt_keys = prompt_pos[None, :] < prompt_lengths[:, None]
    valid = reply_pos[None, :] < response_lengths[:, None]
    enc_allowed = jnp.broadcast_to(prompt_keys[:, None, :], (pairs_here, P_MAX, P_MAX))
    self_allowed = (reply_pos[:, None] >= reply_pos[None, :])[None] & valid[:, None, :]
    seat_keys = jnp.einsum("sp,pk->sk", select_float, prompt_keys.astype(jnp.float32)) > 0.5
    cross_allowed = jnp.broadcast_to(seat_keys[:, None, :], (seat_count, R_MAX, P_MAX))
    batch_data = (
        prompt_ids,
        decoder_input,
        response_ids,
        enc_allowed,
        self_allowed,
        cross_allowed,
        to_low(select_float),
        valid,
    )
    token_ids = jnp.concatenate([prompt_ids.reshape(-1), decoder_input.reshape(-1)])
    token_live = jnp.concatenate([prompt_keys.reshape(-1), valid.reshape(-1)])
    plan = lookup_plan(token_ids, token_live, rows_here)
    packed = jnp.concatenate(
        [
            round_requests(plan, 0, n_dev),
            response_ids.reshape(-1),
            response_lengths,
            pair_local,
            chosen_flag,
            pair_microbatch,
            plan[5][None],
        ]
    )
    packed = jnp.pad(packed, (0, -packed.shape[0] % 1024)).reshape(8, -1)
    notes = gather_whole(packed, packed.shape[1], 0).reshape(n_dev, -1)
    asked = mine_of(notes)
    at = n_dev * SLOTS
    cuts = []
    for width in (seat_count * R_MAX, seat_count, seat_count, seat_count, pairs_here, 1):
        cuts.append(notes[:, at : at + width])
        at += width
    targets, all_lengths, all_pair, all_flag, all_micro, all_rounds = cuts
    targets = targets.reshape(-1)
    rounds = jnp.max(all_rounds)
    all_select = (all_pair[:, :, None] == jnp.arange(pairs_here)).astype(jnp.float32)
    pair_micro = (all_micro[:, :, None] == jnp.arange(MICRO)).astype(jnp.float32)
    seat_micro = jnp.sum(all_select[:, :, :, None] * pair_micro[:, None], axis=2)
    chosen_float = all_flag.astype(jnp.float32)
    pair_total = jnp.sum(pair_micro, axis=(0, 1))
    token_total = jnp.sum(
        seat_micro * (chosen_float * all_lengths.astype(jnp.float32))[:, :, None], axis=(0, 1)
    )
    micro_counts = jnp.stack([pair_total, token_total])
    pair_divisor = jnp.sum(pair_micro * pair_total, axis=2)
    sequence_divisor = jnp.sum(seat_micro * token_total, axis=2)
    all_valid = reply_pos < all_lengths[:, :, None]

    policy_table = to_low(policy_embed)
    both_rows = fetch_rows(plan, asked, rounds, (policy_table, frozen_embed), n_dev)
    policy_low = after(to_low(policy_layers), notes)
    policy_enc = tree_gather(policy_low, ENC_BLOCKS, WAVE_STEP, 1)
    frozen_low = after(frozen_layers, policy_enc[0])
    policy_dec = tree_gather(after(policy_low, policy_enc[0]), DEC_BLOCKS, WAVE_STEP, 2)
    frozen_enc = gather_offloaded(frozen_low, ENC_BLOCKS)
    frozen_dec = gather_offloaded(after(frozen_low, frozen_enc[0]), DEC_BLOCKS)
    policy_layer_full = by_column(ENC_BLOCKS + DEC_BLOCKS, policy_enc + policy_dec)
    frozen_layer_full = by_column(ENC_BLOCKS + DEC_BLOCKS, frozen_enc + frozen_dec)

    def logp_of(token_logp):
        return jnp.sum(jnp.where(all_valid, token_logp.reshape(all_valid.shape), 0.0), axis=2)

    policy_rows, stored = forward(both_rows[:, :D], policy_layer_full, policy_gains, batch_data)
    token_logp, log_own, logits, hot, all_rows = shard_stats(
        policy_rows, policy_table, targets, (3, 4)
    )
    policy_logp = logp_of(token_logp)
    frozen_rows, unused = forward(both_rows[:, D:], frozen_layer_full, frozen_gains, batch_data)
    frozen_logp = logp_of(shard_stats(frozen_rows, frozen_embed, targets, (5, 6))[0])
    frozen_mean = lax.dynamic_index_in_dim(
        frozen_logp / all_lengths.astype(jnp.float32), me, 0, keepdims=False
    )

    sign_value = 2.0 * chosen_float - 1.0
    margin = PREFERENCE_BETA * jnp.sum(
        all_select * (sign_value * (policy_logp - frozen_logp))[:, :, None], axis=1
    )
    loss = (
        jnp.sum(jax.nn.softplus(-margin) / pair_divisor)
        - CHOSEN_WEIGHT * jnp.sum(chosen_float * policy_logp / sequence_divisor)
    ) / MICRO
    pair_slope = -PREFERENCE_BETA * jax.nn.sigmoid(-margin) / pair_divisor
    sequence_slope = (
        sign_value * jnp.sum(all_select * pair_slope[:, None, :], axis=2)
        - CHOSEN_WEIGHT * chosen_float / sequence_divisor
    ) / MICRO
    row_weight = (sequence_slope[:, :, None] * all_valid).reshape(-1)

    grad_logits = to_low(
        row_weight[:, None] * (hot.astype(jnp.float32) - jnp.exp(logits - log_own[:, None]))
    )
    grad_final = scatter_final(to_low(matmul(grad_logits, policy_table)), 10)
    table_grad = jnp.einsum("rc,rd->cd", grad_logits, all_rows, preferred_element_type=jnp.float32)
    gain_grads, layer_pairs, grad_encoder_input, grad_decoder_input = backward(
        policy_layer_full, policy_gains, batch_data, stored, grad_final
    )
    token_gradient = jnp.concatenate([grad_encoder_input, grad_decoder_input], axis=0)
    embed_grad = table_grad + return_rows(plan, asked, rounds, token_gradient, rows_here, n_dev)
    enc_pairs = [layer_pairs[place] for place in (0, 1, 5, 7, 8)]
    dec_pairs = [layer_pairs[place] for place in (2, 3, 4, 6, 9, 10)]
    scattered = scatter_layers(dec_pairs, enc_pairs, policy_layers.shape[0], 8)
    edges, at = ({}, 0)
    for low, width in DEC_BLOCKS + ENC_BLOCKS:
        edges[low] = scattered[:, at : at + width]
        at += width
    layer_grad = jnp.concatenate([edges[low] for low in sorted(edges)], axis=1)
    squares_local = jnp.sum(embed_grad * embed_grad) + jnp.sum(layer_grad * layer_grad)
    shared = jnp.concatenate([gain_grads, jnp.full((1, D), squares_local)], axis=0)
    shared = jnp.sum(gather_whole(shared, D, 9), axis=0)
    gain_total, squares_total = (shared[:7], shared[7, 0])
    grad_norm = jnp.sqrt(squares_total + jnp.sum(gain_total * gain_total))
    factor = jnp.minimum(1.0, CLIP_NORM / grad_norm)
    embed_new = apply_update(policy_embed, momentum_embed, average_embed, embed_grad, factor)
    layers_new = apply_update(policy_layers, momentum_layers, average_layers, layer_grad, factor)
    gains_new = apply_update(policy_gains, momentum_gains, average_gains, gain_total, factor)
    return (
        loss,
        grad_norm,
        micro_counts,
        frozen_mean,
        embed_new[3],
        layers_new[0],
        gains_new[0],
        embed_new[1],
        layers_new[1],
        gains_new[1],
        embed_new[2],
        layers_new[2],
        gains_new[2],
    )


def solution(mesh):
    placed = (
        P(("dp", "fsdp"), None),
        P(("dp", "fsdp")),
        P(("dp", "fsdp"), None),
        P(("dp", "fsdp")),
        P(("dp", "fsdp")),
        P(("dp", "fsdp")),
        P(("dp", "fsdp")),
        P(("dp", "fsdp"), None),
        P(("dp", "fsdp"), None),
        P(),
        P(("dp", "fsdp"), None),
        P(("dp", "fsdp"), None),
        P(),
        P(("dp", "fsdp"), None),
        P(("dp", "fsdp"), None),
        P(),
        P(("dp", "fsdp"), None),
        P(("dp", "fsdp"), None),
        P(),
    )
    return jax.shard_map(
        body,
        mesh=mesh,
        in_specs=placed,
        out_specs=(
            P(),
            P(),
            P(),
            P(("dp", "fsdp")),
            P(("dp", "fsdp"), None),
            P(("dp", "fsdp"), None),
            P(),
            P(("dp", "fsdp"), None),
            P(("dp", "fsdp"), None),
            P(),
            P(("dp", "fsdp"), None),
            P(("dp", "fsdp"), None),
            P(),
        ),
        check_vma=False,
    )
```

```python
import functools

import jax
import jax.numpy as jnp
from jax import lax
from jax.experimental import pallas as pl
from jax.experimental.layout import Layout, with_layout_constraint
from jax.experimental.pallas import tpu as pltpu
from jax.sharding import PartitionSpec as P

D = 1024
HEADS = 16
HEAD = 64
FF = 4096
P_MAX = 192
R_MAX = 32
MICRO = 2


EPSILON = 1e-06
SCORE_SCALE = 0.125
PREFERENCE_BETA = 0.1
CHOSEN_WEIGHT = 1.0
MOMENTUM = 0.9
LEARN_RATE = 2000.0
AVERAGE_DECAY = 0.5
CLIP_NORM = 0.04
MASK_FILL = -1000000000.0
HIGHEST = lax.Precision.HIGHEST


def rms_norm(values, gain_row):
    return (
        values * lax.rsqrt(jnp.mean(values * values, axis=-1, keepdims=True) + EPSILON) * gain_row
    )


def final_norm(values, gain_row):
    return rms_norm(values, gain_row) * D ** (-0.5)


def to_low(values):
    return values.astype(jnp.bfloat16)


def matmul(left_side, right_side):
    return jnp.dot(left_side, right_side, preferred_element_type=jnp.float32)


def matmul_back(grad_low, weight):
    return jnp.einsum("re,de->rd", grad_low, weight, preferred_element_type=jnp.float32)


def split_heads(values):
    return values.reshape(values.shape[0], values.shape[1], HEADS, HEAD)


def scores_of(queries, key_rows, allowed):
    raw_scores = (
        jnp.einsum(
            "bqhe,bkhe->bhqk",
            split_heads(queries),
            split_heads(key_rows),
            preferred_element_type=jnp.float32,
        )
        * SCORE_SCALE
    )
    return jnp.where(allowed[:, None], raw_scores, MASK_FILL)


def attend_forward(queries, key_rows, values, allowed):
    scores = scores_of(queries, key_rows, allowed)
    log_total = jax.nn.logsumexp(scores, axis=-1, keepdims=True)
    softmax_out = to_low(jnp.exp(scores - log_total))
    mixed_out = jnp.einsum(
        "bhqk,bkhe->bqhe", softmax_out, split_heads(values), preferred_element_type=jnp.float32
    )
    return (to_low(mixed_out.reshape(queries.shape)), log_total)


def attend_backward(queries, key_rows, values, allowed, log_total, grad_mixed):
    softmax_out = jnp.exp(scores_of(queries, key_rows, allowed) - log_total)
    grad_heads = split_heads(to_low(grad_mixed))
    grad_values = jnp.einsum(
        "bhqk,bqhe->bhke", to_low(softmax_out), grad_heads, preferred_element_type=jnp.float32
    )
    grad_probs = jnp.einsum(
        "bqhe,bkhe->bhqk", grad_heads, split_heads(values), preferred_element_type=jnp.float32
    )
    grad_scores = to_low(
        softmax_out * (grad_probs - jnp.sum(grad_probs * softmax_out, axis=-1, keepdims=True))
    )
    grad_query = (
        jnp.einsum(
            "bhqk,bkhe->bqhe",
            grad_scores,
            split_heads(key_rows),
            preferred_element_type=jnp.float32,
        )
        * SCORE_SCALE
    )
    grad_keys = (
        jnp.einsum(
            "bhqk,bqhe->bhke", grad_scores, split_heads(queries), preferred_element_type=jnp.float32
        )
        * SCORE_SCALE
    )
    return (grad_query.reshape(queries.shape), grad_keys, grad_values)


def join_heads(values):
    return values.transpose(0, 2, 1, 3).reshape(values.shape[0], values.shape[2], D)


def self_forward(residual, gain_row, weight_three, weight_out, allowed, shape_pair):
    normed = to_low(rms_norm(residual, gain_row))
    triple = to_low(matmul(normed, weight_three)).reshape(shape_pair[0], shape_pair[1], 3 * D)
    mixed_out, log_total = attend_forward(
        triple[..., :D], triple[..., D : 2 * D], triple[..., 2 * D :], allowed
    )
    flat_mixed = mixed_out.reshape(-1, D)
    return (residual + matmul(flat_mixed, weight_out), (normed, triple, log_total, flat_mixed))


def norm_backward(norm, residual, gain_row, grad_normed):
    grad_residual = jax.vjp(lambda values: norm(values, gain_row), residual)[1](grad_normed)[0]
    return grad_residual, grad_normed * norm(residual, jnp.ones_like(gain_row))


def self_backward(residual, gain_row, weight_three, weight_out, allowed, stored, grad_out):
    normed, triple, log_total, flat_mixed = stored
    grad_mixed = matmul_back(to_low(grad_out), weight_out)
    queries = triple[..., :D]
    grad_query, grad_keys, grad_values = attend_backward(
        queries,
        triple[..., D : 2 * D],
        triple[..., 2 * D :],
        allowed,
        log_total,
        grad_mixed.reshape(queries.shape),
    )
    grads = (grad_query, join_heads(grad_keys), join_heads(grad_values))
    grad_triple = jnp.concatenate(grads, axis=-1).reshape(-1, 3 * D)
    grad_normed = matmul_back(to_low(grad_triple), weight_three)
    grad_residual, gain_rows = norm_backward(rms_norm, residual, gain_row, grad_normed)
    return (grad_out + grad_residual, gain_rows, ((normed, grad_triple), (flat_mixed, grad_out)))


def cross_forward(
    residual, gain_row, weight_query, weight_out, cross_memory, pair_local, allowed, shape_pair
):
    normed = to_low(rms_norm(residual, gain_row))
    queries = to_low(matmul(normed, weight_query)).reshape(shape_pair[0], shape_pair[1], D)
    seat_memory = jnp.broadcast_to(cross_memory[:1], (shape_pair[0],) + cross_memory.shape[1:])
    for pair in range(1, cross_memory.shape[0]):
        seat_memory = jnp.where(
            pair_local[:, None, None] == pair, cross_memory[pair][None], seat_memory
        )
    mixed_out, log_total = attend_forward(
        queries, seat_memory[..., :D], seat_memory[..., D:], allowed
    )
    flat_mixed = mixed_out.reshape(-1, D)
    return (
        residual + matmul(flat_mixed, weight_out),
        (normed, queries, seat_memory, log_total, flat_mixed),
    )


def cross_backward(residual, gain_row, weight_query, weight_out, allowed, stored, grad_out):
    normed, queries, seat_memory, log_total, flat_mixed = stored
    grad_mixed = matmul_back(to_low(grad_out), weight_out)
    grad_query, grad_keys, grad_values = attend_backward(
        queries,
        seat_memory[..., :D],
        seat_memory[..., D:],
        allowed,
        log_total,
        grad_mixed.reshape(queries.shape),
    )
    grad_query = grad_query.reshape(-1, D)
    grad_normed = matmul_back(to_low(grad_query), weight_query)
    grad_residual, gain_rows = norm_backward(rms_norm, residual, gain_row, grad_normed)
    return (
        grad_out + grad_residual,
        gain_rows,
        (grad_keys, grad_values),
        ((normed, grad_query), (flat_mixed, grad_out)),
    )


def feed_forward(residual, gain_row, weight_in, weight_out):
    normed = to_low(rms_norm(residual, gain_row))
    before = matmul(normed, weight_in)
    active = to_low(jax.nn.relu(before))
    return (
        residual + jnp.einsum("rf,df->rd", active, weight_out, preferred_element_type=jnp.float32),
        (normed, active),
    )


def feed_backward(residual, gain_row, weight_in, weight_out, stored, grad_out):
    normed, active = stored
    grad_active = matmul(to_low(grad_out), weight_out)
    grad_before = jnp.where(active > 0, grad_active, 0.0)
    grad_normed = matmul_back(to_low(grad_before), weight_in)
    grad_residual, gain_rows = norm_backward(rms_norm, residual, gain_row, grad_normed)
    return (grad_out + grad_residual, gain_rows, ((normed, grad_before), (grad_out, active)))


AXES = ("dp", "fsdp")
SLOTS = 24
MESH = pl.DeviceIdType.MESH
WAVE_STEP = 512


def device_bits():
    bits = []
    for axis in AXES:
        mask = lax.axis_size(axis) // 2
        while mask:
            bits.append((axis, mask))
            mask //= 2
    return bits


def scatter_orders():
    core, across = (("dp", 1), ("dp", 2))
    inner = [bit for bit in reversed(device_bits()) if bit[0] == "fsdp"]
    first, rest = inner[:1], inner[1:]
    return (
        [core, across] + rest + first,
        [core] + inner + [across],
        [core, across] + first + rest,
        [core] + first + [across] + rest,
    )


def wave_orders(wave):
    orders = scatter_orders()
    return orders[2:] if wave % 3 == 1 else orders[:2]


def bit_of(bit):
    axis, mask = bit
    return (lax.axis_index(axis) // mask) % 2


def partner(bit):
    axis, mask = bit
    return {axis: lax.axis_index(axis) + mask * (1 - 2 * bit_of(bit))}


def greet(bits):
    barrier = pltpu.get_barrier_semaphore()
    for bit in bits:
        pl.semaphore_signal(barrier, inc=1, device_id=partner(bit), device_id_type=MESH)
    pl.semaphore_wait(barrier, len(bits))


def gather_kernel(bits, n_in, waves, *refs):
    ins, outs, (own_sem, send_sem, recv_sem) = (refs[:n_in], refs[n_in:-3], refs[-3:])
    mine = {bit: bit_of(bit) for bit in bits}
    depth = len(bits)
    greet(bits)
    index, sent, kept = ({}, {}, {})
    for turn in range(len(waves) + depth):
        for step in range(depth + 1):
            wave = turn - step
            if not 0 <= wave < len(waves):
                continue
            for lane, (number, which, start, low, width, first, count, order) in enumerate(
                waves[wave]
            ):
                slot = index.setdefault((wave, lane), len(index))
                lead = tuple(
                    pl.ds(0, 2) if bit in order[:step] else pl.ds(mine[bit], 1) for bit in bits
                )
                place = outs[which].at[lead + (pl.ds(first, count), pl.ds(low, width))]
                source = place
                if step == 0:
                    whole = (slice(None),) * depth
                    source = ins[number].at[whole + (pl.ds(first, count), pl.ds(start, width))]
                    kept[slot] = pltpu.make_async_copy(source, place, own_sem.at[slot])
                    kept[slot].start()
                else:
                    sent[slot, step - 1].wait_recv()
                if step == 1:
                    kept[slot].wait()
                if step < depth:
                    sent[slot, step] = pltpu.make_async_remote_copy(
                        src_ref=source,
                        dst_ref=place,
                        send_sem=send_sem.at[slot, step],
                        recv_sem=recv_sem.at[slot, step],
                        device_id=partner(order[step]),
                        device_id_type=MESH,
                    )
                    sent[slot, step].start()
    for copy in sent.values():
        copy.wait_send()


def busy_for(micros):
    return pl.CostEstimate(flops=0, bytes_accessed=int(micros * 3.4e6), transcendentals=0)


def tree_gather(shard, blocks, step, collective_id, micros, row_step=None, extra=None):
    bits = device_bits()
    rows = shard.shape[0]
    row_step = row_step or rows
    pieces = []
    for which, (start, width) in enumerate(blocks):
        for low in range(0, width, step):
            for first in range(0, rows, row_step):
                pieces.append((0, which, start + low, low, min(step, width - low), first, row_step))
    waves = []
    for wave in range(-(-len(pieces) // 2)):
        waves.append(
            [
                piece + (tuple(reversed(order)),)
                for piece, order in zip(pieces[2 * wave : 2 * wave + 2], wave_orders(wave))
            ]
        )
    operands = [shard]
    shapes = [((rows, width), shard.dtype) for _, width in blocks]
    if extra is not None:
        operands.append(extra)
        shapes.append((extra.shape, extra.dtype))
        piece = (1, len(blocks), 0, 0, extra.shape[1], 0, extra.shape[0])
        waves[0].append(piece + (tuple(reversed(wave_orders(0)[0])),))
    total = sum(len(wave) for wave in waves)
    gathered = pl.pallas_call(
        functools.partial(gather_kernel, bits, len(operands), waves),
        out_shape=[
            jax.ShapeDtypeStruct((2,) * len(bits) + shape, dtype) for shape, dtype in shapes
        ],
        in_specs=[pl.BlockSpec(memory_space=pl.ANY)] * len(operands),
        out_specs=[pl.BlockSpec(memory_space=pl.ANY)] * len(shapes),
        scratch_shapes=[
            pltpu.SemaphoreType.DMA((total,)),
            pltpu.SemaphoreType.DMA((total, len(bits))),
            pltpu.SemaphoreType.DMA((total, len(bits))),
        ],
        compiler_params=pltpu.CompilerParams(collective_id=collective_id, has_side_effects=True),
        cost_estimate=busy_for(micros),
    )(*[value.reshape((1,) * len(bits) + value.shape) for value in operands])
    return [value.reshape((-1, shape[1])) for value, (shape, _) in zip(gathered, shapes)]


def gather_whole(values, step, collective_id, micros, row_step=None):
    blocks = [(0, values.shape[1])]
    full = tree_gather(values, blocks, step, collective_id, micros, row_step)[0]
    return full.reshape((-1,) + values.shape)


CORE_SLOTS = 4


def scatter_kernel(bits, plan, *refs):
    n_waves, slots, width, wide = (plan["waves"], plan["slots"], plan["step"], plan["wide"])
    n_ins, n_loaded = (plan["operands"], len(plan["loads"]))
    ins, out_ref = (refs[:n_ins], refs[n_ins])
    loaded, rest_refs = (refs[n_ins + 1 : n_ins + 1 + n_loaded], refs[n_ins + 1 + n_loaded :])
    send_core, from_core, total, narrow, arrived, arrived_wide = rest_refs[:6]
    load_sem, send_sem, recv_sem, free_sem = rest_refs[6:]
    depth = len(bits)
    mine = {bit: bit_of(bit) for bit in bits}
    core = scatter_orders()[0][0]
    rest = [bit for bit in bits if bit != core]

    def half(order, step, kept):
        bit_at = {bit: pl.ds(mine[bit], 1) for bit in order[1:step]}
        last = mine[order[step]] if kept else 1 - mine[order[step]]
        bit_at[order[step]] = pl.ds(last, 1)
        return tuple(bit_at.get(bit, pl.ds(0, 2)) for bit in rest)

    def slot_at(piece, step):
        return lax.rem(piece, CORE_SLOTS if step == 0 else slots)

    def copy(piece, step, order):
        slot = slot_at(piece, step)
        if step == 0:
            source, target = (send_core.at[slot], from_core.at[slot])
        else:
            source = (total if step in wide else narrow).at[(slot,) + half(order, step, False)]
            target = arrived_wide if step in wide else arrived
            target = target.at[(slot,) + half(order, step, True)]
        return pltpu.make_async_remote_copy(
            src_ref=source,
            dst_ref=target,
            send_sem=send_sem.at[slot, step],
            recv_sem=recv_sem.at[slot, step],
            device_id=partner(order[step]),
            device_id_type=MESH,
        )

    def kept_entries(order, step):
        left = [bit for bit in rest if bit not in order[: step + 1]]
        for number in range(2 ** len(left)):
            chosen = {bit: (number >> place) % 2 for place, bit in enumerate(reversed(left))}
            here = tuple(chosen.get(bit, mine[bit]) for bit in rest)
            came = tuple(1 - mine[bit] if bit == order[step] else at for bit, at in zip(rest, here))
            yield here, came

    def keep(slot, at, value, step):
        total[(slot,) + at] = value
        if step not in wide:
            narrow[(slot,) + at] = value.astype(jnp.bfloat16)

    def visit(wave, lane, step, order):
        piece = wave * 2 + lane
        slot = slot_at(piece, step)
        span = (CORE_SLOTS if step == 0 else slots) // 2
        reuse = wave >= span
        if step == 0:

            @pl.when(reuse)
            def _():
                copy(piece, 0, order).wait_send()

            def put(at, value):
                send_core[(slot,) + at] = value

            plan["produce"](loaded, piece, 1 - mine[core], put)
        else:
            copy(piece, step - 1, order).wait_recv()
            if step == 1:
                core_slot = slot_at(piece, 0)

                @pl.when(reuse)
                def _():
                    for old in range(1, depth):
                        copy(piece, old, order).wait_send()

                def add(at, value):
                    keep(slot, at, value + from_core[(core_slot,) + at], 1)

                plan["produce"](loaded, piece, mine[core], add)
            else:
                source = arrived_wide if step - 1 in wide else arrived
                for here, came in kept_entries(order, step - 1):
                    value = total[(slot,) + here] + source[(slot,) + came].astype(jnp.float32)
                    if step == depth:
                        start = plan["column"](piece)
                        out_ref[:, pl.ds(pl.multiple_of(start, width), width)] = value
                    else:
                        keep(slot, here, value, step)

            @pl.when(wave + (CORE_SLOTS if step == 1 else slots) // 2 < n_waves)
            def _():
                pl.semaphore_signal(
                    free_sem.at[slot_at(piece, step - 1), step - 1],
                    inc=1,
                    device_id=partner(order[step - 1]),
                    device_id_type=MESH,
                )

        if step < depth:

            @pl.when(reuse)
            def _():
                pl.semaphore_wait(free_sem.at[slot, step], 1)

            copy(piece, step, order).start()

    loads = []
    for number, (_, parts) in enumerate(plan["loads"]):
        for operand, place in parts:
            at = loaded[number].at[place] if place else loaded[number]
            loads.append(pltpu.make_async_copy(ins[operand], at, load_sem.at[operand]))
            loads[-1].start()

    def group(first, carry):
        for phase in range(3):
            for step in range(depth + 1):
                wave = first * 3 + phase - step

                @pl.when((wave >= 0) & (wave < n_waves))
                def _():
                    if step == 0:
                        for late, count in plan["waits"]:

                            @pl.when(wave == late)
                            def _():
                                for load in loads[slice(*count)]:
                                    load.wait()

                    for lane, order in enumerate(wave_orders(phase - step)):
                        visit(wave, lane, step, order)

        return carry

    greet(bits)
    lax.fori_loop(0, -(-(n_waves + depth) // 3), group, 0)
    for step in range(depth):
        for wave in range(max(0, n_waves - (CORE_SLOTS if step == 0 else slots) // 2), n_waves):
            for lane, order in enumerate(wave_orders(wave)):
                copy(wave * 2 + lane, step, order).wait_send()


def tree_scatter(operands, plan, collective_id, micros):
    bits = device_bits()
    slots, width, rows = (plan["slots"], plan["step"], plan["rows"])
    plan = dict(plan, operands=len(operands))
    entries = (2,) * (len(bits) - 1) + (rows, width)
    core_buffer = pltpu.VMEM((CORE_SLOTS,) + entries, jnp.float32)
    low_buffer = pltpu.VMEM((slots,) + entries, jnp.bfloat16)
    sums = pltpu.VMEM((slots,) + entries, jnp.float32)
    wide_buffer = sums if plan["wide"] else pltpu.VMEM((8, 128), jnp.float32)
    return pl.pallas_call(
        functools.partial(scatter_kernel, bits, plan),
        out_shape=jax.ShapeDtypeStruct((rows, 2 * plan["waves"] * width), jnp.float32),
        in_specs=[pl.BlockSpec(memory_space=pl.ANY)] * len(operands),
        out_specs=pl.BlockSpec(memory_space=pltpu.VMEM),
        scratch_shapes=[pltpu.VMEM(shape, jnp.bfloat16) for shape, _ in plan["loads"]]
        + [core_buffer, core_buffer, sums, low_buffer, low_buffer, wide_buffer]
        + [
            pltpu.SemaphoreType.DMA((len(operands),)),
            pltpu.SemaphoreType.DMA((slots, len(bits))),
            pltpu.SemaphoreType.DMA((slots, len(bits))),
            pltpu.SemaphoreType.REGULAR((slots, len(bits))),
        ],
        compiler_params=pltpu.CompilerParams(
            collective_id=collective_id, has_side_effects=True, vmem_limit_bytes=60 * 2**20
        ),
        cost_estimate=busy_for(micros),
    )(*operands)


def unit_of(block, blocks):
    edges, most = ([], sum(blocks))
    for count in blocks[:-1]:
        edges.append(count + (edges[-1] if edges else 0))
    return sum(lax.div(block + (most - edge), most) for edge in edges)


def put_rows(value, across, rows, put):
    rest_count = (value.shape[0] // rows).bit_length() - 1
    for number in range(2**rest_count):
        at = tuple((number >> place) % 2 for place in reversed(range(rest_count)))
        put((across,) + at, value[number * rows : (number + 1) * rows])


def layer_products(dec_blocks, enc_blocks, step, rows, loaded, piece, core, put):
    dec_left, dec_right, enc_left, enc_right = loaded
    dec_pieces = dec_right.shape[1] // step
    quarter = D // 4

    def product(left, right, blocks, number):
        unit = unit_of(lax.div(number * step, D), blocks)
        sides = right[:, pl.ds(pl.multiple_of(number * step, step), step)]
        for across in range(2):
            some = pl.ds(pl.multiple_of((2 * across + core) * quarter, quarter), quarter)
            value = lax.dot_general(
                left[unit, :, some],
                sides,
                (((0,), (0,)), ((), ())),
                preferred_element_type=jnp.float32,
            )
            put_rows(value, across, rows, put)

    @pl.when(piece < dec_pieces)
    def _():
        product(dec_left, dec_right, dec_blocks, piece)

    @pl.when(piece >= dec_pieces)
    def _():
        product(enc_left, enc_right, enc_blocks, piece - dec_pieces)


def layer_column(step, piece):
    per_block = D // step
    half = 14 * per_block
    is_enc = lax.div(piece, half)
    block = lax.div(piece - is_enc * half, per_block)

    def past(edge):
        return lax.div(block + 14 - edge, 14)

    dec_shift = 4 + 2 * past(5) + 8 * past(6)
    enc_shift = 5 * past(4) + past(6)
    shift = dec_shift + is_enc * (enc_shift - dec_shift)
    return (block + shift) * D + lax.rem(piece, per_block) * step


def scatter_layers(dec_pairs, enc_pairs, rows, collective_id):
    operands, loads, counts = ([], [], [])
    for pairs in (dec_pairs, enc_pairs):
        tokens, parts, at = (pairs[0][0].shape[0], [], 0)
        for unit, (left_side, _) in enumerate(pairs):
            parts.append((len(operands), (unit,)))
            operands.append(left_side)
        loads.append(((len(pairs), tokens, D), parts))
        parts = []
        for _, right_side in pairs:
            parts.append((len(operands), (slice(None), pl.ds(at, right_side.shape[1]))))
            operands.append(right_side)
            at += right_side.shape[1]
        loads.append(((tokens, at), parts))
        counts.append([right_side.shape[1] // D for _, right_side in pairs])
    dec_loads = 2 * len(dec_pairs)
    dec_waves = loads[1][0][1] // (2 * WAVE_STEP)
    plan = {
        "waves": dec_waves + loads[3][0][1] // (2 * WAVE_STEP),
        "slots": 12,
        "step": WAVE_STEP,
        "rows": rows,
        "wide": (),
        "loads": loads,
        "waits": ((0, (0, dec_loads)), (dec_waves, (dec_loads, None))),
        "produce": functools.partial(layer_products, counts[0], counts[1], WAVE_STEP, rows),
        "column": functools.partial(layer_column, WAVE_STEP),
    }
    return tree_scatter(operands, plan, collective_id, 230)


def final_products(step, rows, loaded, piece, core, put):
    left, right = loaded
    sides = right[:, pl.ds(pl.multiple_of(piece * step, step), step)]
    for across in range(2):
        value = jnp.dot(left[across, core], sides, preferred_element_type=jnp.float32)
        put_rows(value, across, rows, put)


def scatter_final(grad_logits, table, collective_id):
    bits = device_bits()
    n_dev, step, width = (2 ** len(bits), 128, table.shape[1])
    rows_all = grad_logits.shape[0] // n_dev
    turns = max(1, n_dev // 32)
    rows = rows_all // turns
    sums = []
    for turn in range(turns):
        some = grad_logits.reshape(n_dev, rows_all, -1)[:, turn * rows : (turn + 1) * rows]
        some = some.reshape(2, 2, n_dev // 4 * rows, -1)
        plan = {
            "waves": width // (2 * step),
            "slots": width // step,
            "step": step,
            "rows": rows,
            "wide": (len(bits) - 2, len(bits) - 1),
            "loads": [(some.shape, [(0, ())]), (table.shape, [(1, ())])],
            "waits": ((0, (0, 2)),),
            "produce": functools.partial(final_products, step, rows),
            "column": lambda piece: piece * step,
        }
        sums.append(tree_scatter([some, table], plan, collective_id + turn, 60))
    return jnp.concatenate(sums, axis=0)


def lookup_plan(ids, live, rows_here):
    count = ids.shape[0]
    owner = ids // rows_here
    same = (ids[:, None] == ids[None, :]) & live[None, :]
    earlier = jnp.arange(count)[None, :] < jnp.arange(count)[:, None]
    first = live & ~jnp.any(same & earlier, axis=1)
    below = first[None, :] & (owner[:, None] == owner[None, :]) & (ids[None, :] < ids[:, None])
    rank = jnp.sum(below.astype(jnp.int32), axis=1)
    rounds = jnp.max(jnp.where(live, rank, 0)) // SLOTS + 1
    return (owner, ids - owner * rows_here, first, live, rank, rounds)


def round_flat(plan, turn):
    owner, _, _, live, rank, _ = plan
    slot = rank - turn * SLOTS
    return jnp.where(live & (slot >= 0) & (slot < SLOTS), owner * SLOTS + slot, -1)


def round_requests(plan, turn, n_dev):
    flat = round_flat(plan, turn)
    hit = (flat[:, None] == jnp.arange(n_dev * SLOTS)[None, :]) & plan[2][:, None]
    return jnp.sum(jnp.where(hit, plan[1][:, None] + 1, 0), axis=0) - 1


def picking(plan, turn, n_dev):
    return (
        round_flat(plan, turn)[:, None] == jnp.arange(n_dev * SLOTS)[None, :]
    ).astype(jnp.bfloat16)


def asked_hot(asked, rows_here):
    return (asked.reshape(-1)[:, None] == jnp.arange(rows_here)[None, :]).astype(jnp.bfloat16)


def mine_of(table):
    return lax.dynamic_slice_in_dim(table, lax.axis_index(AXES) * SLOTS, SLOTS, axis=1)


def swap(rows, n_dev):
    wide = rows.shape[-1]
    return lax.all_to_all(
        rows.reshape(n_dev, SLOTS, wide), AXES, 0, 0, tiled=True
    ).reshape(n_dev * SLOTS, wide)


def answer(asked, tables):
    hot = asked_hot(asked, tables[0].shape[0])
    return jnp.concatenate([to_low(matmul(hot, table)) for table in tables], axis=1)


def pick_rows(pick, rows):
    return (to_low(matmul(pick, rows[:, :D])), to_low(matmul(pick, rows[:, D:])))


def added(some, others):
    return jax.tree.map(jnp.add, some, others)


def fetch_rows(plan, answers, rounds, tables, n_dev):
    rows = pick_rows(picking(plan, 0, n_dev), swap(answers, n_dev))

    def more(state):
        turn, rows = state
        asked = mine_of(lax.all_gather(round_requests(plan, turn, n_dev), AXES, axis=0))
        pick = picking(plan, turn, n_dev)
        return (turn + 1, added(rows, pick_rows(pick, swap(answer(asked, tables), n_dev))))

    return lax.while_loop(lambda state: state[0] < rounds, more, (jnp.int32(1), rows))[1]


def collect(asked, sums, rows_here, n_dev):
    return jnp.einsum(
        "kc,kd->cd",
        asked_hot(asked, rows_here),
        swap(sums, n_dev),
        preferred_element_type=jnp.float32,
    )


def row_sums(pick, gradient):
    return to_low(jnp.einsum("nk,nd->kd", pick, gradient, preferred_element_type=jnp.float32))


def return_rows(plan, asked, rounds, first_sums, gradient, rows_here, n_dev):
    sums = collect(asked, first_sums, rows_here, n_dev)

    def more(state):
        turn, sums = state
        asked = mine_of(lax.all_gather(round_requests(plan, turn, n_dev), AXES, axis=0))
        pick = picking(plan, turn, n_dev)
        return (turn + 1, sums + collect(asked, row_sums(pick, gradient), rows_here, n_dev))

    return lax.while_loop(lambda state: state[0] < rounds, more, (jnp.int32(1), sums))[1]


ENC_BLOCKS = ((0, 3 * D), (3 * D, D), (9 * D, 2 * D), (12 * D, FF), (12 * D + FF, FF))
DEC_BLOCKS = (
    (4 * D, 3 * D),
    (7 * D, D),
    (8 * D, D),
    (11 * D, D),
    (12 * D + 2 * FF, FF),
    (12 * D + 3 * FF, FF),
)


def gather_offloaded(shard, blocks):
    part = jnp.concatenate([shard[:, low : low + width] for low, width in blocks], axis=1)
    return lax.all_gather(part, AXES, axis=0, tiled=True)


def split_blocks(part, blocks):
    gathered, at = ([], 0)
    for _, width in blocks:
        gathered.append(part[:, at : at + width])
        at += width
    return by_column(blocks, gathered)


def after(values, *others):
    return lax.optimization_barrier((values,) + others)[0]


def columns(layer_full, first_column, column_count):
    assert layer_full[first_column].shape[1] == column_count
    return layer_full[first_column]


def by_column(blocks, gathered):
    return {low: value for (low, _), value in zip(blocks, gathered)}


def shard_stats(final_rows, table_shard, targets, collective_ids):
    all_rows = gather_whole(final_rows, 128, collective_ids[0], 50, final_rows.shape[0] // 2)
    all_rows = all_rows.reshape(-1, D)
    logits = jnp.einsum("rd,vd->rv", all_rows, table_shard, preferred_element_type=jnp.float32)
    logits = with_layout_constraint(logits, Layout(major_to_minor=(0, 1)))
    low = lax.axis_index(AXES) * table_shard.shape[0]
    hot = (targets - low)[:, None] == jnp.arange(table_shard.shape[0])[None, :]
    largest = jnp.max(logits, axis=1)
    total = jnp.sum(jnp.exp(logits - largest[:, None]), axis=1)
    picked = jnp.sum(jnp.where(hot, logits, 0.0), axis=1)
    stats = jnp.stack([largest, total, picked]).reshape(8, -1)
    stats = gather_whole(stats, stats.shape[1] // 4, collective_ids[1], 20)
    stats = stats.reshape(-1, 3, largest.shape[0])
    peak = jnp.max(stats[:, 0], axis=0)
    log_own = peak + jnp.log(jnp.sum(stats[:, 1] * jnp.exp(stats[:, 0] - peak), axis=0))
    return (jnp.sum(stats[:, 2], axis=0) - log_own, log_own, logits, hot, all_rows)


def forward(token_rows, enc_full, dec_full_after, gain_rows, batch_data):
    (
        prompt_ids,
        decoder_input,
        targets,
        enc_allowed,
        self_allowed,
        cross_allowed,
        pair_local,
        valid,
    ) = batch_data
    pairs_here, seat_count = (prompt_ids.shape[0], decoder_input.shape[0])
    prompt_count = prompt_ids.size
    encoder_input = token_rows[:prompt_count].astype(jnp.float32)
    encoder_one, encoder_attn = self_forward(
        encoder_input,
        gain_rows[0],
        columns(enc_full, 0, 3 * D),
        columns(enc_full, 3 * D, D),
        enc_allowed,
        (pairs_here, P_MAX),
    )
    encoder_two, encoder_ffn = feed_forward(
        encoder_one,
        gain_rows[1],
        columns(enc_full, 12 * D, FF),
        columns(enc_full, 12 * D + FF, FF),
    )
    encoder_final = to_low(rms_norm(encoder_two, gain_rows[2]))
    cross_memory = to_low(matmul(encoder_final, columns(enc_full, 9 * D, 2 * D))).reshape(
        pairs_here, P_MAX, 2 * D
    )
    layer_full = dec_full_after(cross_memory)
    decoder_zero = token_rows[prompt_count:].astype(jnp.float32)
    decoder_one, decoder_attn = self_forward(
        decoder_zero,
        gain_rows[3],
        columns(layer_full, 4 * D, 3 * D),
        columns(layer_full, 7 * D, D),
        self_allowed,
        (seat_count, R_MAX),
    )
    decoder_two, decoder_cross = cross_forward(
        decoder_one,
        gain_rows[4],
        columns(layer_full, 8 * D, D),
        columns(layer_full, 11 * D, D),
        cross_memory,
        pair_local,
        cross_allowed,
        (seat_count, R_MAX),
    )
    decoder_three, decoder_ffn = feed_forward(
        decoder_two,
        gain_rows[5],
        columns(layer_full, 12 * D + 2 * FF, FF),
        columns(layer_full, 12 * D + 3 * FF, FF),
    )
    final_rows = to_low(final_norm(decoder_three, gain_rows[6]))
    stored = (
        encoder_input,
        encoder_one,
        encoder_two,
        encoder_attn,
        encoder_ffn,
        encoder_final,
        decoder_zero,
        decoder_one,
        decoder_two,
        decoder_three,
        decoder_attn,
        decoder_cross,
        decoder_ffn,
    )
    return (final_rows, stored)


def decoder_backward(layer_full, gain_rows, batch_data, stored, grad_final):
    enc_allowed, self_allowed, cross_allowed = batch_data[3:6]
    decoder_zero, decoder_one, decoder_two, decoder_three = stored[6:10]
    decoder_attn, decoder_cross, decoder_ffn = stored[10:]
    grad_three, gain_six = norm_backward(final_norm, decoder_three, gain_rows[6], grad_final)
    grad_two, gain_five, dec_ffn_pairs = feed_backward(
        decoder_two,
        gain_rows[5],
        columns(layer_full, 12 * D + 2 * FF, FF),
        columns(layer_full, 12 * D + 3 * FF, FF),
        decoder_ffn,
        grad_three,
    )
    grad_one, gain_four, grad_memory, cross_pairs = cross_backward(
        decoder_one,
        gain_rows[4],
        columns(layer_full, 8 * D, D),
        columns(layer_full, 11 * D, D),
        cross_allowed,
        decoder_cross,
        grad_two,
    )
    grad_zero, gain_three, dec_self_pairs = self_backward(
        decoder_zero,
        gain_rows[3],
        columns(layer_full, 4 * D, 3 * D),
        columns(layer_full, 7 * D, D),
        self_allowed,
        decoder_attn,
        grad_one,
    )
    return (
        (gain_three, gain_four, gain_five, gain_six),
        dec_self_pairs + cross_pairs + dec_ffn_pairs,
        grad_memory,
        grad_zero,
    )


def encoder_backward(layer_full, gain_rows, batch_data, stored, memory_low):
    enc_allowed = batch_data[3]
    encoder_input, encoder_one, encoder_two, encoder_attn, encoder_ffn, encoder_final = stored[:6]
    grad_encoder_final = matmul_back(memory_low, columns(layer_full, 9 * D, 2 * D))
    grad_encoder_two, gain_two = norm_backward(
        rms_norm, encoder_two, gain_rows[2], grad_encoder_final
    )
    grad_encoder_one, gain_one, enc_ffn_pairs = feed_backward(
        encoder_one,
        gain_rows[1],
        columns(layer_full, 12 * D, FF),
        columns(layer_full, 12 * D + FF, FF),
        encoder_ffn,
        grad_encoder_two,
    )
    grad_encoder_input, gain_zero, enc_self_pairs = self_backward(
        encoder_input,
        gain_rows[0],
        columns(layer_full, 0, 3 * D),
        columns(layer_full, 3 * D, D),
        enc_allowed,
        encoder_attn,
        grad_encoder_one,
    )
    pairs = enc_self_pairs + ((encoder_final, memory_low),) + enc_ffn_pairs
    return ((gain_zero, gain_one, gain_two), pairs, grad_encoder_input)


def apply_update(weight, moment, average, gradient, factor):
    clipped = gradient * factor
    moment_new = MOMENTUM * moment + clipped
    step_size = -LEARN_RATE * (clipped + MOMENTUM * moment_new)
    weight_new = weight + step_size
    return (
        weight_new,
        moment_new,
        AVERAGE_DECAY * average + (1.0 - AVERAGE_DECAY) * weight_new,
        step_size,
    )


def body(
    prompt_ids,
    prompt_lengths,
    response_ids,
    response_lengths,
    sequence_pair,
    chosen_flag,
    pair_microbatch,
    policy_embed,
    policy_layers,
    policy_gains,
    momentum_embed,
    momentum_layers,
    momentum_gains,
    average_embed,
    average_layers,
    average_gains,
    frozen_embed,
    frozen_layers,
    frozen_gains,
):
    n_dev = lax.axis_size(AXES)
    me = lax.axis_index(AXES)
    rows_here = policy_embed.shape[0]
    pairs_here = prompt_ids.shape[0]
    seat_count = response_ids.shape[0]
    decoder_input = jnp.concatenate(
        [jnp.zeros((seat_count, 1), jnp.int32), response_ids[:, :-1]], axis=1
    )
    pair_local = sequence_pair - me * pairs_here
    select_float = (pair_local[:, None] == jnp.arange(pairs_here)[None, :]).astype(jnp.float32)
    prompt_pos = jnp.arange(P_MAX)
    reply_pos = jnp.arange(R_MAX)
    prompt_keys = prompt_pos[None, :] < prompt_lengths[:, None]
    valid = reply_pos[None, :] < response_lengths[:, None]
    enc_allowed = jnp.broadcast_to(prompt_keys[:, None, :], (pairs_here, P_MAX, P_MAX))
    self_allowed = (reply_pos[:, None] >= reply_pos[None, :])[None] & valid[:, None, :]
    seat_keys = jnp.einsum("sp,pk->sk", select_float, prompt_keys.astype(jnp.float32)) > 0.5
    cross_allowed = jnp.broadcast_to(seat_keys[:, None, :], (seat_count, R_MAX, P_MAX))
    batch_data = (
        prompt_ids,
        decoder_input,
        response_ids,
        enc_allowed,
        self_allowed,
        cross_allowed,
        pair_local,
        valid,
    )
    token_ids = jnp.concatenate([prompt_ids.reshape(-1), decoder_input.reshape(-1)])
    token_live = jnp.concatenate([prompt_keys.reshape(-1), valid.reshape(-1)])
    plan = lookup_plan(token_ids, token_live, rows_here)
    packed = jnp.concatenate(
        [
            round_requests(plan, 0, n_dev),
            response_ids.reshape(-1),
            response_lengths,
            pair_local,
            chosen_flag,
            pair_microbatch,
            plan[5][None],
        ]
    )
    packed = jnp.pad(packed, (0, -packed.shape[0] % 1024)).reshape(8, -1)
    *policy_enc, notes = tree_gather(
        to_low(policy_layers), ENC_BLOCKS, WAVE_STEP, 1, 130, extra=packed
    )
    notes = notes.reshape(n_dev, -1)
    asked = mine_of(notes)
    at = n_dev * SLOTS
    cuts = []
    for width in (seat_count * R_MAX, seat_count, seat_count, seat_count, pairs_here, 1):
        cuts.append(notes[:, at : at + width])
        at += width
    targets, all_lengths, all_pair, all_flag, all_micro, all_rounds = cuts
    targets = targets.reshape(-1)
    rounds = jnp.max(all_rounds)
    all_select = (all_pair[:, :, None] == jnp.arange(pairs_here)).astype(jnp.float32)
    pair_micro = (all_micro[:, :, None] == jnp.arange(MICRO)).astype(jnp.float32)
    seat_micro = jnp.sum(all_select[:, :, :, None] * pair_micro[:, None], axis=2)
    chosen_float = all_flag.astype(jnp.float32)
    pair_total = jnp.sum(pair_micro, axis=(0, 1))
    token_total = jnp.sum(
        seat_micro * (chosen_float * all_lengths.astype(jnp.float32))[:, :, None], axis=(0, 1)
    )
    micro_counts = jnp.stack([pair_total, token_total])
    pair_divisor = jnp.sum(pair_micro * pair_total, axis=2)
    sequence_divisor = jnp.sum(seat_micro * token_total, axis=2)
    all_valid = reply_pos < all_lengths[:, :, None]

    policy_table = to_low(policy_embed)
    policy_low = to_low(after(policy_layers, policy_enc[0]))
    policy_dec = gather_offloaded(policy_low, DEC_BLOCKS)
    answers = answer(asked, (policy_table, frozen_embed))
    policy_tokens, frozen_tokens = fetch_rows(plan, answers, rounds, (policy_table, frozen_embed), n_dev)
    policy_layer_enc = by_column(ENC_BLOCKS, policy_enc)
    policy_layer_dec = split_blocks(policy_dec, DEC_BLOCKS)
    policy_layer_full = policy_layer_enc | policy_layer_dec
    def policy_after(memory):
        return policy_layer_dec

    def logp_of(token_logp):
        return jnp.sum(jnp.where(all_valid, token_logp.reshape(all_valid.shape), 0.0), axis=2)

    policy_rows, stored = forward(
        policy_tokens, policy_layer_enc, policy_after, policy_gains, batch_data
    )
    frozen_enc = gather_offloaded(after(frozen_layers, stored[5]), ENC_BLOCKS)
    frozen_dec = gather_offloaded(after(frozen_layers, policy_rows), DEC_BLOCKS)
    frozen_layer_enc = split_blocks(frozen_enc, ENC_BLOCKS)

    def frozen_after(memory):
        return split_blocks(after(frozen_dec, memory), DEC_BLOCKS)

    token_logp, log_own, logits, hot, all_rows = shard_stats(
        policy_rows, policy_table, targets, (3, 4)
    )
    policy_logp = logp_of(token_logp)
    row_slope = jnp.where(
        all_valid.reshape(-1)[:, None], hot.astype(jnp.float32) - jnp.exp(logits - log_own[:, None]), 0.0
    )
    row_slope = with_layout_constraint(to_low(row_slope), Layout(major_to_minor=(0, 1)))
    grad_final = scatter_final(row_slope, policy_table, 10)
    dec_gains, dec_pairs, grad_memory, grad_zero = decoder_backward(
        policy_layer_full, policy_gains, batch_data, stored, grad_final
    )
    frozen_inputs = after(frozen_tokens, grad_zero)
    frozen_rows, unused = forward(
        frozen_inputs, frozen_layer_enc, frozen_after, frozen_gains, batch_data
    )
    frozen_logp = logp_of(shard_stats(frozen_rows, frozen_embed, targets, (5, 6))[0])
    frozen_mean = lax.dynamic_index_in_dim(
        frozen_logp / all_lengths.astype(jnp.float32), me, 0, keepdims=False
    )

    sign_value = 2.0 * chosen_float - 1.0
    margin = PREFERENCE_BETA * jnp.sum(
        all_select * (sign_value * (policy_logp - frozen_logp))[:, :, None], axis=1
    )
    loss = (
        jnp.sum(jax.nn.softplus(-margin) / pair_divisor)
        - CHOSEN_WEIGHT * jnp.sum(chosen_float * policy_logp / sequence_divisor)
    ) / MICRO
    pair_slope = -PREFERENCE_BETA * jax.nn.sigmoid(-margin) / pair_divisor
    sequence_slope = (
        sign_value * jnp.sum(all_select * pair_slope[:, None, :], axis=2)
        - CHOSEN_WEIGHT * chosen_float / sequence_divisor
    ) / MICRO
    table_grad = jnp.einsum(
        "rc,rd->cd",
        row_slope,
        to_low(jnp.repeat(sequence_slope.reshape(-1), R_MAX)[:, None] * all_rows),
        preferred_element_type=jnp.float32,
    )
    slope_here = lax.dynamic_index_in_dim(sequence_slope, me, 0, keepdims=False)
    slope_rows = jnp.repeat(slope_here, R_MAX)[:, None]
    memory_slope = (select_float * slope_here[:, None])[:, :, None, None, None]
    memory_low = jnp.concatenate(
        [
            join_heads(to_low(jnp.sum(memory_slope * part[:, None], axis=0))).reshape(-1, D)
            for part in grad_memory
        ],
        axis=1,
    )
    enc_gains, enc_pairs, grad_encoder_input = encoder_backward(
        policy_layer_full, policy_gains, batch_data, stored, memory_low
    )
    gain_grads = jnp.stack(
        [jnp.sum(rows, axis=0) for rows in enc_gains]
        + [jnp.sum(slope_rows * rows, axis=0) for rows in dec_gains]
    )
    token_gradient = jnp.concatenate([grad_encoder_input, slope_rows * grad_zero], axis=0)
    enc_pairs = [(to_low(left), to_low(right)) for left, right in enc_pairs]
    scaled_pairs = []
    for left, right in dec_pairs:
        if left.dtype == jnp.float32:
            scaled_pairs.append((to_low(slope_rows * left), right))
        else:
            scaled_pairs.append((left, to_low(slope_rows * right)))
    token_gradient = to_low(token_gradient)
    first_sums = row_sums(picking(plan, 0, n_dev), token_gradient)
    table_grad = after(table_grad, first_sums)
    enc_pairs[0] = (after(enc_pairs[0][0], first_sums, table_grad), enc_pairs[0][1])
    embed_grad = table_grad + return_rows(
        plan, asked, rounds, first_sums, token_gradient, rows_here, n_dev
    )
    layer_grad = scatter_layers(scaled_pairs, enc_pairs, policy_layers.shape[0], 8)
    squares_local = jnp.sum(embed_grad * embed_grad) + jnp.sum(layer_grad * layer_grad)
    shared = jnp.concatenate([gain_grads, jnp.full((1, D), squares_local)], axis=0)
    shared = jnp.sum(gather_whole(shared, D, 9, 20), axis=0)
    gain_total, squares_total = (shared[:7], shared[7, 0])
    grad_norm = jnp.sqrt(squares_total + jnp.sum(gain_total * gain_total))
    factor = jnp.minimum(1.0, CLIP_NORM / grad_norm)
    embed_new = apply_update(policy_embed, momentum_embed, average_embed, embed_grad, factor)
    layers_new = apply_update(policy_layers, momentum_layers, average_layers, layer_grad, factor)
    gains_new = apply_update(policy_gains, momentum_gains, average_gains, gain_total, factor)
    return (
        loss,
        grad_norm,
        micro_counts,
        frozen_mean,
        embed_new[3],
        layers_new[0],
        gains_new[0],
        embed_new[1],
        layers_new[1],
        gains_new[1],
        embed_new[2],
        layers_new[2],
        gains_new[2],
    )


def solution(mesh):
    placed = (
        P(("dp", "fsdp"), None),
        P(("dp", "fsdp")),
        P(("dp", "fsdp"), None),
        P(("dp", "fsdp")),
        P(("dp", "fsdp")),
        P(("dp", "fsdp")),
        P(("dp", "fsdp")),
        P(("dp", "fsdp"), None),
        P(("dp", "fsdp"), None),
        P(),
        P(("dp", "fsdp"), None),
        P(("dp", "fsdp"), None),
        P(),
        P(("dp", "fsdp"), None),
        P(("dp", "fsdp"), None),
        P(),
        P(("dp", "fsdp"), None),
        P(("dp", "fsdp"), None),
        P(),
    )
    return jax.shard_map(
        body,
        mesh=mesh,
        in_specs=placed,
        out_specs=(
            P(),
            P(),
            P(),
            P(("dp", "fsdp")),
            P(("dp", "fsdp"), None),
            P(("dp", "fsdp"), None),
            P(),
            P(("dp", "fsdp"), None),
            P(("dp", "fsdp"), None),
            P(),
            P(("dp", "fsdp"), None),
            P(("dp", "fsdp"), None),
            P(),
        ),
        check_vma=False,
    )
```

```python
import functools

import jax
import jax.numpy as jnp
from jax import lax
from jax.experimental import pallas as pl
from jax.experimental.layout import Layout, with_layout_constraint
from jax.experimental.pallas import tpu as pltpu
from jax.sharding import PartitionSpec as P

D = 1024
HEADS = 16
HEAD = 64
FF = 4096
P_MAX = 192
R_MAX = 32
MICRO = 2


EPSILON = 1e-06
SCORE_SCALE = 0.125
PREFERENCE_BETA = 0.1
CHOSEN_WEIGHT = 1.0
MOMENTUM = 0.9
LEARN_RATE = 2000.0
AVERAGE_DECAY = 0.5
CLIP_NORM = 0.04
MASK_FILL = -1000000000.0
HIGHEST = lax.Precision.HIGHEST


def rms_norm(values, gain_row):
    return (
        values * lax.rsqrt(jnp.mean(values * values, axis=-1, keepdims=True) + EPSILON) * gain_row
    )


def final_norm(values, gain_row):
    return rms_norm(values, gain_row) * D ** (-0.5)


def to_low(values):
    return values.astype(jnp.bfloat16)


def matmul(left_side, right_side):
    return jnp.dot(left_side, right_side, preferred_element_type=jnp.float32)


def matmul_back(grad_low, weight):
    return jnp.einsum("re,de->rd", grad_low, weight, preferred_element_type=jnp.float32)


def split_heads(values):
    return values.reshape(values.shape[0], values.shape[1], HEADS, HEAD)


def scores_of(queries, key_rows, allowed):
    raw_scores = (
        jnp.einsum(
            "bqhe,bkhe->bhqk",
            split_heads(queries),
            split_heads(key_rows),
            preferred_element_type=jnp.float32,
        )
        * SCORE_SCALE
    )
    return jnp.where(allowed[:, None], raw_scores, MASK_FILL)


def attend_forward(queries, key_rows, values, allowed):
    scores = scores_of(queries, key_rows, allowed)
    log_total = jax.nn.logsumexp(scores, axis=-1, keepdims=True)
    softmax_out = to_low(jnp.exp(scores - log_total))
    mixed_out = jnp.einsum(
        "bhqk,bkhe->bqhe", softmax_out, split_heads(values), preferred_element_type=jnp.float32
    )
    return (to_low(mixed_out.reshape(queries.shape)), log_total)


def attend_backward(queries, key_rows, values, allowed, log_total, grad_mixed):
    softmax_out = jnp.exp(scores_of(queries, key_rows, allowed) - log_total)
    grad_heads = split_heads(to_low(grad_mixed))
    grad_values = jnp.einsum(
        "bhqk,bqhe->bhke", to_low(softmax_out), grad_heads, preferred_element_type=jnp.float32
    )
    grad_probs = jnp.einsum(
        "bqhe,bkhe->bhqk", grad_heads, split_heads(values), preferred_element_type=jnp.float32
    )
    grad_scores = to_low(
        softmax_out * (grad_probs - jnp.sum(grad_probs * softmax_out, axis=-1, keepdims=True))
    )
    grad_query = (
        jnp.einsum(
            "bhqk,bkhe->bqhe",
            grad_scores,
            split_heads(key_rows),
            preferred_element_type=jnp.float32,
        )
        * SCORE_SCALE
    )
    grad_keys = (
        jnp.einsum(
            "bhqk,bqhe->bhke", grad_scores, split_heads(queries), preferred_element_type=jnp.float32
        )
        * SCORE_SCALE
    )
    return (grad_query.reshape(queries.shape), grad_keys, grad_values)


def join_heads(values):
    return values.transpose(0, 2, 1, 3).reshape(values.shape[0], values.shape[2], D)


def self_forward(residual, gain_row, weight_three, weight_out, allowed, shape_pair):
    normed = to_low(rms_norm(residual, gain_row))
    triple = to_low(matmul(normed, weight_three)).reshape(shape_pair[0], shape_pair[1], 3 * D)
    mixed_out, log_total = attend_forward(
        triple[..., :D], triple[..., D : 2 * D], triple[..., 2 * D :], allowed
    )
    flat_mixed = mixed_out.reshape(-1, D)
    return (residual + matmul(flat_mixed, weight_out), (normed, triple, log_total, flat_mixed))


def norm_backward(norm, residual, gain_row, grad_normed):
    grad_residual = jax.vjp(lambda values: norm(values, gain_row), residual)[1](grad_normed)[0]
    return grad_residual, grad_normed * norm(residual, jnp.ones_like(gain_row))


def self_backward(residual, gain_row, weight_three, weight_out, allowed, stored, grad_out):
    normed, triple, log_total, flat_mixed = stored
    grad_mixed = matmul_back(to_low(grad_out), weight_out)
    queries = triple[..., :D]
    grad_query, grad_keys, grad_values = attend_backward(
        queries,
        triple[..., D : 2 * D],
        triple[..., 2 * D :],
        allowed,
        log_total,
        grad_mixed.reshape(queries.shape),
    )
    grads = (grad_query, join_heads(grad_keys), join_heads(grad_values))
    grad_triple = jnp.concatenate(grads, axis=-1).reshape(-1, 3 * D)
    grad_normed = matmul_back(to_low(grad_triple), weight_three)
    grad_residual, gain_rows = norm_backward(rms_norm, residual, gain_row, grad_normed)
    return (grad_out + grad_residual, gain_rows, ((normed, grad_triple), (flat_mixed, grad_out)))


def cross_forward(
    residual, gain_row, weight_query, weight_out, cross_memory, pair_local, allowed, shape_pair
):
    normed = to_low(rms_norm(residual, gain_row))
    queries = to_low(matmul(normed, weight_query)).reshape(shape_pair[0], shape_pair[1], D)
    seat_memory = jnp.broadcast_to(cross_memory[:1], (shape_pair[0],) + cross_memory.shape[1:])
    for pair in range(1, cross_memory.shape[0]):
        seat_memory = jnp.where(
            pair_local[:, None, None] == pair, cross_memory[pair][None], seat_memory
        )
    mixed_out, log_total = attend_forward(
        queries, seat_memory[..., :D], seat_memory[..., D:], allowed
    )
    flat_mixed = mixed_out.reshape(-1, D)
    return (
        residual + matmul(flat_mixed, weight_out),
        (normed, queries, seat_memory, log_total, flat_mixed),
    )


def cross_backward(residual, gain_row, weight_query, weight_out, allowed, stored, grad_out):
    normed, queries, seat_memory, log_total, flat_mixed = stored
    grad_mixed = matmul_back(to_low(grad_out), weight_out)
    grad_query, grad_keys, grad_values = attend_backward(
        queries,
        seat_memory[..., :D],
        seat_memory[..., D:],
        allowed,
        log_total,
        grad_mixed.reshape(queries.shape),
    )
    grad_query = grad_query.reshape(-1, D)
    grad_normed = matmul_back(to_low(grad_query), weight_query)
    grad_residual, gain_rows = norm_backward(rms_norm, residual, gain_row, grad_normed)
    return (
        grad_out + grad_residual,
        gain_rows,
        (grad_keys, grad_values),
        ((normed, grad_query), (flat_mixed, grad_out)),
    )


def feed_forward(residual, gain_row, weight_in, weight_out):
    normed = to_low(rms_norm(residual, gain_row))
    before = matmul(normed, weight_in)
    active = to_low(jax.nn.relu(before))
    return (
        residual + jnp.einsum("rf,df->rd", active, weight_out, preferred_element_type=jnp.float32),
        (normed, active),
    )


def feed_backward(residual, gain_row, weight_in, weight_out, stored, grad_out):
    normed, active = stored
    grad_active = matmul(to_low(grad_out), weight_out)
    grad_before = jnp.where(active > 0, grad_active, 0.0)
    grad_normed = matmul_back(to_low(grad_before), weight_in)
    grad_residual, gain_rows = norm_backward(rms_norm, residual, gain_row, grad_normed)
    return (grad_out + grad_residual, gain_rows, ((normed, grad_before), (grad_out, active)))


AXES = ("dp", "fsdp")


FF_STEP = 512


def norm_scale(values):
    return lax.rsqrt(jnp.mean(values * values, axis=-1, keepdims=True) + EPSILON)


def feed_kernel(residual_ref, gain_ref, in_ref, out_ref, result_ref, normed_ref):
    @pl.when(pl.program_id(0) == 0)
    def _():
        residual = residual_ref[...]
        normed_ref[...] = to_low(residual * norm_scale(residual) * gain_ref[...])
        result_ref[...] = residual

    before = jnp.dot(normed_ref[...], in_ref[...], preferred_element_type=jnp.float32)
    active = to_low(jax.nn.relu(before))
    result_ref[...] += lax.dot_general(
        active, out_ref[...], (((1,), (1,)), ((), ())), preferred_element_type=jnp.float32
    )


def weight_spec(start):
    return pl.BlockSpec((D, FF_STEP), lambda step: (0, step + start // FF_STEP))


def whole_spec(shape):
    return pl.BlockSpec(shape, lambda step: (0,) * len(shape))


def feed_cost(rows):
    return pl.CostEstimate(flops=4 * rows * D * FF, bytes_accessed=4 * D * FF, transcendentals=0)


def feed_streamed(residual, gain_row, weight_in, weight_out):
    rows = residual.shape[0]
    (source_in, start_in), (source_out, start_out) = (weight_in, weight_out)
    result = pl.pallas_call(
        feed_kernel,
        grid=(FF // FF_STEP,),
        out_shape=jax.ShapeDtypeStruct((rows, D), jnp.float32),
        in_specs=[
            whole_spec((rows, D)),
            whole_spec((1, D)),
            weight_spec(start_in),
            weight_spec(start_out),
        ],
        out_specs=whole_spec((rows, D)),
        scratch_shapes=[pltpu.VMEM((rows, D), jnp.bfloat16)],
        compiler_params=pltpu.CompilerParams(vmem_limit_bytes=40 * 2**20),
        cost_estimate=feed_cost(rows),
    )(residual, gain_row[None], source_in, source_out)
    return (result, None)


SLOTS = 24
MESH = pl.DeviceIdType.MESH


def device_bits():
    bits = []
    for axis in AXES:
        mask = lax.axis_size(axis) // 2
        while mask:
            bits.append((axis, mask))
            mask //= 2
    return bits


def scatter_orders():
    core, across = (("dp", 1), ("dp", 2))
    inner = [bit for bit in reversed(device_bits()) if bit[0] == "fsdp"]
    first, rest = inner[:1], inner[1:]
    return (
        [core, across] + rest + first,
        [core] + inner + [across],
        [core, across] + first + rest,
        [core] + first + [across] + rest,
    )


def lane_widths(width):
    if width % D == 0:
        return (3 * width // 8, 3 * width // 8, width // 8, width // 8)
    return (width // 4,) * 4


def bit_of(bit):
    axis, mask = bit
    return (lax.axis_index(axis) // mask) % 2


def partner(bit):
    axis, mask = bit
    return {axis: lax.axis_index(axis) + mask * (1 - 2 * bit_of(bit))}


def greet(bits):
    barrier = pltpu.get_barrier_semaphore()
    for bit in bits:
        pl.semaphore_signal(barrier, inc=1, device_id=partner(bit), device_id_type=MESH)
    pl.semaphore_wait(barrier, len(bits))


def gather_kernel(bits, n_in, waves, *refs):
    ins, outs, (own_sem, send_sem, recv_sem) = (refs[:n_in], refs[n_in:-3], refs[-3:])
    mine = {bit: bit_of(bit) for bit in bits}
    depth = len(bits)
    greet(bits)
    index, sent, kept = ({}, {}, {})
    for turn in range(len(waves) + depth):
        for step in range(depth + 1):
            wave = turn - step
            if not 0 <= wave < len(waves):
                continue
            for lane, (number, which, start, low, width, first, count, order) in enumerate(
                waves[wave]
            ):
                slot = index.setdefault((wave, lane), len(index))
                lead = tuple(
                    pl.ds(0, 2) if bit in order[:step] else pl.ds(mine[bit], 1) for bit in bits
                )
                place = outs[which].at[lead + (pl.ds(first, count), pl.ds(low, width))]
                source = place
                if step == 0:
                    whole = (slice(None),) * depth
                    source = ins[number].at[whole + (pl.ds(first, count), pl.ds(start, width))]
                    kept[slot] = pltpu.make_async_copy(source, place, own_sem.at[slot])
                    kept[slot].start()
                else:
                    sent[slot, step - 1].wait_recv()
                if step == 1:
                    kept[slot].wait()
                if step < depth:
                    sent[slot, step] = pltpu.make_async_remote_copy(
                        src_ref=source,
                        dst_ref=place,
                        send_sem=send_sem.at[slot, step],
                        recv_sem=recv_sem.at[slot, step],
                        device_id=partner(order[step]),
                        device_id_type=MESH,
                    )
                    sent[slot, step].start()
    for copy in sent.values():
        copy.wait_send()


def busy_for(micros):
    return pl.CostEstimate(flops=0, bytes_accessed=int(micros * 3.4e6), transcendentals=0)


def tree_gather(shard, blocks, step, collective_id, micros, row_step=None, extra=None):
    bits = device_bits()
    rows = shard.shape[0]
    row_step = row_step or rows
    waves = []
    for which, (start, width) in enumerate(blocks):
        for low in range(0, width, step):
            for first in range(0, rows, row_step):
                wave, at = ([], low)
                for lane, order in zip(lane_widths(step), scatter_orders()):
                    piece = (0, which, start + at, at, lane, first, row_step)
                    wave.append(piece + (tuple(reversed(order)),))
                    at += lane
                waves.append(wave)
    operands = [shard]
    shapes = [((rows, width), shard.dtype) for _, width in blocks]
    if extra is not None:
        operands.append(extra)
        shapes.append((extra.shape, extra.dtype))
        piece = (1, len(blocks), 0, 0, extra.shape[1], 0, extra.shape[0])
        waves[0].append(piece + (tuple(reversed(scatter_orders()[0])),))
    total = sum(len(wave) for wave in waves)
    gathered = pl.pallas_call(
        functools.partial(gather_kernel, bits, len(operands), waves),
        out_shape=[
            jax.ShapeDtypeStruct((2,) * len(bits) + shape, dtype) for shape, dtype in shapes
        ],
        in_specs=[pl.BlockSpec(memory_space=pl.ANY)] * len(operands),
        out_specs=[pl.BlockSpec(memory_space=pl.ANY)] * len(shapes),
        scratch_shapes=[
            pltpu.SemaphoreType.DMA((total,)),
            pltpu.SemaphoreType.DMA((total, len(bits))),
            pltpu.SemaphoreType.DMA((total, len(bits))),
        ],
        compiler_params=pltpu.CompilerParams(collective_id=collective_id, has_side_effects=True),
        cost_estimate=busy_for(micros),
    )(*[value.reshape((1,) * len(bits) + value.shape) for value in operands])
    return [value.reshape((-1, shape[1])) for value, (shape, _) in zip(gathered, shapes)]


def gather_whole(values, step, collective_id, micros, row_step=None):
    blocks = [(0, values.shape[1])]
    full = tree_gather(values, blocks, step, collective_id, micros, row_step)[0]
    return full.reshape((-1,) + values.shape)


def total_kernel(sizes, x_ref, sum_ref, *scratch):
    held, send_sem, recv_sem = (scratch[:2], scratch[2:4], scratch[4:6])
    barrier = pltpu.get_barrier_semaphore()
    peers = [(axis, hop) for axis, size in sizes for hop in range(1, size)]

    def peer(axis, size, hop):
        return {axis: lax.rem(lax.axis_index(axis) + hop, size)}

    for axis, hop in peers:
        pl.semaphore_signal(
            barrier, inc=1, device_id=peer(axis, dict(sizes)[axis], hop), device_id_type=MESH
        )
    pl.semaphore_wait(barrier, len(peers))
    value = x_ref[...]
    for turn, (axis, size) in enumerate(sizes):
        me = lax.axis_index(axis)
        held[turn][me] = value
        copies = []
        for hop in range(1, size):
            copies.append(
                pltpu.make_async_remote_copy(
                    src_ref=held[turn].at[me],
                    dst_ref=held[turn].at[me],
                    send_sem=send_sem[turn].at[hop],
                    recv_sem=recv_sem[turn].at[hop],
                    device_id=peer(axis, size, hop),
                    device_id_type=MESH,
                )
            )
            copies[-1].start()
        for hop, copy in enumerate(copies, 1):
            other = lax.rem(me + size - hop, size)
            pltpu.make_async_remote_copy(
                src_ref=held[turn].at[other],
                dst_ref=held[turn].at[other],
                send_sem=send_sem[turn].at[hop],
                recv_sem=recv_sem[turn].at[hop],
                device_id=peer(axis, size, hop),
                device_id_type=MESH,
            ).wait_recv()
        value = held[turn][0]
        for other in range(1, size):
            value = value + held[turn][other]
        for copy in copies:
            copy.wait_send()
    sum_ref[...] = value


def total_of(tile, collective_id):
    sizes = [(axis, lax.axis_size(axis)) for axis in reversed(AXES)]
    in_vmem = pl.BlockSpec(memory_space=pltpu.VMEM)
    marks = [pltpu.SemaphoreType.DMA((size,)) for _, size in sizes]
    return pl.pallas_call(
        functools.partial(total_kernel, sizes),
        out_shape=jax.ShapeDtypeStruct(tile.shape, jnp.float32),
        in_specs=[in_vmem],
        out_specs=in_vmem,
        scratch_shapes=[pltpu.VMEM((size,) + tile.shape, jnp.float32) for _, size in sizes]
        + marks
        + marks,
        compiler_params=pltpu.CompilerParams(collective_id=collective_id, has_side_effects=True),
        cost_estimate=busy_for(12),
    )(tile)


CORE_SLOTS = 2


def scatter_kernel(bits, plan, *refs):
    n_waves, slots, wide, widths = (plan["waves"], plan["slots"], plan["wide"], plan["widths"])
    n_ins, n_loaded = (plan["operands"], len(plan["loads"]))
    ins, out_ref = (refs[:n_ins], refs[n_ins])
    loaded, rest_refs = (refs[n_ins + 1 : n_ins + 1 + n_loaded], refs[n_ins + 1 + n_loaded :])
    buffers = [rest_refs[6 * lane : 6 * lane + 6] for lane in range(len(widths))]
    load_sem, send_sem, recv_sem, free_sem = rest_refs[6 * len(widths) :]
    depth = len(bits)
    mine = {bit: bit_of(bit) for bit in bits}
    core = scatter_orders()[0][0]
    rest = [bit for bit in bits if bit != core]

    def half(order, step, kept):
        bit_at = {bit: pl.ds(mine[bit], 1) for bit in order[1:step]}
        last = mine[order[step]] if kept else 1 - mine[order[step]]
        bit_at[order[step]] = pl.ds(last, 1)
        return tuple(bit_at.get(bit, pl.ds(0, 2)) for bit in rest)

    def span_of(step):
        return CORE_SLOTS if step == 0 else slots

    def copy(wave, lane, step, order):
        send_core, from_core, total, narrow, arrived, arrived_wide = buffers[lane]
        slot = lax.rem(wave, span_of(step))
        if step == 0:
            source, target = (send_core.at[slot], from_core.at[slot])
        else:
            source = (total if step in wide else narrow).at[(slot,) + half(order, step, False)]
            target = arrived_wide if step in wide else arrived
            target = target.at[(slot,) + half(order, step, True)]
        return pltpu.make_async_remote_copy(
            src_ref=source,
            dst_ref=target,
            send_sem=send_sem.at[lane, slot, step],
            recv_sem=recv_sem.at[lane, slot, step],
            device_id=partner(order[step]),
            device_id_type=MESH,
        )

    def kept_entries(order, step):
        left = [bit for bit in rest if bit not in order[: step + 1]]
        for number in range(2 ** len(left)):
            chosen = {bit: (number >> place) % 2 for place, bit in enumerate(reversed(left))}
            here = tuple(chosen.get(bit, mine[bit]) for bit in rest)
            came = tuple(1 - mine[bit] if bit == order[step] else at for bit, at in zip(rest, here))
            yield here, came

    def visit(wave, lane, step, order):
        send_core, from_core, total, narrow, arrived, arrived_wide = buffers[lane]
        low, width = (sum(widths[:lane]), widths[lane])
        slot = lax.rem(wave, span_of(step))
        reuse = wave >= span_of(step)

        def keep(at, value, next_step):
            total[(slot,) + at] = value
            if next_step not in wide:
                narrow[(slot,) + at] = value.astype(jnp.bfloat16)

        if step == 0:

            @pl.when(reuse)
            def _():
                copy(wave, lane, 0, order).wait_send()

            def put(at, value):
                send_core[(slot,) + at] = value

            plan["produce"](loaded, wave, low, width, 1 - mine[core], put)
        else:
            copy(wave, lane, step - 1, order).wait_recv()
            if step == 1:
                core_slot = lax.rem(wave, CORE_SLOTS)

                @pl.when(reuse)
                def _():
                    for old in range(1, depth):
                        copy(wave, lane, old, order).wait_send()

                def add(at, value):
                    keep(at, value + from_core[(core_slot,) + at], 1)

                plan["produce"](loaded, wave, low, width, mine[core], add)
            else:
                source = arrived_wide if step - 1 in wide else arrived
                for here, came in kept_entries(order, step - 1):
                    value = total[(slot,) + here] + source[(slot,) + came].astype(jnp.float32)
                    if step == depth:
                        start = plan["column"](wave) + low
                        out_ref[:, pl.ds(pl.multiple_of(start, 128), width)] = value
                    else:
                        keep(here, value, step)

            @pl.when(wave + span_of(step - 1) < n_waves)
            def _():
                pl.semaphore_signal(
                    free_sem.at[lane, lax.rem(wave, span_of(step - 1)), step - 1],
                    inc=1,
                    device_id=partner(order[step - 1]),
                    device_id_type=MESH,
                )

        if step < depth:

            @pl.when(reuse)
            def _():
                pl.semaphore_wait(free_sem.at[lane, slot, step], 1)

            copy(wave, lane, step, order).start()

    loads = []
    for number, (_, parts) in enumerate(plan["loads"]):
        for operand, place in parts:
            at = loaded[number].at[place] if place else loaded[number]
            loads.append(pltpu.make_async_copy(ins[operand], at, load_sem.at[operand]))
            loads[-1].start()

    def turn_of(turn, carry):
        for step in range(depth + 1):
            wave = turn - step

            @pl.when((wave >= 0) & (wave < n_waves))
            def _():
                if step == 0:
                    for late, count in plan["waits"]:

                        @pl.when(wave == late)
                        def _():
                            for load in loads[slice(*count)]:
                                load.wait()

                for lane, order in enumerate(plan["orders"]):
                    visit(wave, lane, step, order)

        return carry

    greet(bits)
    lax.fori_loop(0, n_waves + depth, turn_of, 0)
    for step in range(depth):
        for wave in range(max(0, n_waves - span_of(step)), n_waves):
            for lane, order in enumerate(plan["orders"]):
                copy(wave, lane, step, order).wait_send()


def tree_scatter(operands, plan, collective_id, micros):
    bits = device_bits()
    slots, widths, rows = (plan["slots"], plan["widths"], plan["rows"])
    plan = dict(plan, operands=len(operands))
    scratch = [pltpu.VMEM(shape, jnp.bfloat16) for shape, _ in plan["loads"]]
    for width in widths:
        entries = (2,) * (len(bits) - 1) + (rows, width)
        core_buffer = pltpu.VMEM((CORE_SLOTS,) + entries, jnp.float32)
        low_buffer = pltpu.VMEM((slots,) + entries, jnp.bfloat16)
        sums = pltpu.VMEM((slots,) + entries, jnp.float32)
        wide_buffer = sums if plan["wide"] else pltpu.VMEM((8, 128), jnp.float32)
        scratch += [core_buffer, core_buffer, sums, low_buffer, low_buffer, wide_buffer]
    marks = (len(widths), slots, len(bits))
    return pl.pallas_call(
        functools.partial(scatter_kernel, bits, plan),
        out_shape=jax.ShapeDtypeStruct((rows, plan["waves"] * sum(widths)), jnp.float32),
        in_specs=[pl.BlockSpec(memory_space=pl.ANY)] * len(operands),
        out_specs=pl.BlockSpec(memory_space=pltpu.VMEM),
        scratch_shapes=scratch
        + [
            pltpu.SemaphoreType.DMA((len(operands),)),
            pltpu.SemaphoreType.DMA(marks),
            pltpu.SemaphoreType.DMA(marks),
            pltpu.SemaphoreType.REGULAR(marks),
        ],
        compiler_params=pltpu.CompilerParams(
            collective_id=collective_id, has_side_effects=True, vmem_limit_bytes=60 * 2**20
        ),
        cost_estimate=busy_for(micros),
    )(*operands)


def unit_of(block, blocks):
    edges, most = ([], sum(blocks))
    for count in blocks[:-1]:
        edges.append(count + (edges[-1] if edges else 0))
    return sum(lax.div(block + (most - edge), most) for edge in edges)


def put_rows(value, across, rows, put):
    rest_count = (value.shape[0] // rows).bit_length() - 1
    for number in range(2**rest_count):
        at = tuple((number >> place) % 2 for place in reversed(range(rest_count)))
        put((across,) + at, value[number * rows : (number + 1) * rows])


def layer_products(dec_blocks, enc_blocks, rows, loaded, wave, low, width, core, put):
    dec_left, dec_right, enc_left, enc_right = loaded
    dec_waves = sum(dec_blocks)
    quarter = D // 4

    def product(left, right, blocks, block):
        unit = unit_of(block, blocks)
        sides = right[:, pl.ds(pl.multiple_of(block * D + low, 128), width)]
        for across in range(2):
            some = pl.ds(pl.multiple_of((2 * across + core) * quarter, quarter), quarter)
            value = lax.dot_general(
                left[unit, :, some],
                sides,
                (((0,), (0,)), ((), ())),
                preferred_element_type=jnp.float32,
            )
            put_rows(value, across, rows, put)

    @pl.when(wave < dec_waves)
    def _():
        product(dec_left, dec_right, dec_blocks, wave)

    @pl.when(wave >= dec_waves)
    def _():
        product(enc_left, enc_right, enc_blocks, wave - dec_waves)


def layer_column(wave):
    is_enc = lax.div(wave, 14)
    block = wave - is_enc * 14

    def past(edge):
        return lax.div(block + 14 - edge, 14)

    dec_shift = 4 + 2 * past(5) + 8 * past(6)
    enc_shift = 5 * past(4) + past(6)
    shift = dec_shift + is_enc * (enc_shift - dec_shift)
    return (block + shift) * D


def scatter_layers(dec_pairs, enc_pairs, rows, collective_id):
    operands, loads, counts = ([], [], [])
    for pairs in (dec_pairs, enc_pairs):
        tokens, parts, at = (pairs[0][0].shape[0], [], 0)
        for unit, (left_side, _) in enumerate(pairs):
            parts.append((len(operands), (unit,)))
            operands.append(left_side)
        loads.append(((len(pairs), tokens, D), parts))
        parts = []
        for _, right_side in pairs:
            parts.append((len(operands), (slice(None), pl.ds(at, right_side.shape[1]))))
            operands.append(right_side)
            at += right_side.shape[1]
        loads.append(((tokens, at), parts))
        counts.append([right_side.shape[1] // D for _, right_side in pairs])
    dec_loads = 2 * len(dec_pairs)
    plan = {
        "waves": sum(counts[0]) + sum(counts[1]),
        "slots": 6,
        "widths": lane_widths(D),
        "orders": scatter_orders(),
        "rows": rows,
        "wide": (),
        "loads": loads,
        "waits": ((0, (0, dec_loads)), (sum(counts[0]), (dec_loads, None))),
        "produce": functools.partial(layer_products, counts[0], counts[1], rows),
        "column": layer_column,
    }
    return tree_scatter(operands, plan, collective_id, 210)


def final_products(step, rows, loaded, wave, low, width, core, put):
    left, right = loaded
    sides = right[:, pl.ds(pl.multiple_of(wave * step + low, 128), width)]
    for across in range(2):
        value = jnp.dot(left[across, core], sides, preferred_element_type=jnp.float32)
        put_rows(value, across, rows, put)


def scatter_final(grad_logits, table, collective_id):
    bits = device_bits()
    n_dev, step, width = (2 ** len(bits), 256, table.shape[1])
    rows_all = grad_logits.shape[0] // n_dev
    turns = max(1, n_dev // 32)
    rows = rows_all // turns
    sums = []
    for turn in range(turns):
        some = grad_logits.reshape(n_dev, rows_all, -1)[:, turn * rows : (turn + 1) * rows]
        some = some.reshape(2, 2, n_dev // 4 * rows, -1)
        plan = {
            "waves": width // step,
            "slots": width // step,
            "widths": (step // 2, step // 2),
            "orders": scatter_orders()[:2],
            "rows": rows,
            "wide": (len(bits) - 2, len(bits) - 1),
            "loads": [(some.shape, [(0, ())]), (table.shape, [(1, ())])],
            "waits": ((0, (0, 2)),),
            "produce": functools.partial(final_products, step, rows),
            "column": lambda wave: wave * step,
        }
        sums.append(tree_scatter([some, table], plan, collective_id + turn, 60))
    return jnp.concatenate(sums, axis=0)


def lookup_plan(ids, live, rows_here):
    count = ids.shape[0]
    owner = ids // rows_here
    same = (ids[:, None] == ids[None, :]) & live[None, :]
    earlier = jnp.arange(count)[None, :] < jnp.arange(count)[:, None]
    first = live & ~jnp.any(same & earlier, axis=1)
    below = first[None, :] & (owner[:, None] == owner[None, :]) & (ids[None, :] < ids[:, None])
    rank = jnp.sum(below.astype(jnp.int32), axis=1)
    rounds = jnp.max(jnp.where(live, rank, 0)) // SLOTS + 1
    return (owner, ids - owner * rows_here, first, live, rank, rounds)


def round_flat(plan, turn):
    owner, _, _, live, rank, _ = plan
    slot = rank - turn * SLOTS
    return jnp.where(live & (slot >= 0) & (slot < SLOTS), owner * SLOTS + slot, -1)


def round_requests(plan, turn, n_dev):
    flat = round_flat(plan, turn)
    hit = (flat[:, None] == jnp.arange(n_dev * SLOTS)[None, :]) & plan[2][:, None]
    return jnp.sum(jnp.where(hit, plan[1][:, None] + 1, 0), axis=0) - 1


def picking(plan, turn, n_dev):
    return (
        round_flat(plan, turn)[:, None] == jnp.arange(n_dev * SLOTS)[None, :]
    ).astype(jnp.bfloat16)


def asked_hot(asked, rows_here):
    return (asked.reshape(-1)[:, None] == jnp.arange(rows_here)[None, :]).astype(jnp.bfloat16)


def mine_of(table):
    return lax.dynamic_slice_in_dim(table, lax.axis_index(AXES) * SLOTS, SLOTS, axis=1)


def swap(rows, n_dev):
    wide = rows.shape[-1]
    return lax.all_to_all(
        rows.reshape(n_dev, SLOTS, wide), AXES, 0, 0, tiled=True
    ).reshape(n_dev * SLOTS, wide)


def answer(asked, tables):
    hot = asked_hot(asked, tables[0].shape[0])
    return jnp.concatenate([to_low(matmul(hot, table)) for table in tables], axis=1)


def pick_rows(pick, rows):
    return (to_low(matmul(pick, rows[:, :D])), to_low(matmul(pick, rows[:, D:])))


def added(some, others):
    return jax.tree.map(jnp.add, some, others)


def fetch_rows(plan, answers, rounds, tables, n_dev):
    rows = pick_rows(picking(plan, 0, n_dev), swap(answers, n_dev))

    def more(state):
        turn, rows = state
        asked = mine_of(lax.all_gather(round_requests(plan, turn, n_dev), AXES, axis=0))
        pick = picking(plan, turn, n_dev)
        return (turn + 1, added(rows, pick_rows(pick, swap(answer(asked, tables), n_dev))))

    return lax.while_loop(lambda state: state[0] < rounds, more, (jnp.int32(1), rows))[1]


def collect(asked, sums, rows_here, n_dev):
    return jnp.einsum(
        "kc,kd->cd",
        asked_hot(asked, rows_here),
        swap(sums, n_dev),
        preferred_element_type=jnp.float32,
    )


def row_sums(pick, gradient):
    return to_low(jnp.einsum("nk,nd->kd", pick, gradient, preferred_element_type=jnp.float32))


def return_rows(plan, asked, rounds, first_sums, gradient, table_grad, n_dev):
    rows_here = table_grad.shape[0]

    def more(state):
        turn, sums = state
        asked = mine_of(lax.all_gather(round_requests(plan, turn, n_dev), AXES, axis=0))
        pick = picking(plan, turn, n_dev)
        return (turn + 1, sums + collect(asked, row_sums(pick, gradient), rows_here, n_dev))

    sums = lax.while_loop(lambda state: state[0] < rounds, more, (jnp.int32(1), table_grad))[1]
    return sums + collect(asked, first_sums, rows_here, n_dev)


ENC_BLOCKS = ((0, 3 * D), (3 * D, D), (9 * D, 2 * D), (12 * D, FF), (12 * D + FF, FF))
DEC_BLOCKS = (
    (4 * D, 3 * D),
    (7 * D, D),
    (8 * D, D),
    (11 * D, D),
    (12 * D + 2 * FF, FF),
    (12 * D + 3 * FF, FF),
)


def gather_offloaded(shard, blocks):
    part = jnp.concatenate([shard[:, low : low + width] for low, width in blocks], axis=1)
    return lax.all_gather(part, AXES, axis=0, tiled=True)


def split_blocks(part, blocks):
    gathered, at = ({}, 0)
    for low, width in blocks:
        gathered[low] = (part, at, width)
        at += width
    return gathered


def after(values, *others):
    return lax.optimization_barrier((values,) + others)[0]


def columns(layer_full, first_column, column_count):
    part, start, width = layer_full[first_column]
    assert width == column_count
    return part[:, start : start + width]


def by_column(blocks, gathered):
    return {low: (value, 0, width) for (low, width), value in zip(blocks, gathered)}


def feed(residual, gain_row, layer_full, first_column, streamed):
    if streamed:
        weights = [layer_full[low][:2] for low in (first_column, first_column + FF)]
        return feed_streamed(residual, gain_row, *weights)
    weights = [columns(layer_full, low, FF) for low in (first_column, first_column + FF)]
    return feed_forward(residual, gain_row, *weights)


def shard_stats(final_rows, table_shard, targets, collective_ids):
    all_rows = gather_whole(final_rows, D, collective_ids[0], 45, final_rows.shape[0] // 4)
    all_rows = all_rows.reshape(-1, D)
    logits = jnp.einsum("rd,vd->rv", all_rows, table_shard, preferred_element_type=jnp.float32)
    logits = with_layout_constraint(logits, Layout(major_to_minor=(0, 1)))
    low = lax.axis_index(AXES) * table_shard.shape[0]
    hot = (targets - low)[:, None] == jnp.arange(table_shard.shape[0])[None, :]
    largest = jnp.max(logits, axis=1)
    total = jnp.sum(jnp.exp(logits - largest[:, None]), axis=1)
    picked = jnp.sum(jnp.where(hot, logits, 0.0), axis=1)
    stats = jnp.concatenate([part.reshape(8, -1) for part in (largest, total, picked)], axis=0)
    stats = gather_whole(stats, stats.shape[1], collective_ids[1], 20)
    peak = jnp.max(stats[:, :8], axis=0)
    log_own = peak + jnp.log(jnp.sum(stats[:, 8:16] * jnp.exp(stats[:, :8] - peak), axis=0))
    token_logp = (jnp.sum(stats[:, 16:], axis=0) - log_own).reshape(-1)
    return (token_logp, log_own.reshape(-1), logits, hot, all_rows)


def forward(token_rows, enc_full, dec_full_after, gain_rows, batch_data, streamed=False):
    (
        prompt_ids,
        decoder_input,
        targets,
        enc_allowed,
        self_allowed,
        cross_allowed,
        pair_local,
        valid,
    ) = batch_data
    pairs_here, seat_count = (prompt_ids.shape[0], decoder_input.shape[0])
    prompt_count = prompt_ids.size
    encoder_input = token_rows[:prompt_count].astype(jnp.float32)
    encoder_one, encoder_attn = self_forward(
        encoder_input,
        gain_rows[0],
        columns(enc_full, 0, 3 * D),
        columns(enc_full, 3 * D, D),
        enc_allowed,
        (pairs_here, P_MAX),
    )
    encoder_two, encoder_ffn = feed(encoder_one, gain_rows[1], enc_full, 12 * D, streamed)
    encoder_final = to_low(rms_norm(encoder_two, gain_rows[2]))
    cross_memory = to_low(matmul(encoder_final, columns(enc_full, 9 * D, 2 * D))).reshape(
        pairs_here, P_MAX, 2 * D
    )
    layer_full = dec_full_after(cross_memory)
    decoder_zero = token_rows[prompt_count:].astype(jnp.float32)
    decoder_one, decoder_attn = self_forward(
        decoder_zero,
        gain_rows[3],
        columns(layer_full, 4 * D, 3 * D),
        columns(layer_full, 7 * D, D),
        self_allowed,
        (seat_count, R_MAX),
    )
    decoder_two, decoder_cross = cross_forward(
        decoder_one,
        gain_rows[4],
        columns(layer_full, 8 * D, D),
        columns(layer_full, 11 * D, D),
        cross_memory,
        pair_local,
        cross_allowed,
        (seat_count, R_MAX),
    )
    decoder_three, decoder_ffn = feed(
        decoder_two, gain_rows[5], layer_full, 12 * D + 2 * FF, streamed
    )
    final_rows = to_low(final_norm(decoder_three, gain_rows[6]))
    stored = (
        encoder_input,
        encoder_one,
        encoder_two,
        encoder_attn,
        encoder_ffn,
        encoder_final,
        decoder_zero,
        decoder_one,
        decoder_two,
        decoder_three,
        decoder_attn,
        decoder_cross,
        decoder_ffn,
    )
    return (final_rows, stored)


def decoder_backward(layer_full, gain_rows, batch_data, stored, grad_final):
    enc_allowed, self_allowed, cross_allowed = batch_data[3:6]
    decoder_zero, decoder_one, decoder_two, decoder_three = stored[6:10]
    decoder_attn, decoder_cross, decoder_ffn = stored[10:]
    grad_three, gain_six = norm_backward(final_norm, decoder_three, gain_rows[6], grad_final)
    grad_two, gain_five, dec_ffn_pairs = feed_backward(
        decoder_two,
        gain_rows[5],
        columns(layer_full, 12 * D + 2 * FF, FF),
        columns(layer_full, 12 * D + 3 * FF, FF),
        decoder_ffn,
        grad_three,
    )
    grad_one, gain_four, grad_memory, cross_pairs = cross_backward(
        decoder_one,
        gain_rows[4],
        columns(layer_full, 8 * D, D),
        columns(layer_full, 11 * D, D),
        cross_allowed,
        decoder_cross,
        grad_two,
    )
    grad_zero, gain_three, dec_self_pairs = self_backward(
        decoder_zero,
        gain_rows[3],
        columns(layer_full, 4 * D, 3 * D),
        columns(layer_full, 7 * D, D),
        self_allowed,
        decoder_attn,
        grad_one,
    )
    return (
        (gain_three, gain_four, gain_five, gain_six),
        dec_self_pairs + cross_pairs + dec_ffn_pairs,
        grad_memory,
        grad_zero,
    )


def encoder_backward(layer_full, gain_rows, batch_data, stored, memory_low):
    enc_allowed = batch_data[3]
    encoder_input, encoder_one, encoder_two, encoder_attn, encoder_ffn, encoder_final = stored[:6]
    grad_encoder_final = matmul_back(memory_low, columns(layer_full, 9 * D, 2 * D))
    grad_encoder_two, gain_two = norm_backward(
        rms_norm, encoder_two, gain_rows[2], grad_encoder_final
    )
    grad_encoder_one, gain_one, enc_ffn_pairs = feed_backward(
        encoder_one,
        gain_rows[1],
        columns(layer_full, 12 * D, FF),
        columns(layer_full, 12 * D + FF, FF),
        encoder_ffn,
        grad_encoder_two,
    )
    grad_encoder_input, gain_zero, enc_self_pairs = self_backward(
        encoder_input,
        gain_rows[0],
        columns(layer_full, 0, 3 * D),
        columns(layer_full, 3 * D, D),
        enc_allowed,
        encoder_attn,
        grad_encoder_one,
    )
    pairs = enc_self_pairs + ((encoder_final, memory_low),) + enc_ffn_pairs
    return ((gain_zero, gain_one, gain_two), pairs, grad_encoder_input)


def apply_update(weight, moment, average, gradient, factor):
    clipped = gradient * factor
    moment_new = MOMENTUM * moment + clipped
    step_size = -LEARN_RATE * (clipped + MOMENTUM * moment_new)
    weight_new = weight + step_size
    return (
        weight_new,
        moment_new,
        AVERAGE_DECAY * average + (1.0 - AVERAGE_DECAY) * weight_new,
        step_size,
    )


def body(
    prompt_ids,
    prompt_lengths,
    response_ids,
    response_lengths,
    sequence_pair,
    chosen_flag,
    pair_microbatch,
    policy_embed,
    policy_layers,
    policy_gains,
    momentum_embed,
    momentum_layers,
    momentum_gains,
    average_embed,
    average_layers,
    average_gains,
    frozen_embed,
    frozen_layers,
    frozen_gains,
):
    n_dev = lax.axis_size(AXES)
    me = lax.axis_index(AXES)
    rows_here = policy_embed.shape[0]
    pairs_here = prompt_ids.shape[0]
    seat_count = response_ids.shape[0]
    decoder_input = jnp.concatenate(
        [jnp.zeros((seat_count, 1), jnp.int32), response_ids[:, :-1]], axis=1
    )
    pair_local = sequence_pair - me * pairs_here
    select_float = (pair_local[:, None] == jnp.arange(pairs_here)[None, :]).astype(jnp.float32)
    prompt_pos = jnp.arange(P_MAX)
    reply_pos = jnp.arange(R_MAX)
    prompt_keys = prompt_pos[None, :] < prompt_lengths[:, None]
    valid = reply_pos[None, :] < response_lengths[:, None]
    enc_allowed = jnp.broadcast_to(prompt_keys[:, None, :], (pairs_here, P_MAX, P_MAX))
    self_allowed = (reply_pos[:, None] >= reply_pos[None, :])[None] & valid[:, None, :]
    seat_keys = jnp.einsum("sp,pk->sk", select_float, prompt_keys.astype(jnp.float32)) > 0.5
    cross_allowed = jnp.broadcast_to(seat_keys[:, None, :], (seat_count, R_MAX, P_MAX))
    batch_data = (
        prompt_ids,
        decoder_input,
        response_ids,
        enc_allowed,
        self_allowed,
        cross_allowed,
        pair_local,
        valid,
    )
    token_ids = jnp.concatenate([prompt_ids.reshape(-1), decoder_input.reshape(-1)])
    token_live = jnp.concatenate([prompt_keys.reshape(-1), valid.reshape(-1)])
    plan = lookup_plan(token_ids, token_live, rows_here)
    packed = jnp.concatenate(
        [
            round_requests(plan, 0, n_dev),
            response_ids.reshape(-1),
            response_lengths,
            pair_local,
            chosen_flag,
            pair_microbatch,
            plan[5][None],
        ]
    )
    packed = jnp.pad(packed, (0, -packed.shape[0] % 1024)).reshape(8, -1)
    *policy_enc, notes = tree_gather(
        to_low(policy_layers), ENC_BLOCKS, D, 1, 115, extra=packed
    )
    notes = notes.reshape(n_dev, -1)
    asked = mine_of(notes)
    at = n_dev * SLOTS
    cuts = []
    for width in (seat_count * R_MAX, seat_count, seat_count, seat_count, pairs_here, 1):
        cuts.append(notes[:, at : at + width])
        at += width
    targets, all_lengths, all_pair, all_flag, all_micro, all_rounds = cuts
    targets = targets.reshape(-1)
    rounds = jnp.max(all_rounds)
    all_select = (all_pair[:, :, None] == jnp.arange(pairs_here)).astype(jnp.float32)
    pair_micro = (all_micro[:, :, None] == jnp.arange(MICRO)).astype(jnp.float32)
    seat_micro = jnp.sum(all_select[:, :, :, None] * pair_micro[:, None], axis=2)
    chosen_float = all_flag.astype(jnp.float32)
    pair_total = jnp.sum(pair_micro, axis=(0, 1))
    token_total = jnp.sum(
        seat_micro * (chosen_float * all_lengths.astype(jnp.float32))[:, :, None], axis=(0, 1)
    )
    micro_counts = jnp.stack([pair_total, token_total])
    pair_divisor = jnp.sum(pair_micro * pair_total, axis=2)
    sequence_divisor = jnp.sum(seat_micro * token_total, axis=2)
    all_valid = reply_pos < all_lengths[:, :, None]

    policy_table = to_low(policy_embed)
    policy_low = to_low(after(policy_layers, policy_enc[0]))
    policy_dec = gather_offloaded(policy_low, DEC_BLOCKS)
    answers = answer(asked, (policy_table, frozen_embed))
    policy_tokens, frozen_tokens = fetch_rows(plan, answers, rounds, (policy_table, frozen_embed), n_dev)
    policy_layer_enc = by_column(ENC_BLOCKS, policy_enc)
    policy_layer_dec = split_blocks(policy_dec, DEC_BLOCKS)
    policy_layer_full = policy_layer_enc | policy_layer_dec
    def policy_after(memory):
        return policy_layer_dec

    def logp_of(token_logp):
        return jnp.sum(jnp.where(all_valid, token_logp.reshape(all_valid.shape), 0.0), axis=2)

    policy_rows, stored = forward(
        policy_tokens, policy_layer_enc, policy_after, policy_gains, batch_data
    )
    frozen_enc = gather_offloaded(after(frozen_layers, stored[5]), ENC_BLOCKS)
    frozen_dec = gather_offloaded(after(frozen_layers, policy_rows), DEC_BLOCKS)
    frozen_layer_enc = split_blocks(frozen_enc, ENC_BLOCKS)

    def frozen_after(memory):
        return split_blocks(after(frozen_dec, memory), DEC_BLOCKS)

    token_logp, log_own, logits, hot, all_rows = shard_stats(
        policy_rows, policy_table, targets, (3, 4)
    )
    policy_logp = logp_of(token_logp)
    row_slope = jnp.where(
        all_valid.reshape(-1)[:, None], hot.astype(jnp.float32) - jnp.exp(logits - log_own[:, None]), 0.0
    )
    row_slope = with_layout_constraint(to_low(row_slope), Layout(major_to_minor=(0, 1)))
    grad_final = scatter_final(row_slope, policy_table, 10)
    dec_gains, dec_pairs, grad_memory, grad_zero = decoder_backward(
        policy_layer_full, policy_gains, batch_data, stored, grad_final
    )
    frozen_inputs = after(frozen_tokens, grad_zero)
    frozen_rows, unused = forward(
        frozen_inputs, frozen_layer_enc, frozen_after, frozen_gains, batch_data, True
    )
    frozen_logp = logp_of(shard_stats(frozen_rows, frozen_embed, targets, (5, 6))[0])
    frozen_mean = lax.dynamic_index_in_dim(
        frozen_logp / all_lengths.astype(jnp.float32), me, 0, keepdims=False
    )

    sign_value = 2.0 * chosen_float - 1.0
    margin = PREFERENCE_BETA * jnp.sum(
        all_select * (sign_value * (policy_logp - frozen_logp))[:, :, None], axis=1
    )
    loss = (
        jnp.sum(jax.nn.softplus(-margin) / pair_divisor)
        - CHOSEN_WEIGHT * jnp.sum(chosen_float * policy_logp / sequence_divisor)
    ) / MICRO
    pair_slope = -PREFERENCE_BETA * jax.nn.sigmoid(-margin) / pair_divisor
    sequence_slope = (
        sign_value * jnp.sum(all_select * pair_slope[:, None, :], axis=2)
        - CHOSEN_WEIGHT * chosen_float / sequence_divisor
    ) / MICRO
    slope_here = lax.dynamic_index_in_dim(sequence_slope, me, 0, keepdims=False)
    slope_rows = jnp.repeat(slope_here, R_MAX)[:, None]
    memory_slope = (select_float * slope_here[:, None])[:, :, None, None, None]
    memory_low = jnp.concatenate(
        [
            join_heads(to_low(jnp.sum(memory_slope * part[:, None], axis=0))).reshape(-1, D)
            for part in grad_memory
        ],
        axis=1,
    )
    enc_gains, enc_pairs, grad_encoder_input = encoder_backward(
        policy_layer_full, policy_gains, batch_data, stored, memory_low
    )
    gain_grads = jnp.stack(
        [jnp.sum(rows, axis=0) for rows in enc_gains]
        + [jnp.sum(slope_rows * rows, axis=0) for rows in dec_gains]
    )
    token_gradient = jnp.concatenate([grad_encoder_input, slope_rows * grad_zero], axis=0)
    enc_pairs = [(to_low(left), to_low(right)) for left, right in enc_pairs]
    scaled_pairs = []
    for left, right in dec_pairs:
        if left.dtype == jnp.float32:
            scaled_pairs.append((to_low(slope_rows * left), right))
        else:
            scaled_pairs.append((left, to_low(slope_rows * right)))
    token_gradient = to_low(token_gradient)
    first_sums = row_sums(picking(plan, 0, n_dev), token_gradient)
    late_slope = after(sequence_slope, first_sums)
    table_grad = jnp.einsum(
        "rc,rd->cd",
        row_slope,
        to_low(jnp.repeat(late_slope.reshape(-1), R_MAX)[:, None] * all_rows),
        preferred_element_type=jnp.float32,
    )
    table_grad = after(table_grad, first_sums)
    enc_pairs[0] = (after(enc_pairs[0][0], first_sums, table_grad), enc_pairs[0][1])
    embed_grad = return_rows(plan, asked, rounds, first_sums, token_gradient, table_grad, n_dev)
    layer_grad = scatter_layers(scaled_pairs, enc_pairs, policy_layers.shape[0], 8)
    squares_local = jnp.sum(embed_grad * embed_grad) + jnp.sum(layer_grad * layer_grad)
    shared = total_of(jnp.concatenate([gain_grads, jnp.full((1, D), squares_local)], axis=0), 9)
    gain_total, squares_total = (shared[:7], shared[7, 0])
    grad_norm = jnp.sqrt(squares_total + jnp.sum(gain_total * gain_total))
    factor = jnp.minimum(1.0, CLIP_NORM / grad_norm)
    embed_new = apply_update(policy_embed, momentum_embed, average_embed, embed_grad, factor)
    layers_new = apply_update(policy_layers, momentum_layers, average_layers, layer_grad, factor)
    gains_new = apply_update(policy_gains, momentum_gains, average_gains, gain_total, factor)
    return (
        loss,
        grad_norm,
        micro_counts,
        frozen_mean,
        embed_new[3],
        layers_new[0],
        gains_new[0],
        embed_new[1],
        layers_new[1],
        gains_new[1],
        embed_new[2],
        layers_new[2],
        gains_new[2],
    )


def solution(mesh):
    placed = (
        P(("dp", "fsdp"), None),
        P(("dp", "fsdp")),
        P(("dp", "fsdp"), None),
        P(("dp", "fsdp")),
        P(("dp", "fsdp")),
        P(("dp", "fsdp")),
        P(("dp", "fsdp")),
        P(("dp", "fsdp"), None),
        P(("dp", "fsdp"), None),
        P(),
        P(("dp", "fsdp"), None),
        P(("dp", "fsdp"), None),
        P(),
        P(("dp", "fsdp"), None),
        P(("dp", "fsdp"), None),
        P(),
        P(("dp", "fsdp"), None),
        P(("dp", "fsdp"), None),
        P(),
    )
    return jax.shard_map(
        body,
        mesh=mesh,
        in_specs=placed,
        out_specs=(
            P(),
            P(),
            P(),
            P(("dp", "fsdp")),
            P(("dp", "fsdp"), None),
            P(("dp", "fsdp"), None),
            P(),
            P(("dp", "fsdp"), None),
            P(("dp", "fsdp"), None),
            P(),
            P(("dp", "fsdp"), None),
            P(("dp", "fsdp"), None),
            P(),
        ),
        check_vma=False,
    )
```

```python
import functools

import jax
import jax.numpy as jnp
from jax import lax
from jax.experimental import pallas as pl
from jax.experimental.layout import Layout, with_layout_constraint
from jax.experimental.pallas import tpu as pltpu
from jax.sharding import PartitionSpec as P

D = 1024
HEADS = 16
HEAD = 64
FF = 4096
P_MAX = 192
R_MAX = 32
MICRO = 2


EPSILON = 1e-06
SCORE_SCALE = 0.125
PREFERENCE_BETA = 0.1
CHOSEN_WEIGHT = 1.0
MOMENTUM = 0.9
LEARN_RATE = 2000.0
AVERAGE_DECAY = 0.5
CLIP_NORM = 0.04
MASK_FILL = -1000000000.0
HIGHEST = lax.Precision.HIGHEST


def rms_norm(values, gain_row):
    return (
        values * lax.rsqrt(jnp.mean(values * values, axis=-1, keepdims=True) + EPSILON) * gain_row
    )


def final_norm(values, gain_row):
    return rms_norm(values, gain_row) * D ** (-0.5)


def to_low(values):
    return values.astype(jnp.bfloat16)


def matmul(left_side, right_side):
    return jnp.dot(left_side, right_side, preferred_element_type=jnp.float32)


def matmul_back(grad_low, weight):
    return jnp.einsum("re,de->rd", grad_low, weight, preferred_element_type=jnp.float32)


def split_heads(values):
    return values.reshape(values.shape[0], values.shape[1], HEADS, HEAD)


def scores_of(queries, key_rows, allowed):
    raw_scores = (
        jnp.einsum(
            "bqhe,bkhe->bhqk",
            split_heads(queries),
            split_heads(key_rows),
            preferred_element_type=jnp.float32,
        )
        * SCORE_SCALE
    )
    return jnp.where(allowed[:, None], raw_scores, MASK_FILL)


def attend_forward(queries, key_rows, values, allowed):
    scores = scores_of(queries, key_rows, allowed)
    log_total = jax.nn.logsumexp(scores, axis=-1, keepdims=True)
    softmax_out = to_low(jnp.exp(scores - log_total))
    mixed_out = jnp.einsum(
        "bhqk,bkhe->bqhe", softmax_out, split_heads(values), preferred_element_type=jnp.float32
    )
    return (to_low(mixed_out.reshape(queries.shape)), log_total)


def attend_backward(queries, key_rows, values, allowed, log_total, grad_mixed):
    softmax_out = jnp.exp(scores_of(queries, key_rows, allowed) - log_total)
    grad_heads = split_heads(to_low(grad_mixed))
    grad_values = jnp.einsum(
        "bhqk,bqhe->bhke", to_low(softmax_out), grad_heads, preferred_element_type=jnp.float32
    )
    grad_probs = jnp.einsum(
        "bqhe,bkhe->bhqk", grad_heads, split_heads(values), preferred_element_type=jnp.float32
    )
    grad_scores = to_low(
        softmax_out * (grad_probs - jnp.sum(grad_probs * softmax_out, axis=-1, keepdims=True))
    )
    grad_query = (
        jnp.einsum(
            "bhqk,bkhe->bqhe",
            grad_scores,
            split_heads(key_rows),
            preferred_element_type=jnp.float32,
        )
        * SCORE_SCALE
    )
    grad_keys = (
        jnp.einsum(
            "bhqk,bqhe->bhke", grad_scores, split_heads(queries), preferred_element_type=jnp.float32
        )
        * SCORE_SCALE
    )
    return (grad_query.reshape(queries.shape), grad_keys, grad_values)


def join_heads(values):
    return values.transpose(0, 2, 1, 3).reshape(values.shape[0], values.shape[2], D)


def self_forward(residual, gain_row, weight_three, weight_out, allowed, shape_pair):
    normed = to_low(rms_norm(residual, gain_row))
    triple = to_low(matmul(normed, weight_three)).reshape(shape_pair[0], shape_pair[1], 3 * D)
    mixed_out, log_total = attend_forward(
        triple[..., :D], triple[..., D : 2 * D], triple[..., 2 * D :], allowed
    )
    flat_mixed = mixed_out.reshape(-1, D)
    return (residual + matmul(flat_mixed, weight_out), (normed, triple, log_total, flat_mixed))


def norm_backward(norm, residual, gain_row, grad_normed):
    grad_residual = jax.vjp(lambda values: norm(values, gain_row), residual)[1](grad_normed)[0]
    return grad_residual, grad_normed * norm(residual, jnp.ones_like(gain_row))


def self_backward(residual, gain_row, weight_three, weight_out, allowed, stored, grad_out):
    normed, triple, log_total, flat_mixed = stored
    grad_mixed = matmul_back(to_low(grad_out), weight_out)
    queries = triple[..., :D]
    grad_query, grad_keys, grad_values = attend_backward(
        queries,
        triple[..., D : 2 * D],
        triple[..., 2 * D :],
        allowed,
        log_total,
        grad_mixed.reshape(queries.shape),
    )
    grads = (grad_query, join_heads(grad_keys), join_heads(grad_values))
    grad_triple = jnp.concatenate(grads, axis=-1).reshape(-1, 3 * D)
    grad_normed = matmul_back(to_low(grad_triple), weight_three)
    grad_residual, gain_rows = norm_backward(rms_norm, residual, gain_row, grad_normed)
    return (grad_out + grad_residual, gain_rows, ((normed, grad_triple), (flat_mixed, grad_out)))


def cross_forward(
    residual, gain_row, weight_query, weight_out, cross_memory, pair_local, allowed, shape_pair
):
    normed = to_low(rms_norm(residual, gain_row))
    queries = to_low(matmul(normed, weight_query)).reshape(shape_pair[0], shape_pair[1], D)
    seat_memory = jnp.broadcast_to(cross_memory[:1], (shape_pair[0],) + cross_memory.shape[1:])
    for pair in range(1, cross_memory.shape[0]):
        seat_memory = jnp.where(
            pair_local[:, None, None] == pair, cross_memory[pair][None], seat_memory
        )
    mixed_out, log_total = attend_forward(
        queries, seat_memory[..., :D], seat_memory[..., D:], allowed
    )
    flat_mixed = mixed_out.reshape(-1, D)
    return (
        residual + matmul(flat_mixed, weight_out),
        (normed, queries, seat_memory, log_total, flat_mixed),
    )


def cross_backward(residual, gain_row, weight_query, weight_out, allowed, stored, grad_out):
    normed, queries, seat_memory, log_total, flat_mixed = stored
    grad_mixed = matmul_back(to_low(grad_out), weight_out)
    grad_query, grad_keys, grad_values = attend_backward(
        queries,
        seat_memory[..., :D],
        seat_memory[..., D:],
        allowed,
        log_total,
        grad_mixed.reshape(queries.shape),
    )
    grad_query = grad_query.reshape(-1, D)
    grad_normed = matmul_back(to_low(grad_query), weight_query)
    grad_residual, gain_rows = norm_backward(rms_norm, residual, gain_row, grad_normed)
    return (
        grad_out + grad_residual,
        gain_rows,
        (grad_keys, grad_values),
        ((normed, grad_query), (flat_mixed, grad_out)),
    )


def feed_forward(residual, gain_row, weight_in, weight_out):
    normed = to_low(rms_norm(residual, gain_row))
    before = matmul(normed, weight_in)
    active = to_low(jax.nn.relu(before))
    return (
        residual + jnp.einsum("rf,df->rd", active, weight_out, preferred_element_type=jnp.float32),
        (normed, active),
    )


def feed_backward(residual, gain_row, weight_in, weight_out, stored, grad_out):
    normed, active = stored
    grad_active = matmul(to_low(grad_out), weight_out)
    grad_before = jnp.where(active > 0, grad_active, 0.0)
    grad_normed = matmul_back(to_low(grad_before), weight_in)
    grad_residual, gain_rows = norm_backward(rms_norm, residual, gain_row, grad_normed)
    return (grad_out + grad_residual, gain_rows, ((normed, grad_before), (grad_out, active)))


AXES = ("dp", "fsdp")


FF_STEP = 512


def norm_scale(values):
    return lax.rsqrt(jnp.mean(values * values, axis=-1, keepdims=True) + EPSILON)


def feed_kernel(residual_ref, gain_ref, in_ref, out_ref, result_ref, normed_ref):
    @pl.when(pl.program_id(0) == 0)
    def _():
        residual = residual_ref[...]
        normed_ref[...] = to_low(residual * norm_scale(residual) * gain_ref[...])
        result_ref[...] = residual

    before = jnp.dot(normed_ref[...], in_ref[...], preferred_element_type=jnp.float32)
    active = to_low(jax.nn.relu(before))
    result_ref[...] += lax.dot_general(
        active, out_ref[...], (((1,), (1,)), ((), ())), preferred_element_type=jnp.float32
    )


def weight_spec(start):
    return pl.BlockSpec((D, FF_STEP), lambda step: (0, step + start // FF_STEP))


def whole_spec(shape):
    return pl.BlockSpec(shape, lambda step: (0,) * len(shape))


def feed_cost(rows):
    return pl.CostEstimate(flops=4 * rows * D * FF, bytes_accessed=4 * D * FF, transcendentals=0)


def feed_streamed(residual, gain_row, weight_in, weight_out):
    rows = residual.shape[0]
    (source_in, start_in), (source_out, start_out) = (weight_in, weight_out)
    result = pl.pallas_call(
        feed_kernel,
        grid=(FF // FF_STEP,),
        out_shape=jax.ShapeDtypeStruct((rows, D), jnp.float32),
        in_specs=[
            whole_spec((rows, D)),
            whole_spec((1, D)),
            weight_spec(start_in),
            weight_spec(start_out),
        ],
        out_specs=whole_spec((rows, D)),
        scratch_shapes=[pltpu.VMEM((rows, D), jnp.bfloat16)],
        compiler_params=pltpu.CompilerParams(vmem_limit_bytes=40 * 2**20),
        cost_estimate=feed_cost(rows),
    )(residual, gain_row[None], source_in, source_out)
    return (result, None)


SLOTS = 24
MESH = pl.DeviceIdType.MESH


def device_bits():
    bits = []
    for axis in AXES:
        mask = lax.axis_size(axis) // 2
        while mask:
            bits.append((axis, mask))
            mask //= 2
    return bits


def scatter_orders():
    core, across = (("dp", 1), ("dp", 2))
    inner = [bit for bit in reversed(device_bits()) if bit[0] == "fsdp"]
    first, rest = inner[:1], inner[1:]
    return (
        [core, across] + rest + first,
        [core] + inner + [across],
        [core, across] + first + rest,
        [core] + first + [across] + rest,
    )


def lane_widths(width):
    if width % D == 0:
        return (3 * width // 8, 3 * width // 8, width // 8, width // 8)
    return (width // 4,) * 4 if width % 512 == 0 else (width,)


def bit_of(bit):
    axis, mask = bit
    return (lax.axis_index(axis) // mask) % 2


def partner(bit):
    axis, mask = bit
    return {axis: lax.axis_index(axis) + mask * (1 - 2 * bit_of(bit))}


def greet(bits):
    barrier = pltpu.get_barrier_semaphore()
    for bit in bits:
        pl.semaphore_signal(barrier, inc=1, device_id=partner(bit), device_id_type=MESH)
    pl.semaphore_wait(barrier, len(bits))


def gather_kernel(bits, n_in, waves, *refs):
    ins, outs, (own_sem, send_sem, recv_sem) = (refs[:n_in], refs[n_in:-3], refs[-3:])
    mine = {bit: bit_of(bit) for bit in bits}
    depth = len(bits)
    greet(bits)
    index, sent, kept = ({}, {}, {})
    for turn in range(len(waves) + depth):
        for step in range(depth + 1):
            wave = turn - step
            if not 0 <= wave < len(waves):
                continue
            for lane, (number, which, start, low, width, first, count, order) in enumerate(
                waves[wave]
            ):
                slot = index.setdefault((wave, lane), len(index))
                lead = tuple(
                    pl.ds(0, 2) if bit in order[:step] else pl.ds(mine[bit], 1) for bit in bits
                )
                place = outs[which].at[lead + (pl.ds(first, count), pl.ds(low, width))]
                source = place
                if step == 0:
                    whole = (slice(None),) * depth
                    source = ins[number].at[whole + (pl.ds(first, count), pl.ds(start, width))]
                    kept[slot] = pltpu.make_async_copy(source, place, own_sem.at[slot])
                    kept[slot].start()
                else:
                    sent[slot, step - 1].wait_recv()
                if step == 1:
                    kept[slot].wait()
                if step < depth:
                    sent[slot, step] = pltpu.make_async_remote_copy(
                        src_ref=source,
                        dst_ref=place,
                        send_sem=send_sem.at[slot, step],
                        recv_sem=recv_sem.at[slot, step],
                        device_id=partner(order[step]),
                        device_id_type=MESH,
                    )
                    sent[slot, step].start()
    for copy in sent.values():
        copy.wait_send()


def busy_for(micros):
    return pl.CostEstimate(flops=0, bytes_accessed=int(micros * 3.4e6), transcendentals=0)


def tree_gather(shard, blocks, step, collective_id, micros, row_step=None, extra=None):
    bits = device_bits()
    rows = shard.shape[0]
    row_step = row_step or rows
    waves = []
    for which, (start, width) in enumerate(blocks):
        for low in range(0, width, step):
            for first in range(0, rows, row_step):
                wave, at = ([], low)
                for lane, order in zip(lane_widths(step), scatter_orders()):
                    piece = (0, which, start + at, at, lane, first, row_step)
                    wave.append(piece + (tuple(reversed(order)),))
                    at += lane
                waves.append(wave)
    operands = [shard]
    shapes = [((rows, width), shard.dtype) for _, width in blocks]
    if extra is not None:
        operands.append(extra)
        shapes.append((extra.shape, extra.dtype))
        piece = (1, len(blocks), 0, 0, extra.shape[1], 0, extra.shape[0])
        waves[0].append(piece + (tuple(reversed(scatter_orders()[0])),))
    total = sum(len(wave) for wave in waves)
    gathered = pl.pallas_call(
        functools.partial(gather_kernel, bits, len(operands), waves),
        out_shape=[
            jax.ShapeDtypeStruct((2,) * len(bits) + shape, dtype) for shape, dtype in shapes
        ],
        in_specs=[pl.BlockSpec(memory_space=pl.ANY)] * len(operands),
        out_specs=[pl.BlockSpec(memory_space=pl.ANY)] * len(shapes),
        scratch_shapes=[
            pltpu.SemaphoreType.DMA((total,)),
            pltpu.SemaphoreType.DMA((total, len(bits))),
            pltpu.SemaphoreType.DMA((total, len(bits))),
        ],
        compiler_params=pltpu.CompilerParams(collective_id=collective_id, has_side_effects=True),
        cost_estimate=busy_for(micros),
    )(*[value.reshape((1,) * len(bits) + value.shape) for value in operands])
    return [value.reshape((-1, shape[1])) for value, (shape, _) in zip(gathered, shapes)]


def gather_whole(values, step, collective_id, micros, row_step=None):
    blocks = [(0, values.shape[1])]
    full = tree_gather(values, blocks, step, collective_id, micros, row_step)[0]
    return full.reshape((-1,) + values.shape)


def total_kernel(sizes, x_ref, sum_ref, *scratch):
    held, send_sem, recv_sem = (scratch[:2], scratch[2:4], scratch[4:6])
    barrier = pltpu.get_barrier_semaphore()
    peers = [(axis, hop) for axis, size in sizes for hop in range(1, size)]

    def peer(axis, size, hop):
        return {axis: lax.rem(lax.axis_index(axis) + hop, size)}

    for axis, hop in peers:
        pl.semaphore_signal(
            barrier, inc=1, device_id=peer(axis, dict(sizes)[axis], hop), device_id_type=MESH
        )
    pl.semaphore_wait(barrier, len(peers))
    value = x_ref[...]
    for turn, (axis, size) in enumerate(sizes):
        me = lax.axis_index(axis)
        held[turn][me] = value
        copies = []
        for hop in range(1, size):
            copies.append(
                pltpu.make_async_remote_copy(
                    src_ref=held[turn].at[me],
                    dst_ref=held[turn].at[me],
                    send_sem=send_sem[turn].at[hop],
                    recv_sem=recv_sem[turn].at[hop],
                    device_id=peer(axis, size, hop),
                    device_id_type=MESH,
                )
            )
            copies[-1].start()
        for hop, copy in enumerate(copies, 1):
            other = lax.rem(me + size - hop, size)
            pltpu.make_async_remote_copy(
                src_ref=held[turn].at[other],
                dst_ref=held[turn].at[other],
                send_sem=send_sem[turn].at[hop],
                recv_sem=recv_sem[turn].at[hop],
                device_id=peer(axis, size, hop),
                device_id_type=MESH,
            ).wait_recv()
        value = held[turn][0]
        for other in range(1, size):
            value = value + held[turn][other]
        for copy in copies:
            copy.wait_send()
    sum_ref[...] = value


def total_of(tile, collective_id):
    sizes = [(axis, lax.axis_size(axis)) for axis in reversed(AXES)]
    in_vmem = pl.BlockSpec(memory_space=pltpu.VMEM)
    marks = [pltpu.SemaphoreType.DMA((size,)) for _, size in sizes]
    return pl.pallas_call(
        functools.partial(total_kernel, sizes),
        out_shape=jax.ShapeDtypeStruct(tile.shape, jnp.float32),
        in_specs=[in_vmem],
        out_specs=in_vmem,
        scratch_shapes=[pltpu.VMEM((size,) + tile.shape, jnp.float32) for _, size in sizes]
        + marks
        + marks,
        compiler_params=pltpu.CompilerParams(collective_id=collective_id, has_side_effects=True),
        cost_estimate=busy_for(12),
    )(tile)


CORE_SLOTS = 2


def scatter_kernel(bits, plan, *refs):
    n_waves, slots, wide, widths = (plan["waves"], plan["slots"], plan["wide"], plan["widths"])
    n_ins, n_loaded = (plan["operands"], len(plan["loads"]))
    ins, out_ref, squares_ref = (refs[:n_ins], refs[n_ins], refs[n_ins + 1])
    loaded, rest_refs = (refs[n_ins + 2 : n_ins + 2 + n_loaded], refs[n_ins + 2 + n_loaded :])
    buffers = [rest_refs[6 * lane : 6 * lane + 6] for lane in range(len(widths))]
    load_sem, send_sem, recv_sem, free_sem = rest_refs[6 * len(widths) :]
    depth = len(bits)
    mine = {bit: bit_of(bit) for bit in bits}
    core = scatter_orders()[0][0]
    rest = [bit for bit in bits if bit != core]

    def half(order, step, kept):
        bit_at = {bit: pl.ds(mine[bit], 1) for bit in order[1:step]}
        last = mine[order[step]] if kept else 1 - mine[order[step]]
        bit_at[order[step]] = pl.ds(last, 1)
        return tuple(bit_at.get(bit, pl.ds(0, 2)) for bit in rest)

    def span_of(step):
        return CORE_SLOTS if step == 0 else slots

    def copy(wave, lane, step, order):
        send_core, from_core, total, narrow, arrived, arrived_wide = buffers[lane]
        slot = lax.rem(wave, span_of(step))
        if step == 0:
            source, target = (send_core.at[slot], from_core.at[slot])
        else:
            source = (total if step in wide else narrow).at[(slot,) + half(order, step, False)]
            target = arrived_wide if step in wide else arrived
            target = target.at[(slot,) + half(order, step, True)]
        return pltpu.make_async_remote_copy(
            src_ref=source,
            dst_ref=target,
            send_sem=send_sem.at[lane, slot, step],
            recv_sem=recv_sem.at[lane, slot, step],
            device_id=partner(order[step]),
            device_id_type=MESH,
        )

    def kept_entries(order, step):
        left = [bit for bit in rest if bit not in order[: step + 1]]
        for number in range(2 ** len(left)):
            chosen = {bit: (number >> place) % 2 for place, bit in enumerate(reversed(left))}
            here = tuple(chosen.get(bit, mine[bit]) for bit in rest)
            came = tuple(1 - mine[bit] if bit == order[step] else at for bit, at in zip(rest, here))
            yield here, came

    def visit(wave, lane, step, order):
        send_core, from_core, total, narrow, arrived, arrived_wide = buffers[lane]
        low, width = (sum(widths[:lane]), widths[lane])
        slot = lax.rem(wave, span_of(step))
        reuse = wave >= span_of(step)

        def keep(at, value, next_step):
            total[(slot,) + at] = value
            if next_step not in wide:
                narrow[(slot,) + at] = value.astype(jnp.bfloat16)

        if step == 0:

            @pl.when(reuse)
            def _():
                copy(wave, lane, 0, order).wait_send()

            def put(at, value):
                send_core[(slot,) + at] = value

            plan["produce"](loaded, wave, low, width, 1 - mine[core], put)
        else:
            copy(wave, lane, step - 1, order).wait_recv()
            if step == 1:
                core_slot = lax.rem(wave, CORE_SLOTS)

                @pl.when(reuse)
                def _():
                    for old in range(1, depth):
                        copy(wave, lane, old, order).wait_send()

                def add(at, value):
                    keep(at, value + from_core[(core_slot,) + at], 1)

                plan["produce"](loaded, wave, low, width, mine[core], add)
            else:
                source = arrived_wide if step - 1 in wide else arrived
                for here, came in kept_entries(order, step - 1):
                    value = total[(slot,) + here] + source[(slot,) + came].astype(jnp.float32)
                    if step == depth:
                        start = plan["column"](wave) + low
                        out_ref[:, pl.ds(pl.multiple_of(start, 128), width)] = value
                        squares = value * value
                        squares_ref[...] += sum(
                            squares[:, at : at + 128] for at in range(0, width, 128)
                        )
                    else:
                        keep(here, value, step)

            @pl.when(wave + span_of(step - 1) < n_waves)
            def _():
                pl.semaphore_signal(
                    free_sem.at[lane, lax.rem(wave, span_of(step - 1)), step - 1],
                    inc=1,
                    device_id=partner(order[step - 1]),
                    device_id_type=MESH,
                )

        if step < depth:

            @pl.when(reuse)
            def _():
                pl.semaphore_wait(free_sem.at[lane, slot, step], 1)

            copy(wave, lane, step, order).start()

    loads = []
    for number, (_, parts) in enumerate(plan["loads"]):
        for operand, place in parts:
            at = loaded[number].at[place] if place else loaded[number]
            loads.append(pltpu.make_async_copy(ins[operand], at, load_sem.at[operand]))
            loads[-1].start()

    def turn_of(turn, carry):
        for step in range(depth + 1):
            wave = turn - step

            @pl.when((wave >= 0) & (wave < n_waves))
            def _():
                if step == 0:
                    for late, count in plan["waits"]:

                        @pl.when(wave == late)
                        def _():
                            for load in loads[slice(*count)]:
                                load.wait()

                for lane, order in enumerate(plan["orders"]):
                    visit(wave, lane, step, order)

        return carry

    squares_ref[...] = jnp.zeros_like(squares_ref)
    greet(bits)
    lax.fori_loop(0, n_waves + depth, turn_of, 0)
    for step in range(depth):
        for wave in range(max(0, n_waves - span_of(step)), n_waves):
            for lane, order in enumerate(plan["orders"]):
                copy(wave, lane, step, order).wait_send()


def tree_scatter(operands, plan, collective_id, micros):
    bits = device_bits()
    slots, widths, rows = (plan["slots"], plan["widths"], plan["rows"])
    plan = dict(plan, operands=len(operands))
    scratch = [pltpu.VMEM(shape, jnp.bfloat16) for shape, _ in plan["loads"]]
    for width in widths:
        entries = (2,) * (len(bits) - 1) + (rows, width)
        core_buffer = pltpu.VMEM((CORE_SLOTS,) + entries, jnp.float32)
        low_buffer = pltpu.VMEM((slots,) + entries, jnp.bfloat16)
        sums = pltpu.VMEM((slots,) + entries, jnp.float32)
        wide_buffer = sums if plan["wide"] else pltpu.VMEM((8, 128), jnp.float32)
        scratch += [core_buffer, core_buffer, sums, low_buffer, low_buffer, wide_buffer]
    marks = (len(widths), slots, len(bits))
    return pl.pallas_call(
        functools.partial(scatter_kernel, bits, plan),
        out_shape=[
            jax.ShapeDtypeStruct((rows, plan["waves"] * sum(widths)), jnp.float32),
            jax.ShapeDtypeStruct((rows, 128), jnp.float32),
        ],
        in_specs=[pl.BlockSpec(memory_space=pl.ANY)] * len(operands),
        out_specs=[pl.BlockSpec(memory_space=pltpu.VMEM)] * 2,
        scratch_shapes=scratch
        + [
            pltpu.SemaphoreType.DMA((len(operands),)),
            pltpu.SemaphoreType.DMA(marks),
            pltpu.SemaphoreType.DMA(marks),
            pltpu.SemaphoreType.REGULAR(marks),
        ],
        compiler_params=pltpu.CompilerParams(
            collective_id=collective_id, has_side_effects=True, vmem_limit_bytes=60 * 2**20
        ),
        cost_estimate=busy_for(micros),
    )(*operands)


def unit_of(block, blocks):
    edges, most = ([], sum(blocks))
    for count in blocks[:-1]:
        edges.append(count + (edges[-1] if edges else 0))
    return sum(lax.div(block + (most - edge), most) for edge in edges)


def put_rows(value, across, rows, put):
    rest_count = (value.shape[0] // rows).bit_length() - 1
    for number in range(2**rest_count):
        at = tuple((number >> place) % 2 for place in reversed(range(rest_count)))
        put((across,) + at, value[number * rows : (number + 1) * rows])


def layer_products(dec_blocks, enc_blocks, rows, loaded, wave, low, width, core, put):
    dec_left, dec_right, enc_left, enc_right = loaded
    dec_waves = sum(dec_blocks)
    quarter = D // 4

    def product(left, right, blocks, block):
        unit = unit_of(block, blocks)
        sides = right[:, pl.ds(pl.multiple_of(block * D + low, 128), width)]
        for across in range(2):
            some = pl.ds(pl.multiple_of((2 * across + core) * quarter, quarter), quarter)
            value = lax.dot_general(
                left[unit, :, some],
                sides,
                (((0,), (0,)), ((), ())),
                preferred_element_type=jnp.float32,
            )
            put_rows(value, across, rows, put)

    @pl.when(wave < dec_waves)
    def _():
        product(dec_left, dec_right, dec_blocks, wave)

    @pl.when(wave >= dec_waves)
    def _():
        product(enc_left, enc_right, enc_blocks, wave - dec_waves)


def layer_column(wave):
    is_enc = lax.div(wave, 14)
    block = wave - is_enc * 14

    def past(edge):
        return lax.div(block + 14 - edge, 14)

    dec_shift = 4 + 2 * past(5) + 8 * past(6)
    enc_shift = 5 * past(4) + past(6)
    shift = dec_shift + is_enc * (enc_shift - dec_shift)
    return (block + shift) * D


def scatter_layers(dec_pairs, enc_pairs, rows, collective_id):
    operands, loads, counts = ([], [], [])
    for pairs in (dec_pairs, enc_pairs):
        tokens, parts, at = (pairs[0][0].shape[0], [], 0)
        for unit, (left_side, _) in enumerate(pairs):
            parts.append((len(operands), (unit,)))
            operands.append(left_side)
        loads.append(((len(pairs), tokens, D), parts))
        parts = []
        for _, right_side in pairs:
            parts.append((len(operands), (slice(None), pl.ds(at, right_side.shape[1]))))
            operands.append(right_side)
            at += right_side.shape[1]
        loads.append(((tokens, at), parts))
        counts.append([right_side.shape[1] // D for _, right_side in pairs])
    dec_loads = 2 * len(dec_pairs)
    plan = {
        "waves": sum(counts[0]) + sum(counts[1]),
        "slots": 6,
        "widths": lane_widths(D),
        "orders": scatter_orders(),
        "rows": rows,
        "wide": (),
        "loads": loads,
        "waits": ((0, (0, dec_loads)), (sum(counts[0]), (dec_loads, None))),
        "produce": functools.partial(layer_products, counts[0], counts[1], rows),
        "column": layer_column,
    }
    return tree_scatter(operands, plan, collective_id, 210)


def final_products(step, rows, loaded, wave, low, width, core, put):
    left, right = loaded
    sides = right[:, pl.ds(pl.multiple_of(wave * step + low, 128), width)]
    for across in range(2):
        value = jnp.dot(left[across, core], sides, preferred_element_type=jnp.float32)
        put_rows(value, across, rows, put)


def scatter_final(grad_logits, table, collective_id):
    bits = device_bits()
    n_dev, step, width = (2 ** len(bits), 256, table.shape[1])
    rows_all = grad_logits.shape[0] // n_dev
    turns = max(1, n_dev // 32)
    rows = rows_all // turns
    sums = []
    for turn in range(turns):
        some = grad_logits.reshape(n_dev, rows_all, -1)[:, turn * rows : (turn + 1) * rows]
        some = some.reshape(2, 2, n_dev // 4 * rows, -1)
        plan = {
            "waves": width // step,
            "slots": width // step,
            "widths": (step // 2, step // 2),
            "orders": scatter_orders()[:2],
            "rows": rows,
            "wide": (len(bits) - 2, len(bits) - 1),
            "loads": [(some.shape, [(0, ())]), (table.shape, [(1, ())])],
            "waits": ((0, (0, 2)),),
            "produce": functools.partial(final_products, step, rows),
            "column": lambda wave: wave * step,
        }
        sums.append(tree_scatter([some, table], plan, collective_id + turn, 60)[0])
    return jnp.concatenate(sums, axis=0)


def lookup_plan(ids, live, rows_here):
    count = ids.shape[0]
    owner = ids // rows_here
    same = (ids[:, None] == ids[None, :]) & live[None, :]
    earlier = jnp.arange(count)[None, :] < jnp.arange(count)[:, None]
    first = live & ~jnp.any(same & earlier, axis=1)
    below = first[None, :] & (owner[:, None] == owner[None, :]) & (ids[None, :] < ids[:, None])
    rank = jnp.sum(below.astype(jnp.int32), axis=1)
    rounds = jnp.max(jnp.where(live, rank, 0)) // SLOTS + 1
    return (owner, ids - owner * rows_here, first, live, rank, rounds)


def round_flat(plan, turn):
    owner, _, _, live, rank, _ = plan
    slot = rank - turn * SLOTS
    return jnp.where(live & (slot >= 0) & (slot < SLOTS), owner * SLOTS + slot, -1)


def round_requests(plan, turn, n_dev):
    flat = round_flat(plan, turn)
    hit = (flat[:, None] == jnp.arange(n_dev * SLOTS)[None, :]) & plan[2][:, None]
    return jnp.sum(jnp.where(hit, plan[1][:, None] + 1, 0), axis=0) - 1


def picking(plan, turn, n_dev):
    return (
        round_flat(plan, turn)[:, None] == jnp.arange(n_dev * SLOTS)[None, :]
    ).astype(jnp.bfloat16)


def asked_hot(asked, rows_here):
    return (asked.reshape(-1)[:, None] == jnp.arange(rows_here)[None, :]).astype(jnp.bfloat16)


def mine_of(table):
    return lax.dynamic_slice_in_dim(table, lax.axis_index(AXES) * SLOTS, SLOTS, axis=1)


def swap(rows, n_dev):
    wide = rows.shape[-1]
    return lax.all_to_all(
        rows.reshape(n_dev, SLOTS, wide), AXES, 0, 0, tiled=True
    ).reshape(n_dev * SLOTS, wide)


def answer(asked, tables):
    hot = asked_hot(asked, tables[0].shape[0])
    return jnp.concatenate([to_low(matmul(hot, table)) for table in tables], axis=1)


def pick_rows(pick, rows):
    return (to_low(matmul(pick, rows[:, :D])), to_low(matmul(pick, rows[:, D:])))


def added(some, others):
    return jax.tree.map(jnp.add, some, others)


def fetch_rows(plan, answers, rounds, tables, n_dev):
    rows = pick_rows(picking(plan, 0, n_dev), swap(answers, n_dev))

    def more(state):
        turn, rows = state
        asked = mine_of(lax.all_gather(round_requests(plan, turn, n_dev), AXES, axis=0))
        pick = picking(plan, turn, n_dev)
        return (turn + 1, added(rows, pick_rows(pick, swap(answer(asked, tables), n_dev))))

    return lax.while_loop(lambda state: state[0] < rounds, more, (jnp.int32(1), rows))[1]


def collect(asked, sums, rows_here, n_dev):
    return jnp.einsum(
        "kc,kd->cd",
        asked_hot(asked, rows_here),
        swap(sums, n_dev),
        preferred_element_type=jnp.float32,
    )


def row_sums(pick, gradient):
    return to_low(jnp.einsum("nk,nd->kd", pick, gradient, preferred_element_type=jnp.float32))


def return_rows(plan, asked, rounds, first_sums, gradient, table_grad, n_dev):
    rows_here = table_grad.shape[0]

    def more(state):
        turn, sums = state
        asked = mine_of(lax.all_gather(round_requests(plan, turn, n_dev), AXES, axis=0))
        pick = picking(plan, turn, n_dev)
        return (turn + 1, sums + collect(asked, row_sums(pick, gradient), rows_here, n_dev))

    sums = lax.while_loop(lambda state: state[0] < rounds, more, (jnp.int32(1), table_grad))[1]
    return sums + collect(asked, first_sums, rows_here, n_dev)


ENC_BLOCKS = ((0, 3 * D), (3 * D, D), (9 * D, 2 * D), (12 * D, FF), (12 * D + FF, FF))
DEC_BLOCKS = (
    (4 * D, 3 * D),
    (7 * D, D),
    (8 * D, D),
    (11 * D, D),
    (12 * D + 2 * FF, FF),
    (12 * D + 3 * FF, FF),
)


def gather_offloaded(shard, blocks):
    part = jnp.concatenate([shard[:, low : low + width] for low, width in blocks], axis=1)
    return lax.all_gather(part, AXES, axis=0, tiled=True)


def split_blocks(part, blocks):
    gathered, at = ({}, 0)
    for low, width in blocks:
        gathered[low] = (part, at, width)
        at += width
    return gathered


def after(values, *others):
    return lax.optimization_barrier((values,) + others)[0]


def columns(layer_full, first_column, column_count):
    part, start, width = layer_full[first_column]
    assert width == column_count
    return part[:, start : start + width]


def by_column(blocks, gathered):
    return {low: (value, 0, width) for (low, width), value in zip(blocks, gathered)}


def feed(residual, gain_row, layer_full, first_column, streamed):
    if streamed:
        weights = [layer_full[low][:2] for low in (first_column, first_column + FF)]
        return feed_streamed(residual, gain_row, *weights)
    weights = [columns(layer_full, low, FF) for low in (first_column, first_column + FF)]
    return feed_forward(residual, gain_row, *weights)


STAT_ROWS = 512


def stats_kernel(rows_ref, table_ref, targets_ref, stats_ref):
    logits = lax.dot_general(
        table_ref[...], rows_ref[...], (((1,), (1,)), ((), ())), preferred_element_type=jnp.float32
    )
    largest = jnp.max(logits, axis=0, keepdims=True)
    total = jnp.sum(jnp.exp(logits - largest), axis=0, keepdims=True)
    hot = lax.broadcasted_iota(jnp.int32, logits.shape, 0) == targets_ref[...]
    picked = jnp.sum(jnp.where(hot, logits, 0.0), axis=0, keepdims=True)
    stats_ref[...] = jnp.concatenate([largest, total, picked], axis=0)


def stats_alone(all_rows, table_shard, targets_here):
    tokens, vocab = (all_rows.shape[0], table_shard.shape[0])
    return pl.pallas_call(
        stats_kernel,
        grid=(tokens // STAT_ROWS,),
        out_shape=jax.ShapeDtypeStruct((3, tokens), jnp.float32),
        in_specs=[
            pl.BlockSpec((STAT_ROWS, D), lambda step: (step, 0)),
            pl.BlockSpec((vocab, D), lambda step: (0, 0)),
            pl.BlockSpec((1, STAT_ROWS), lambda step: (0, step)),
        ],
        out_specs=pl.BlockSpec((3, STAT_ROWS), lambda step: (0, step)),
        compiler_params=pltpu.CompilerParams(vmem_limit_bytes=40 * 2**20),
        cost_estimate=pl.CostEstimate(
            flops=2 * tokens * vocab * D,
            bytes_accessed=2 * (tokens + vocab) * D,
            transcendentals=tokens * vocab,
        ),
    )(all_rows, table_shard, targets_here[None])


def gather_rows(final_rows, collective_id):
    rows = gather_whole(final_rows, D, collective_id, 45, final_rows.shape[0] // 4)
    return rows.reshape(-1, D)


def combine_stats(stats, collective_id):
    tokens = stats.shape[1]
    stats = stats.reshape(8, -1)
    stats = gather_whole(stats, stats.shape[1], collective_id, 20).reshape(-1, 3, tokens)
    peak = jnp.max(stats[:, 0], axis=0)
    log_own = peak + jnp.log(jnp.sum(stats[:, 1] * jnp.exp(stats[:, 0] - peak), axis=0))
    return (jnp.sum(stats[:, 2], axis=0) - log_own, log_own)


def shard_stats(final_rows, table_shard, targets_here, collective_ids):
    all_rows = gather_rows(final_rows, collective_ids[0])
    logits = jnp.einsum("rd,vd->rv", all_rows, table_shard, preferred_element_type=jnp.float32)
    logits = with_layout_constraint(logits, Layout(major_to_minor=(0, 1)))
    hot = targets_here[:, None] == jnp.arange(table_shard.shape[0])[None, :]
    largest = jnp.max(logits, axis=1)
    total = jnp.sum(jnp.exp(logits - largest[:, None]), axis=1)
    picked = jnp.sum(jnp.where(hot, logits, 0.0), axis=1)
    token_logp, log_own = combine_stats(jnp.stack([largest, total, picked]), collective_ids[1])
    return (token_logp, log_own, logits, hot, all_rows)


def forward(token_rows, enc_full, dec_full_after, gain_rows, batch_data, streamed=False):
    (
        prompt_ids,
        decoder_input,
        targets,
        enc_allowed,
        self_allowed,
        cross_allowed,
        pair_local,
        valid,
    ) = batch_data
    pairs_here, seat_count = (prompt_ids.shape[0], decoder_input.shape[0])
    prompt_count = prompt_ids.size
    encoder_input = token_rows[:prompt_count].astype(jnp.float32)
    encoder_one, encoder_attn = self_forward(
        encoder_input,
        gain_rows[0],
        columns(enc_full, 0, 3 * D),
        columns(enc_full, 3 * D, D),
        enc_allowed,
        (pairs_here, P_MAX),
    )
    encoder_two, encoder_ffn = feed(encoder_one, gain_rows[1], enc_full, 12 * D, streamed)
    encoder_final = to_low(rms_norm(encoder_two, gain_rows[2]))
    cross_memory = to_low(matmul(encoder_final, columns(enc_full, 9 * D, 2 * D))).reshape(
        pairs_here, P_MAX, 2 * D
    )
    layer_full = dec_full_after(cross_memory)
    decoder_zero = token_rows[prompt_count:].astype(jnp.float32)
    decoder_one, decoder_attn = self_forward(
        decoder_zero,
        gain_rows[3],
        columns(layer_full, 4 * D, 3 * D),
        columns(layer_full, 7 * D, D),
        self_allowed,
        (seat_count, R_MAX),
    )
    decoder_two, decoder_cross = cross_forward(
        decoder_one,
        gain_rows[4],
        columns(layer_full, 8 * D, D),
        columns(layer_full, 11 * D, D),
        cross_memory,
        pair_local,
        cross_allowed,
        (seat_count, R_MAX),
    )
    decoder_three, decoder_ffn = feed(
        decoder_two, gain_rows[5], layer_full, 12 * D + 2 * FF, streamed
    )
    final_rows = to_low(final_norm(decoder_three, gain_rows[6]))
    stored = (
        encoder_input,
        encoder_one,
        encoder_two,
        encoder_attn,
        encoder_ffn,
        encoder_final,
        decoder_zero,
        decoder_one,
        decoder_two,
        decoder_three,
        decoder_attn,
        decoder_cross,
        decoder_ffn,
    )
    return (final_rows, stored)


def decoder_backward(layer_full, gain_rows, batch_data, stored, grad_final):
    enc_allowed, self_allowed, cross_allowed = batch_data[3:6]
    decoder_zero, decoder_one, decoder_two, decoder_three = stored[6:10]
    decoder_attn, decoder_cross, decoder_ffn = stored[10:]
    grad_three, gain_six = norm_backward(final_norm, decoder_three, gain_rows[6], grad_final)
    grad_two, gain_five, dec_ffn_pairs = feed_backward(
        decoder_two,
        gain_rows[5],
        columns(layer_full, 12 * D + 2 * FF, FF),
        columns(layer_full, 12 * D + 3 * FF, FF),
        decoder_ffn,
        grad_three,
    )
    grad_one, gain_four, grad_memory, cross_pairs = cross_backward(
        decoder_one,
        gain_rows[4],
        columns(layer_full, 8 * D, D),
        columns(layer_full, 11 * D, D),
        cross_allowed,
        decoder_cross,
        grad_two,
    )
    grad_zero, gain_three, dec_self_pairs = self_backward(
        decoder_zero,
        gain_rows[3],
        columns(layer_full, 4 * D, 3 * D),
        columns(layer_full, 7 * D, D),
        self_allowed,
        decoder_attn,
        grad_one,
    )
    return (
        (gain_three, gain_four, gain_five, gain_six),
        dec_self_pairs + cross_pairs + dec_ffn_pairs,
        grad_memory,
        grad_zero,
    )


def encoder_backward(layer_full, gain_rows, batch_data, stored, memory_low):
    enc_allowed = batch_data[3]
    encoder_input, encoder_one, encoder_two, encoder_attn, encoder_ffn, encoder_final = stored[:6]
    grad_encoder_final = matmul_back(memory_low, columns(layer_full, 9 * D, 2 * D))
    grad_encoder_two, gain_two = norm_backward(
        rms_norm, encoder_two, gain_rows[2], grad_encoder_final
    )
    grad_encoder_one, gain_one, enc_ffn_pairs = feed_backward(
        encoder_one,
        gain_rows[1],
        columns(layer_full, 12 * D, FF),
        columns(layer_full, 12 * D + FF, FF),
        encoder_ffn,
        grad_encoder_two,
    )
    grad_encoder_input, gain_zero, enc_self_pairs = self_backward(
        encoder_input,
        gain_rows[0],
        columns(layer_full, 0, 3 * D),
        columns(layer_full, 3 * D, D),
        enc_allowed,
        encoder_attn,
        grad_encoder_one,
    )
    pairs = enc_self_pairs + ((encoder_final, memory_low),) + enc_ffn_pairs
    return ((gain_zero, gain_one, gain_two), pairs, grad_encoder_input)


def apply_update(weight, moment, average, gradient, factor):
    clipped = gradient * factor
    moment_new = MOMENTUM * moment + clipped
    step_size = -LEARN_RATE * (clipped + MOMENTUM * moment_new)
    weight_new = weight + step_size
    return (
        weight_new,
        moment_new,
        AVERAGE_DECAY * average + (1.0 - AVERAGE_DECAY) * weight_new,
        step_size,
    )


def body(
    prompt_ids,
    prompt_lengths,
    response_ids,
    response_lengths,
    sequence_pair,
    chosen_flag,
    pair_microbatch,
    policy_embed,
    policy_layers,
    policy_gains,
    momentum_embed,
    momentum_layers,
    momentum_gains,
    average_embed,
    average_layers,
    average_gains,
    frozen_embed,
    frozen_layers,
    frozen_gains,
):
    n_dev = lax.axis_size(AXES)
    me = lax.axis_index(AXES)
    rows_here = policy_embed.shape[0]
    pairs_here = prompt_ids.shape[0]
    seat_count = response_ids.shape[0]
    decoder_input = jnp.concatenate(
        [jnp.zeros((seat_count, 1), jnp.int32), response_ids[:, :-1]], axis=1
    )
    pair_local = sequence_pair - me * pairs_here
    select_float = (pair_local[:, None] == jnp.arange(pairs_here)[None, :]).astype(jnp.float32)
    prompt_pos = jnp.arange(P_MAX)
    reply_pos = jnp.arange(R_MAX)
    prompt_keys = prompt_pos[None, :] < prompt_lengths[:, None]
    valid = reply_pos[None, :] < response_lengths[:, None]
    enc_allowed = jnp.broadcast_to(prompt_keys[:, None, :], (pairs_here, P_MAX, P_MAX))
    self_allowed = (reply_pos[:, None] >= reply_pos[None, :])[None] & valid[:, None, :]
    seat_keys = jnp.einsum("sp,pk->sk", select_float, prompt_keys.astype(jnp.float32)) > 0.5
    cross_allowed = jnp.broadcast_to(seat_keys[:, None, :], (seat_count, R_MAX, P_MAX))
    batch_data = (
        prompt_ids,
        decoder_input,
        response_ids,
        enc_allowed,
        self_allowed,
        cross_allowed,
        pair_local,
        valid,
    )
    token_ids = jnp.concatenate([prompt_ids.reshape(-1), decoder_input.reshape(-1)])
    token_live = jnp.concatenate([prompt_keys.reshape(-1), valid.reshape(-1)])
    plan = lookup_plan(token_ids, token_live, rows_here)
    packed = jnp.concatenate(
        [
            round_requests(plan, 0, n_dev),
            response_ids.reshape(-1),
            response_lengths,
            pair_local,
            chosen_flag,
            pair_microbatch,
            plan[5][None],
        ]
    )
    packed = jnp.pad(packed, (0, -packed.shape[0] % 1024)).reshape(8, -1)
    *policy_enc, notes = tree_gather(
        to_low(policy_layers), ENC_BLOCKS, D, 1, 115, extra=packed
    )
    notes = notes.reshape(n_dev, -1)
    asked = mine_of(notes)
    at = n_dev * SLOTS
    cuts = []
    for width in (seat_count * R_MAX, seat_count, seat_count, seat_count, pairs_here, 1):
        cuts.append(notes[:, at : at + width])
        at += width
    targets, all_lengths, all_pair, all_flag, all_micro, all_rounds = cuts
    targets_here = targets.reshape(-1) - me * rows_here
    rounds = jnp.max(all_rounds)
    all_select = (all_pair[:, :, None] == jnp.arange(pairs_here)).astype(jnp.float32)
    pair_micro = (all_micro[:, :, None] == jnp.arange(MICRO)).astype(jnp.float32)
    seat_micro = jnp.sum(all_select[:, :, :, None] * pair_micro[:, None], axis=2)
    chosen_float = all_flag.astype(jnp.float32)
    pair_total = jnp.sum(pair_micro, axis=(0, 1))
    token_total = jnp.sum(
        seat_micro * (chosen_float * all_lengths.astype(jnp.float32))[:, :, None], axis=(0, 1)
    )
    micro_counts = jnp.stack([pair_total, token_total])
    pair_divisor = jnp.sum(pair_micro * pair_total, axis=2)
    sequence_divisor = jnp.sum(seat_micro * token_total, axis=2)
    all_valid = reply_pos < all_lengths[:, :, None]

    policy_table = to_low(policy_embed)
    policy_low = to_low(after(policy_layers, policy_enc[0]))
    policy_dec = gather_offloaded(policy_low, DEC_BLOCKS)
    answers = answer(asked, (policy_table, frozen_embed))
    policy_tokens, frozen_tokens = fetch_rows(plan, answers, rounds, (policy_table, frozen_embed), n_dev)
    policy_layer_enc = by_column(ENC_BLOCKS, policy_enc)
    policy_layer_dec = split_blocks(policy_dec, DEC_BLOCKS)
    policy_layer_full = policy_layer_enc | policy_layer_dec
    def policy_after(memory):
        return policy_layer_dec

    def logp_of(token_logp):
        return jnp.sum(jnp.where(all_valid, token_logp.reshape(all_valid.shape), 0.0), axis=2)

    policy_rows, stored = forward(
        policy_tokens, policy_layer_enc, policy_after, policy_gains, batch_data
    )
    frozen_enc = gather_offloaded(after(frozen_layers, stored[5]), ENC_BLOCKS)
    frozen_dec = gather_offloaded(after(frozen_layers, policy_rows), DEC_BLOCKS)
    frozen_layer_enc = split_blocks(frozen_enc, ENC_BLOCKS)

    def frozen_after(memory):
        return split_blocks(after(frozen_dec, memory), DEC_BLOCKS)

    token_logp, log_own, logits, hot, all_rows = shard_stats(
        policy_rows, policy_table, targets_here, (3, 4)
    )
    policy_logp = logp_of(token_logp)
    row_slope = jnp.where(
        all_valid.reshape(-1)[:, None], hot.astype(jnp.float32) - jnp.exp(logits - log_own[:, None]), 0.0
    )
    row_slope = with_layout_constraint(to_low(row_slope), Layout(major_to_minor=(0, 1)))
    grad_final = scatter_final(row_slope, policy_table, 10)
    dec_gains, dec_pairs, grad_memory, grad_zero = decoder_backward(
        policy_layer_full, policy_gains, batch_data, stored, grad_final
    )
    frozen_inputs = after(frozen_tokens, grad_zero)
    frozen_rows, unused = forward(
        frozen_inputs, frozen_layer_enc, frozen_after, frozen_gains, batch_data, True
    )
    frozen_stats = stats_alone(gather_rows(frozen_rows, 5), frozen_embed, targets_here)
    frozen_logp = logp_of(combine_stats(frozen_stats, 6)[0])
    frozen_mean = lax.dynamic_index_in_dim(
        frozen_logp / all_lengths.astype(jnp.float32), me, 0, keepdims=False
    )

    sign_value = 2.0 * chosen_float - 1.0
    margin = PREFERENCE_BETA * jnp.sum(
        all_select * (sign_value * (policy_logp - frozen_logp))[:, :, None], axis=1
    )
    loss = (
        jnp.sum(jax.nn.softplus(-margin) / pair_divisor)
        - CHOSEN_WEIGHT * jnp.sum(chosen_float * policy_logp / sequence_divisor)
    ) / MICRO
    pair_slope = -PREFERENCE_BETA * jax.nn.sigmoid(-margin) / pair_divisor
    sequence_slope = (
        sign_value * jnp.sum(all_select * pair_slope[:, None, :], axis=2)
        - CHOSEN_WEIGHT * chosen_float / sequence_divisor
    ) / MICRO
    slope_here = lax.dynamic_index_in_dim(sequence_slope, me, 0, keepdims=False)
    slope_rows = jnp.repeat(slope_here, R_MAX)[:, None]
    memory_slope = (select_float * slope_here[:, None])[:, :, None, None, None]
    memory_low = jnp.concatenate(
        [
            join_heads(to_low(jnp.sum(memory_slope * part[:, None], axis=0))).reshape(-1, D)
            for part in grad_memory
        ],
        axis=1,
    )
    enc_gains, enc_pairs, grad_encoder_input = encoder_backward(
        policy_layer_full, policy_gains, batch_data, stored, memory_low
    )
    gain_grads = jnp.stack(
        [jnp.sum(rows, axis=0) for rows in enc_gains]
        + [jnp.sum(slope_rows * rows, axis=0) for rows in dec_gains]
    )
    token_gradient = jnp.concatenate([grad_encoder_input, slope_rows * grad_zero], axis=0)
    enc_pairs = [(to_low(left), to_low(right)) for left, right in enc_pairs]
    scaled_pairs = []
    for left, right in dec_pairs:
        if left.dtype == jnp.float32:
            scaled_pairs.append((to_low(slope_rows * left), right))
        else:
            scaled_pairs.append((left, to_low(slope_rows * right)))
    token_gradient = to_low(token_gradient)
    first_sums = row_sums(picking(plan, 0, n_dev), token_gradient)
    late_slope = after(sequence_slope, first_sums)
    table_grad = jnp.einsum(
        "rc,rd->cd",
        row_slope,
        to_low(jnp.repeat(late_slope.reshape(-1), R_MAX)[:, None] * all_rows),
        preferred_element_type=jnp.float32,
    )
    table_grad = after(table_grad, first_sums)
    enc_pairs[0] = (after(enc_pairs[0][0], first_sums, table_grad), enc_pairs[0][1])
    embed_grad = return_rows(plan, asked, rounds, first_sums, token_gradient, table_grad, n_dev)
    layer_grad, layer_squares = scatter_layers(scaled_pairs, enc_pairs, policy_layers.shape[0], 8)
    squares_local = jnp.sum(embed_grad * embed_grad) + jnp.sum(layer_squares)
    shared = total_of(jnp.concatenate([gain_grads, jnp.full((1, D), squares_local)], axis=0), 9)
    gain_total, squares_total = (shared[:7], shared[7, 0])
    grad_norm = jnp.sqrt(squares_total + jnp.sum(gain_total * gain_total))
    factor = jnp.minimum(1.0, CLIP_NORM / grad_norm)
    embed_new = apply_update(policy_embed, momentum_embed, average_embed, embed_grad, factor)
    layers_new = apply_update(policy_layers, momentum_layers, average_layers, layer_grad, factor)
    gains_new = apply_update(policy_gains, momentum_gains, average_gains, gain_total, factor)
    return (
        loss,
        grad_norm,
        micro_counts,
        frozen_mean,
        embed_new[3],
        layers_new[0],
        gains_new[0],
        embed_new[1],
        layers_new[1],
        gains_new[1],
        embed_new[2],
        layers_new[2],
        gains_new[2],
    )


def solution(mesh):
    placed = (
        P(("dp", "fsdp"), None),
        P(("dp", "fsdp")),
        P(("dp", "fsdp"), None),
        P(("dp", "fsdp")),
        P(("dp", "fsdp")),
        P(("dp", "fsdp")),
        P(("dp", "fsdp")),
        P(("dp", "fsdp"), None),
        P(("dp", "fsdp"), None),
        P(),
        P(("dp", "fsdp"), None),
        P(("dp", "fsdp"), None),
        P(),
        P(("dp", "fsdp"), None),
        P(("dp", "fsdp"), None),
        P(),
        P(("dp", "fsdp"), None),
        P(("dp", "fsdp"), None),
        P(),
    )
    return jax.shard_map(
        body,
        mesh=mesh,
        in_specs=placed,
        out_specs=(
            P(),
            P(),
            P(),
            P(("dp", "fsdp")),
            P(("dp", "fsdp"), None),
            P(("dp", "fsdp"), None),
            P(),
            P(("dp", "fsdp"), None),
            P(("dp", "fsdp"), None),
            P(),
            P(("dp", "fsdp"), None),
            P(("dp", "fsdp"), None),
            P(),
        ),
        check_vma=False,
    )
```

```python
import functools

import jax
import jax.numpy as jnp
from jax import lax
from jax.experimental import pallas as pl
from jax.experimental.layout import Layout, with_layout_constraint
from jax.experimental.pallas import tpu as pltpu
from jax.sharding import PartitionSpec as P

D = 1024
HEADS = 16
HEAD = 64
FF = 4096
P_MAX = 192
R_MAX = 32
MICRO = 2


EPSILON = 1e-06
SCORE_SCALE = 0.125
PREFERENCE_BETA = 0.1
CHOSEN_WEIGHT = 1.0
MOMENTUM = 0.9
LEARN_RATE = 2000.0
AVERAGE_DECAY = 0.5
CLIP_NORM = 0.04
MASK_FILL = -1000000000.0
HIGHEST = lax.Precision.HIGHEST


def rms_norm(values, gain_row):
    return (
        values * lax.rsqrt(jnp.mean(values * values, axis=-1, keepdims=True) + EPSILON) * gain_row
    )


def final_norm(values, gain_row):
    return rms_norm(values, gain_row) * D ** (-0.5)


def to_low(values):
    return values.astype(jnp.bfloat16)


def matmul(left_side, right_side):
    return jnp.dot(left_side, right_side, preferred_element_type=jnp.float32)


def matmul_back(grad_low, weight):
    return jnp.einsum("re,de->rd", grad_low, weight, preferred_element_type=jnp.float32)


def split_heads(values):
    return values.reshape(values.shape[0], values.shape[1], HEADS, HEAD)


def scores_of(queries, key_rows, allowed):
    raw_scores = (
        jnp.einsum(
            "bqhe,bkhe->bhqk",
            split_heads(queries),
            split_heads(key_rows),
            preferred_element_type=jnp.float32,
        )
        * SCORE_SCALE
    )
    return jnp.where(allowed[:, None], raw_scores, MASK_FILL)


def attend_forward(queries, key_rows, values, allowed):
    scores = scores_of(queries, key_rows, allowed)
    log_total = jax.nn.logsumexp(scores, axis=-1, keepdims=True)
    softmax_out = to_low(jnp.exp(scores - log_total))
    mixed_out = jnp.einsum(
        "bhqk,bkhe->bqhe", softmax_out, split_heads(values), preferred_element_type=jnp.float32
    )
    return (to_low(mixed_out.reshape(queries.shape)), log_total)


def attend_backward(queries, key_rows, values, allowed, log_total, grad_mixed):
    softmax_out = jnp.exp(scores_of(queries, key_rows, allowed) - log_total)
    grad_heads = split_heads(to_low(grad_mixed))
    grad_values = jnp.einsum(
        "bhqk,bqhe->bhke", to_low(softmax_out), grad_heads, preferred_element_type=jnp.float32
    )
    grad_probs = jnp.einsum(
        "bqhe,bkhe->bhqk", grad_heads, split_heads(values), preferred_element_type=jnp.float32
    )
    grad_scores = to_low(
        softmax_out * (grad_probs - jnp.sum(grad_probs * softmax_out, axis=-1, keepdims=True))
    )
    grad_query = (
        jnp.einsum(
            "bhqk,bkhe->bqhe",
            grad_scores,
            split_heads(key_rows),
            preferred_element_type=jnp.float32,
        )
        * SCORE_SCALE
    )
    grad_keys = (
        jnp.einsum(
            "bhqk,bqhe->bhke", grad_scores, split_heads(queries), preferred_element_type=jnp.float32
        )
        * SCORE_SCALE
    )
    return (grad_query.reshape(queries.shape), grad_keys, grad_values)


def join_heads(values):
    return values.transpose(0, 2, 1, 3).reshape(values.shape[0], values.shape[2], D)


def self_forward(residual, gain_row, weight_three, weight_out, allowed, shape_pair):
    normed = to_low(rms_norm(residual, gain_row))
    triple = to_low(matmul(normed, weight_three)).reshape(shape_pair[0], shape_pair[1], 3 * D)
    mixed_out, log_total = attend_forward(
        triple[..., :D], triple[..., D : 2 * D], triple[..., 2 * D :], allowed
    )
    flat_mixed = mixed_out.reshape(-1, D)
    return (residual + matmul(flat_mixed, weight_out), (normed, triple, log_total, flat_mixed))


def norm_backward(norm, residual, gain_row, grad_normed):
    grad_residual = jax.vjp(lambda values: norm(values, gain_row), residual)[1](grad_normed)[0]
    return grad_residual, grad_normed * norm(residual, jnp.ones_like(gain_row))


def self_backward(residual, gain_row, weight_three, weight_out, allowed, stored, grad_out):
    normed, triple, log_total, flat_mixed = stored
    grad_mixed = matmul_back(to_low(grad_out), weight_out)
    queries = triple[..., :D]
    grad_query, grad_keys, grad_values = attend_backward(
        queries,
        triple[..., D : 2 * D],
        triple[..., 2 * D :],
        allowed,
        log_total,
        grad_mixed.reshape(queries.shape),
    )
    grads = (grad_query, join_heads(grad_keys), join_heads(grad_values))
    grad_triple = jnp.concatenate(grads, axis=-1).reshape(-1, 3 * D)
    grad_normed = matmul_back(to_low(grad_triple), weight_three)
    grad_residual, gain_rows = norm_backward(rms_norm, residual, gain_row, grad_normed)
    return (grad_out + grad_residual, gain_rows, ((normed, grad_triple), (flat_mixed, grad_out)))


def cross_forward(
    residual, gain_row, weight_query, weight_out, cross_memory, pair_local, allowed, shape_pair
):
    normed = to_low(rms_norm(residual, gain_row))
    queries = to_low(matmul(normed, weight_query)).reshape(shape_pair[0], shape_pair[1], D)
    seat_memory = jnp.broadcast_to(cross_memory[:1], (shape_pair[0],) + cross_memory.shape[1:])
    for pair in range(1, cross_memory.shape[0]):
        seat_memory = jnp.where(
            pair_local[:, None, None] == pair, cross_memory[pair][None], seat_memory
        )
    mixed_out, log_total = attend_forward(
        queries, seat_memory[..., :D], seat_memory[..., D:], allowed
    )
    flat_mixed = mixed_out.reshape(-1, D)
    return (
        residual + matmul(flat_mixed, weight_out),
        (normed, queries, seat_memory, log_total, flat_mixed),
    )


def cross_backward(residual, gain_row, weight_query, weight_out, allowed, stored, grad_out):
    normed, queries, seat_memory, log_total, flat_mixed = stored
    grad_mixed = matmul_back(to_low(grad_out), weight_out)
    grad_query, grad_keys, grad_values = attend_backward(
        queries,
        seat_memory[..., :D],
        seat_memory[..., D:],
        allowed,
        log_total,
        grad_mixed.reshape(queries.shape),
    )
    grad_query = grad_query.reshape(-1, D)
    grad_normed = matmul_back(to_low(grad_query), weight_query)
    grad_residual, gain_rows = norm_backward(rms_norm, residual, gain_row, grad_normed)
    return (
        grad_out + grad_residual,
        gain_rows,
        (grad_keys, grad_values),
        ((normed, grad_query), (flat_mixed, grad_out)),
    )


def feed_forward(residual, gain_row, weight_in, weight_out):
    normed = to_low(rms_norm(residual, gain_row))
    before = matmul(normed, weight_in)
    active = to_low(jax.nn.relu(before))
    return (
        residual + jnp.einsum("rf,df->rd", active, weight_out, preferred_element_type=jnp.float32),
        (normed, active),
    )


def feed_backward(residual, gain_row, weight_in, weight_out, stored, grad_out):
    normed, active = stored
    grad_active = matmul(to_low(grad_out), weight_out)
    grad_before = jnp.where(active > 0, grad_active, 0.0)
    grad_normed = matmul_back(to_low(grad_before), weight_in)
    grad_residual, gain_rows = norm_backward(rms_norm, residual, gain_row, grad_normed)
    return (grad_out + grad_residual, gain_rows, ((normed, grad_before), (grad_out, active)))


AXES = ("dp", "fsdp")


FF_STEP = 512


def norm_scale(values):
    return lax.rsqrt(jnp.mean(values * values, axis=-1, keepdims=True) + EPSILON)


def feed_kernel(residual_ref, gain_ref, in_ref, out_ref, result_ref, normed_ref):
    @pl.when(pl.program_id(0) == 0)
    def _():
        residual = residual_ref[...]
        normed_ref[...] = to_low(residual * norm_scale(residual) * gain_ref[...])
        result_ref[...] = residual

    before = jnp.dot(normed_ref[...], in_ref[...], preferred_element_type=jnp.float32)
    active = to_low(jax.nn.relu(before))
    result_ref[...] += lax.dot_general(
        active, out_ref[...], (((1,), (1,)), ((), ())), preferred_element_type=jnp.float32
    )


def weight_spec(start):
    return pl.BlockSpec((D, FF_STEP), lambda step: (0, step + start // FF_STEP))


def whole_spec(shape):
    return pl.BlockSpec(shape, lambda step: (0,) * len(shape))


def feed_cost(rows):
    return pl.CostEstimate(flops=4 * rows * D * FF, bytes_accessed=4 * D * FF, transcendentals=0)


def feed_streamed(residual, gain_row, weight_in, weight_out):
    rows = residual.shape[0]
    (source_in, start_in), (source_out, start_out) = (weight_in, weight_out)
    result = pl.pallas_call(
        feed_kernel,
        grid=(FF // FF_STEP,),
        out_shape=jax.ShapeDtypeStruct((rows, D), jnp.float32),
        in_specs=[
            whole_spec((rows, D)),
            whole_spec((1, D)),
            weight_spec(start_in),
            weight_spec(start_out),
        ],
        out_specs=whole_spec((rows, D)),
        scratch_shapes=[pltpu.VMEM((rows, D), jnp.bfloat16)],
        compiler_params=pltpu.CompilerParams(vmem_limit_bytes=40 * 2**20),
        cost_estimate=feed_cost(rows),
    )(residual, gain_row[None], source_in, source_out)
    return (result, None)


SLOTS = 24
MESH = pl.DeviceIdType.MESH


def device_bits():
    bits = []
    for axis in AXES:
        mask = lax.axis_size(axis) // 2
        while mask:
            bits.append((axis, mask))
            mask //= 2
    return bits


def scatter_orders():
    core, across = (("dp", 1), ("dp", 2))
    inner = [bit for bit in reversed(device_bits()) if bit[0] == "fsdp"]
    first, rest = inner[:1], inner[1:]
    return (
        [core, across] + rest + first,
        [core] + inner + [across],
        [core, across] + first + rest,
        [core] + first + [across] + rest,
    )


def lane_widths(width):
    if width % D == 0:
        return (3 * width // 8, 3 * width // 8, width // 8, width // 8)
    return (width // 4,) * 4


def bit_of(bit):
    axis, mask = bit
    return (lax.axis_index(axis) // mask) % 2


def partner(bit):
    axis, mask = bit
    return {axis: lax.axis_index(axis) + mask * (1 - 2 * bit_of(bit))}


def greet(bits):
    barrier = pltpu.get_barrier_semaphore()
    for bit in bits:
        pl.semaphore_signal(barrier, inc=1, device_id=partner(bit), device_id_type=MESH)
    pl.semaphore_wait(barrier, len(bits))


def gather_kernel(bits, n_in, waves, *refs):
    ins, outs, (own_sem, send_sem, recv_sem) = (refs[:n_in], refs[n_in:-3], refs[-3:])
    mine = {bit: bit_of(bit) for bit in bits}
    depth = len(bits)
    greet(bits)
    index, sent, kept = ({}, {}, {})
    for turn in range(len(waves) + depth):
        for step in range(depth + 1):
            wave = turn - step
            if not 0 <= wave < len(waves):
                continue
            for lane, (number, which, start, low, width, first, count, order) in enumerate(
                waves[wave]
            ):
                slot = index.setdefault((wave, lane), len(index))
                lead = tuple(
                    pl.ds(0, 2) if bit in order[:step] else pl.ds(mine[bit], 1) for bit in bits
                )
                place = outs[which].at[lead + (pl.ds(first, count), pl.ds(low, width))]
                source = place
                if step == 0:
                    whole = (slice(None),) * depth
                    source = ins[number].at[whole + (pl.ds(first, count), pl.ds(start, width))]
                    kept[slot] = pltpu.make_async_copy(source, place, own_sem.at[slot])
                    kept[slot].start()
                else:
                    sent[slot, step - 1].wait_recv()
                if step == 1:
                    kept[slot].wait()
                if step < depth:
                    sent[slot, step] = pltpu.make_async_remote_copy(
                        src_ref=source,
                        dst_ref=place,
                        send_sem=send_sem.at[slot, step],
                        recv_sem=recv_sem.at[slot, step],
                        device_id=partner(order[step]),
                        device_id_type=MESH,
                    )
                    sent[slot, step].start()
    for copy in sent.values():
        copy.wait_send()


def busy_for(micros):
    return pl.CostEstimate(flops=0, bytes_accessed=int(micros * 3.4e6), transcendentals=0)


def tree_gather(shard, blocks, step, collective_id, micros, row_step=None, extra=None):
    bits = device_bits()
    rows = shard.shape[0]
    row_step = row_step or rows
    waves = []
    for which, (start, width) in enumerate(blocks):
        for low in range(0, width, step):
            for first in range(0, rows, row_step):
                wave, at = ([], low)
                for lane, order in zip(lane_widths(step), scatter_orders()):
                    piece = (0, which, start + at, at, lane, first, row_step)
                    wave.append(piece + (tuple(reversed(order)),))
                    at += lane
                waves.append(wave)
    operands = [shard]
    shapes = [((rows, width), shard.dtype) for _, width in blocks]
    if extra is not None:
        operands.append(extra)
        shapes.append((extra.shape, extra.dtype))
        piece = (1, len(blocks), 0, 0, extra.shape[1], 0, extra.shape[0])
        waves[0].append(piece + (tuple(reversed(scatter_orders()[0])),))
    total = sum(len(wave) for wave in waves)
    gathered = pl.pallas_call(
        functools.partial(gather_kernel, bits, len(operands), waves),
        out_shape=[
            jax.ShapeDtypeStruct((2,) * len(bits) + shape, dtype) for shape, dtype in shapes
        ],
        in_specs=[pl.BlockSpec(memory_space=pl.ANY)] * len(operands),
        out_specs=[pl.BlockSpec(memory_space=pl.ANY)] * len(shapes),
        scratch_shapes=[
            pltpu.SemaphoreType.DMA((total,)),
            pltpu.SemaphoreType.DMA((total, len(bits))),
            pltpu.SemaphoreType.DMA((total, len(bits))),
        ],
        compiler_params=pltpu.CompilerParams(collective_id=collective_id, has_side_effects=True),
        cost_estimate=busy_for(micros),
    )(*[value.reshape((1,) * len(bits) + value.shape) for value in operands])
    return [value.reshape((-1, shape[1])) for value, (shape, _) in zip(gathered, shapes)]


def gather_whole(values, step, collective_id, micros, row_step=None):
    blocks = [(0, values.shape[1])]
    full = tree_gather(values, blocks, step, collective_id, micros, row_step)[0]
    return full.reshape((-1,) + values.shape)


def total_kernel(sizes, x_ref, sum_ref, *scratch):
    held, send_sem, recv_sem = (scratch[:2], scratch[2:4], scratch[4:6])
    barrier = pltpu.get_barrier_semaphore()
    peers = [(axis, hop) for axis, size in sizes for hop in range(1, size)]

    def peer(axis, size, hop):
        return {axis: lax.rem(lax.axis_index(axis) + hop, size)}

    for axis, hop in peers:
        pl.semaphore_signal(
            barrier, inc=1, device_id=peer(axis, dict(sizes)[axis], hop), device_id_type=MESH
        )
    pl.semaphore_wait(barrier, len(peers))
    value = x_ref[...]
    for turn, (axis, size) in enumerate(sizes):
        me = lax.axis_index(axis)
        held[turn][me] = value
        copies = []
        for hop in range(1, size):
            copies.append(
                pltpu.make_async_remote_copy(
                    src_ref=held[turn].at[me],
                    dst_ref=held[turn].at[me],
                    send_sem=send_sem[turn].at[hop],
                    recv_sem=recv_sem[turn].at[hop],
                    device_id=peer(axis, size, hop),
                    device_id_type=MESH,
                )
            )
            copies[-1].start()
        for hop, copy in enumerate(copies, 1):
            other = lax.rem(me + size - hop, size)
            pltpu.make_async_remote_copy(
                src_ref=held[turn].at[other],
                dst_ref=held[turn].at[other],
                send_sem=send_sem[turn].at[hop],
                recv_sem=recv_sem[turn].at[hop],
                device_id=peer(axis, size, hop),
                device_id_type=MESH,
            ).wait_recv()
        value = held[turn][0]
        for other in range(1, size):
            value = value + held[turn][other]
        for copy in copies:
            copy.wait_send()
    sum_ref[...] = value


def total_of(tile, collective_id):
    sizes = [(axis, lax.axis_size(axis)) for axis in reversed(AXES)]
    in_vmem = pl.BlockSpec(memory_space=pltpu.VMEM)
    marks = [pltpu.SemaphoreType.DMA((size,)) for _, size in sizes]
    return pl.pallas_call(
        functools.partial(total_kernel, sizes),
        out_shape=jax.ShapeDtypeStruct(tile.shape, jnp.float32),
        in_specs=[in_vmem],
        out_specs=in_vmem,
        scratch_shapes=[pltpu.VMEM((size,) + tile.shape, jnp.float32) for _, size in sizes]
        + marks
        + marks,
        compiler_params=pltpu.CompilerParams(collective_id=collective_id, has_side_effects=True),
        cost_estimate=busy_for(12),
    )(tile)


CORE_SLOTS = 2


def scatter_kernel(bits, plan, *refs):
    n_waves, slots, wide, widths = (plan["waves"], plan["slots"], plan["wide"], plan["widths"])
    n_ins, n_loaded = (plan["operands"], len(plan["loads"]))
    ins, out_ref = (refs[:n_ins], refs[n_ins])
    loaded, rest_refs = (refs[n_ins + 1 : n_ins + 1 + n_loaded], refs[n_ins + 1 + n_loaded :])
    buffers = [rest_refs[6 * lane : 6 * lane + 6] for lane in range(len(widths))]
    load_sem, send_sem, recv_sem, free_sem = rest_refs[6 * len(widths) :]
    depth = len(bits)
    mine = {bit: bit_of(bit) for bit in bits}
    core = scatter_orders()[0][0]
    rest = [bit for bit in bits if bit != core]

    def half(order, step, kept):
        bit_at = {bit: pl.ds(mine[bit], 1) for bit in order[1:step]}
        last = mine[order[step]] if kept else 1 - mine[order[step]]
        bit_at[order[step]] = pl.ds(last, 1)
        return tuple(bit_at.get(bit, pl.ds(0, 2)) for bit in rest)

    def span_of(step):
        return CORE_SLOTS if step == 0 else slots

    def copy(wave, lane, step, order):
        send_core, from_core, total, narrow, arrived, arrived_wide = buffers[lane]
        slot = lax.rem(wave, span_of(step))
        if step == 0:
            source, target = (send_core.at[slot], from_core.at[slot])
        else:
            source = (total if step in wide else narrow).at[(slot,) + half(order, step, False)]
            target = arrived_wide if step in wide else arrived
            target = target.at[(slot,) + half(order, step, True)]
        return pltpu.make_async_remote_copy(
            src_ref=source,
            dst_ref=target,
            send_sem=send_sem.at[lane, slot, step],
            recv_sem=recv_sem.at[lane, slot, step],
            device_id=partner(order[step]),
            device_id_type=MESH,
        )

    def kept_entries(order, step):
        left = [bit for bit in rest if bit not in order[: step + 1]]
        for number in range(2 ** len(left)):
            chosen = {bit: (number >> place) % 2 for place, bit in enumerate(reversed(left))}
            here = tuple(chosen.get(bit, mine[bit]) for bit in rest)
            came = tuple(1 - mine[bit] if bit == order[step] else at for bit, at in zip(rest, here))
            yield here, came

    def visit(wave, lane, step, order):
        send_core, from_core, total, narrow, arrived, arrived_wide = buffers[lane]
        low, width = (sum(widths[:lane]), widths[lane])
        slot = lax.rem(wave, span_of(step))
        reuse = wave >= span_of(step)

        def keep(at, value, next_step):
            total[(slot,) + at] = value
            if next_step not in wide:
                narrow[(slot,) + at] = value.astype(jnp.bfloat16)

        if step == 0:

            @pl.when(reuse)
            def _():
                copy(wave, lane, 0, order).wait_send()

            def put(at, value):
                send_core[(slot,) + at] = value

            plan["produce"](loaded, wave, low, width, 1 - mine[core], put)
        else:
            copy(wave, lane, step - 1, order).wait_recv()
            if step == 1:
                core_slot = lax.rem(wave, CORE_SLOTS)

                @pl.when(reuse)
                def _():
                    for old in range(1, depth):
                        copy(wave, lane, old, order).wait_send()

                def add(at, value):
                    keep(at, value + from_core[(core_slot,) + at], 1)

                plan["produce"](loaded, wave, low, width, mine[core], add)
            else:
                source = arrived_wide if step - 1 in wide else arrived
                for here, came in kept_entries(order, step - 1):
                    value = total[(slot,) + here] + source[(slot,) + came].astype(jnp.float32)
                    if step == depth:
                        start = plan["column"](wave) + low
                        out_ref[:, pl.ds(pl.multiple_of(start, 128), width)] = value
                    else:
                        keep(here, value, step)

            @pl.when(wave + span_of(step - 1) < n_waves)
            def _():
                pl.semaphore_signal(
                    free_sem.at[lane, lax.rem(wave, span_of(step - 1)), step - 1],
                    inc=1,
                    device_id=partner(order[step - 1]),
                    device_id_type=MESH,
                )

        if step < depth:

            @pl.when(reuse)
            def _():
                pl.semaphore_wait(free_sem.at[lane, slot, step], 1)

            copy(wave, lane, step, order).start()

    loads = []
    for number, (_, parts) in enumerate(plan["loads"]):
        for operand, place in parts:
            at = loaded[number].at[place] if place else loaded[number]
            loads.append(pltpu.make_async_copy(ins[operand], at, load_sem.at[operand]))
            loads[-1].start()

    def turn_of(turn, carry):
        for step in range(depth + 1):
            wave = turn - step

            @pl.when((wave >= 0) & (wave < n_waves))
            def _():
                if step == 0:
                    for late, count in plan["waits"]:

                        @pl.when(wave == late)
                        def _():
                            for load in loads[slice(*count)]:
                                load.wait()

                for lane, order in enumerate(plan["orders"]):
                    visit(wave, lane, step, order)

        return carry

    greet(bits)
    lax.fori_loop(0, n_waves + depth, turn_of, 0)
    for step in range(depth):
        for wave in range(max(0, n_waves - span_of(step)), n_waves):
            for lane, order in enumerate(plan["orders"]):
                copy(wave, lane, step, order).wait_send()


def tree_scatter(operands, plan, collective_id, micros):
    bits = device_bits()
    slots, widths, rows = (plan["slots"], plan["widths"], plan["rows"])
    plan = dict(plan, operands=len(operands))
    scratch = [pltpu.VMEM(shape, jnp.bfloat16) for shape, _ in plan["loads"]]
    for width in widths:
        entries = (2,) * (len(bits) - 1) + (rows, width)
        core_buffer = pltpu.VMEM((CORE_SLOTS,) + entries, jnp.float32)
        low_buffer = pltpu.VMEM((slots,) + entries, jnp.bfloat16)
        sums = pltpu.VMEM((slots,) + entries, jnp.float32)
        wide_buffer = sums if plan["wide"] else pltpu.VMEM((8, 128), jnp.float32)
        scratch += [core_buffer, core_buffer, sums, low_buffer, low_buffer, wide_buffer]
    marks = (len(widths), slots, len(bits))
    return pl.pallas_call(
        functools.partial(scatter_kernel, bits, plan),
        out_shape=jax.ShapeDtypeStruct((rows, plan["waves"] * sum(widths)), jnp.float32),
        in_specs=[pl.BlockSpec(memory_space=pl.ANY)] * len(operands),
        out_specs=pl.BlockSpec(memory_space=pltpu.VMEM),
        scratch_shapes=scratch
        + [
            pltpu.SemaphoreType.DMA((len(operands),)),
            pltpu.SemaphoreType.DMA(marks),
            pltpu.SemaphoreType.DMA(marks),
            pltpu.SemaphoreType.REGULAR(marks),
        ],
        compiler_params=pltpu.CompilerParams(
            collective_id=collective_id, has_side_effects=True, vmem_limit_bytes=60 * 2**20
        ),
        cost_estimate=busy_for(micros),
    )(*operands)


def unit_of(block, blocks):
    edges, most = ([], sum(blocks))
    for count in blocks[:-1]:
        edges.append(count + (edges[-1] if edges else 0))
    return sum(lax.div(block + (most - edge), most) for edge in edges)


def put_rows(value, across, rows, put):
    rest_count = (value.shape[0] // rows).bit_length() - 1
    for number in range(2**rest_count):
        at = tuple((number >> place) % 2 for place in reversed(range(rest_count)))
        put((across,) + at, value[number * rows : (number + 1) * rows])


def layer_products(dec_blocks, enc_blocks, rows, loaded, wave, low, width, core, put):
    dec_left, dec_right, enc_left, enc_right = loaded
    dec_waves = sum(dec_blocks)
    quarter = D // 4

    def product(left, right, blocks, block):
        unit = unit_of(block, blocks)
        sides = right[:, pl.ds(pl.multiple_of(block * D + low, 128), width)]
        for across in range(2):
            some = pl.ds(pl.multiple_of((2 * across + core) * quarter, quarter), quarter)
            value = lax.dot_general(
                left[unit, :, some],
                sides,
                (((0,), (0,)), ((), ())),
                preferred_element_type=jnp.float32,
            )
            put_rows(value, across, rows, put)

    @pl.when(wave < dec_waves)
    def _():
        product(dec_left, dec_right, dec_blocks, wave)

    @pl.when(wave >= dec_waves)
    def _():
        product(enc_left, enc_right, enc_blocks, wave - dec_waves)


def layer_column(wave):
    is_enc = lax.div(wave, 14)
    block = wave - is_enc * 14

    def past(edge):
        return lax.div(block + 14 - edge, 14)

    dec_shift = 4 + 2 * past(5) + 8 * past(6)
    enc_shift = 5 * past(4) + past(6)
    shift = dec_shift + is_enc * (enc_shift - dec_shift)
    return (block + shift) * D


def scatter_layers(dec_pairs, enc_pairs, rows, collective_id):
    operands, loads, counts = ([], [], [])
    for pairs in (dec_pairs, enc_pairs):
        tokens, parts, at = (pairs[0][0].shape[0], [], 0)
        for unit, (left_side, _) in enumerate(pairs):
            parts.append((len(operands), (unit,)))
            operands.append(left_side)
        loads.append(((len(pairs), tokens, D), parts))
        parts = []
        for _, right_side in pairs:
            parts.append((len(operands), (slice(None), pl.ds(at, right_side.shape[1]))))
            operands.append(right_side)
            at += right_side.shape[1]
        loads.append(((tokens, at), parts))
        counts.append([right_side.shape[1] // D for _, right_side in pairs])
    dec_loads = 2 * len(dec_pairs)
    plan = {
        "waves": sum(counts[0]) + sum(counts[1]),
        "slots": 6,
        "widths": lane_widths(D),
        "orders": scatter_orders(),
        "rows": rows,
        "wide": (),
        "loads": loads,
        "waits": ((0, (0, dec_loads)), (sum(counts[0]), (dec_loads, None))),
        "produce": functools.partial(layer_products, counts[0], counts[1], rows),
        "column": layer_column,
    }
    return tree_scatter(operands, plan, collective_id, 210)


def final_products(step, rows, loaded, wave, low, width, core, put):
    left, right = loaded
    sides = right[:, pl.ds(pl.multiple_of(wave * step + low, 128), width)]
    for across in range(2):
        value = jnp.dot(left[across, core], sides, preferred_element_type=jnp.float32)
        put_rows(value, across, rows, put)


def scatter_final(grad_logits, table, collective_id):
    bits = device_bits()
    n_dev, step, width = (2 ** len(bits), 256, table.shape[1])
    rows_all = grad_logits.shape[0] // n_dev
    turns = max(1, n_dev // 32)
    rows = rows_all // turns
    sums = []
    for turn in range(turns):
        some = grad_logits.reshape(n_dev, rows_all, -1)[:, turn * rows : (turn + 1) * rows]
        some = some.reshape(2, 2, n_dev // 4 * rows, -1)
        plan = {
            "waves": width // step,
            "slots": width // step,
            "widths": (step // 2, step // 2),
            "orders": scatter_orders()[:2],
            "rows": rows,
            "wide": (),
            "loads": [(some.shape, [(0, ())]), (table.shape, [(1, ())])],
            "waits": ((0, (0, 2)),),
            "produce": functools.partial(final_products, step, rows),
            "column": lambda wave: wave * step,
        }
        sums.append(tree_scatter([some, table], plan, collective_id + turn, 60))
    return jnp.concatenate(sums, axis=0)


def lookup_plan(ids, live, rows_here):
    count = ids.shape[0]
    owner = ids // rows_here
    same = (ids[:, None] == ids[None, :]) & live[None, :]
    earlier = jnp.arange(count)[None, :] < jnp.arange(count)[:, None]
    first = live & ~jnp.any(same & earlier, axis=1)
    below = first[None, :] & (owner[:, None] == owner[None, :]) & (ids[None, :] < ids[:, None])
    rank = jnp.sum(below.astype(jnp.int32), axis=1)
    rounds = jnp.max(jnp.where(live, rank, 0)) // SLOTS + 1
    return (owner, ids - owner * rows_here, first, live, rank, rounds)


def round_flat(plan, turn):
    owner, _, _, live, rank, _ = plan
    slot = rank - turn * SLOTS
    return jnp.where(live & (slot >= 0) & (slot < SLOTS), owner * SLOTS + slot, -1)


def round_requests(plan, turn, n_dev):
    flat = round_flat(plan, turn)
    hit = (flat[:, None] == jnp.arange(n_dev * SLOTS)[None, :]) & plan[2][:, None]
    return jnp.sum(jnp.where(hit, plan[1][:, None] + 1, 0), axis=0) - 1


def picking(plan, turn, n_dev):
    return (
        round_flat(plan, turn)[:, None] == jnp.arange(n_dev * SLOTS)[None, :]
    ).astype(jnp.bfloat16)


def asked_hot(asked, rows_here):
    return (asked.reshape(-1)[:, None] == jnp.arange(rows_here)[None, :]).astype(jnp.bfloat16)


def mine_of(table):
    return lax.dynamic_slice_in_dim(table, lax.axis_index(AXES) * SLOTS, SLOTS, axis=1)


def swap(rows, n_dev):
    wide = rows.shape[-1]
    return lax.all_to_all(
        rows.reshape(n_dev, SLOTS, wide), AXES, 0, 0, tiled=True
    ).reshape(n_dev * SLOTS, wide)


def answer(asked, tables):
    hot = asked_hot(asked, tables[0].shape[0])
    return jnp.concatenate([to_low(matmul(hot, table)) for table in tables], axis=1)


def pick_rows(pick, rows):
    return (to_low(matmul(pick, rows[:, :D])), to_low(matmul(pick, rows[:, D:])))


def added(some, others):
    return jax.tree.map(jnp.add, some, others)


def fetch_rows(plan, answers, rounds, tables, n_dev):
    rows = pick_rows(picking(plan, 0, n_dev), swap(answers, n_dev))

    def more(state):
        turn, rows = state
        asked = mine_of(lax.all_gather(round_requests(plan, turn, n_dev), AXES, axis=0))
        pick = picking(plan, turn, n_dev)
        return (turn + 1, added(rows, pick_rows(pick, swap(answer(asked, tables), n_dev))))

    return lax.while_loop(lambda state: state[0] < rounds, more, (jnp.int32(1), rows))[1]


def collect(asked, sums, rows_here, n_dev):
    return jnp.einsum(
        "kc,kd->cd",
        asked_hot(asked, rows_here),
        swap(sums, n_dev),
        preferred_element_type=jnp.float32,
    )


def row_sums(pick, gradient):
    return to_low(jnp.einsum("nk,nd->kd", pick, gradient, preferred_element_type=jnp.float32))


def return_rows(plan, asked, rounds, first_sums, gradient, table_grad, n_dev):
    rows_here = table_grad.shape[0]

    def more(state):
        turn, sums = state
        asked = mine_of(lax.all_gather(round_requests(plan, turn, n_dev), AXES, axis=0))
        pick = picking(plan, turn, n_dev)
        return (turn + 1, sums + collect(asked, row_sums(pick, gradient), rows_here, n_dev))

    sums = lax.while_loop(lambda state: state[0] < rounds, more, (jnp.int32(1), table_grad))[1]
    return sums + collect(asked, first_sums, rows_here, n_dev)


ENC_BLOCKS = ((0, 3 * D), (3 * D, D), (9 * D, 2 * D), (12 * D, FF), (12 * D + FF, FF))
DEC_BLOCKS = (
    (4 * D, 3 * D),
    (7 * D, D),
    (8 * D, D),
    (11 * D, D),
    (12 * D + 2 * FF, FF),
    (12 * D + 3 * FF, FF),
)


def gather_offloaded(shard, blocks):
    part = jnp.concatenate([shard[:, low : low + width] for low, width in blocks], axis=1)
    return lax.all_gather(part, AXES, axis=0, tiled=True)


def split_blocks(part, blocks):
    gathered, at = ({}, 0)
    for low, width in blocks:
        gathered[low] = (part, at, width)
        at += width
    return gathered


def after(values, *others):
    return lax.optimization_barrier((values,) + others)[0]


def columns(layer_full, first_column, column_count):
    part, start, width = layer_full[first_column]
    assert width == column_count
    return part[:, start : start + width]


def by_column(blocks, gathered):
    return {low: (value, 0, width) for (low, width), value in zip(blocks, gathered)}


def feed(residual, gain_row, layer_full, first_column, streamed):
    if streamed:
        weights = [layer_full[low][:2] for low in (first_column, first_column + FF)]
        return feed_streamed(residual, gain_row, *weights)
    weights = [columns(layer_full, low, FF) for low in (first_column, first_column + FF)]
    return feed_forward(residual, gain_row, *weights)


def shard_stats(final_rows, table_shard, targets, collective_ids):
    all_rows = gather_whole(final_rows, D, collective_ids[0], 45, final_rows.shape[0] // 4)
    all_rows = all_rows.reshape(-1, D)
    logits = jnp.einsum("rd,vd->rv", all_rows, table_shard, preferred_element_type=jnp.float32)
    logits = with_layout_constraint(logits, Layout(major_to_minor=(0, 1)))
    low = lax.axis_index(AXES) * table_shard.shape[0]
    hot = (targets - low)[:, None] == jnp.arange(table_shard.shape[0])[None, :]
    largest = jnp.max(logits, axis=1)
    total = jnp.sum(jnp.exp(logits - largest[:, None]), axis=1)
    picked = jnp.sum(jnp.where(hot, logits, 0.0), axis=1)
    stats = jnp.concatenate([part.reshape(8, -1) for part in (largest, total, picked)], axis=0)
    stats = gather_whole(stats, stats.shape[1], collective_ids[1], 20)
    peak = jnp.max(stats[:, :8], axis=0)
    log_own = peak + jnp.log(jnp.sum(stats[:, 8:16] * jnp.exp(stats[:, :8] - peak), axis=0))
    token_logp = (jnp.sum(stats[:, 16:], axis=0) - log_own).reshape(-1)
    return (token_logp, log_own.reshape(-1), logits, hot, all_rows)


def forward(token_rows, enc_full, dec_full_after, gain_rows, batch_data, streamed=False):
    (
        prompt_ids,
        decoder_input,
        targets,
        enc_allowed,
        self_allowed,
        cross_allowed,
        pair_local,
        valid,
    ) = batch_data
    pairs_here, seat_count = (prompt_ids.shape[0], decoder_input.shape[0])
    prompt_count = prompt_ids.size
    encoder_input = token_rows[:prompt_count].astype(jnp.float32)
    encoder_one, encoder_attn = self_forward(
        encoder_input,
        gain_rows[0],
        columns(enc_full, 0, 3 * D),
        columns(enc_full, 3 * D, D),
        enc_allowed,
        (pairs_here, P_MAX),
    )
    encoder_two, encoder_ffn = feed(encoder_one, gain_rows[1], enc_full, 12 * D, streamed)
    encoder_final = to_low(rms_norm(encoder_two, gain_rows[2]))
    cross_memory = to_low(matmul(encoder_final, columns(enc_full, 9 * D, 2 * D))).reshape(
        pairs_here, P_MAX, 2 * D
    )
    layer_full = dec_full_after(cross_memory)
    decoder_zero = token_rows[prompt_count:].astype(jnp.float32)
    decoder_one, decoder_attn = self_forward(
        decoder_zero,
        gain_rows[3],
        columns(layer_full, 4 * D, 3 * D),
        columns(layer_full, 7 * D, D),
        self_allowed,
        (seat_count, R_MAX),
    )
    decoder_two, decoder_cross = cross_forward(
        decoder_one,
        gain_rows[4],
        columns(layer_full, 8 * D, D),
        columns(layer_full, 11 * D, D),
        cross_memory,
        pair_local,
        cross_allowed,
        (seat_count, R_MAX),
    )
    decoder_three, decoder_ffn = feed(
        decoder_two, gain_rows[5], layer_full, 12 * D + 2 * FF, streamed
    )
    final_rows = to_low(final_norm(decoder_three, gain_rows[6]))
    stored = (
        encoder_input,
        encoder_one,
        encoder_two,
        encoder_attn,
        encoder_ffn,
        encoder_final,
        decoder_zero,
        decoder_one,
        decoder_two,
        decoder_three,
        decoder_attn,
        decoder_cross,
        decoder_ffn,
    )
    return (final_rows, stored)


def decoder_backward(layer_full, gain_rows, batch_data, stored, grad_final):
    enc_allowed, self_allowed, cross_allowed = batch_data[3:6]
    decoder_zero, decoder_one, decoder_two, decoder_three = stored[6:10]
    decoder_attn, decoder_cross, decoder_ffn = stored[10:]
    grad_three, gain_six = norm_backward(final_norm, decoder_three, gain_rows[6], grad_final)
    grad_two, gain_five, dec_ffn_pairs = feed_backward(
        decoder_two,
        gain_rows[5],
        columns(layer_full, 12 * D + 2 * FF, FF),
        columns(layer_full, 12 * D + 3 * FF, FF),
        decoder_ffn,
        grad_three,
    )
    grad_one, gain_four, grad_memory, cross_pairs = cross_backward(
        decoder_one,
        gain_rows[4],
        columns(layer_full, 8 * D, D),
        columns(layer_full, 11 * D, D),
        cross_allowed,
        decoder_cross,
        grad_two,
    )
    grad_zero, gain_three, dec_self_pairs = self_backward(
        decoder_zero,
        gain_rows[3],
        columns(layer_full, 4 * D, 3 * D),
        columns(layer_full, 7 * D, D),
        self_allowed,
        decoder_attn,
        grad_one,
    )
    return (
        (gain_three, gain_four, gain_five, gain_six),
        dec_self_pairs + cross_pairs + dec_ffn_pairs,
        grad_memory,
        grad_zero,
    )


def encoder_backward(layer_full, gain_rows, batch_data, stored, memory_low):
    enc_allowed = batch_data[3]
    encoder_input, encoder_one, encoder_two, encoder_attn, encoder_ffn, encoder_final = stored[:6]
    grad_encoder_final = matmul_back(memory_low, columns(layer_full, 9 * D, 2 * D))
    grad_encoder_two, gain_two = norm_backward(
        rms_norm, encoder_two, gain_rows[2], grad_encoder_final
    )
    grad_encoder_one, gain_one, enc_ffn_pairs = feed_backward(
        encoder_one,
        gain_rows[1],
        columns(layer_full, 12 * D, FF),
        columns(layer_full, 12 * D + FF, FF),
        encoder_ffn,
        grad_encoder_two,
    )
    grad_encoder_input, gain_zero, enc_self_pairs = self_backward(
        encoder_input,
        gain_rows[0],
        columns(layer_full, 0, 3 * D),
        columns(layer_full, 3 * D, D),
        enc_allowed,
        encoder_attn,
        grad_encoder_one,
    )
    pairs = enc_self_pairs + ((encoder_final, memory_low),) + enc_ffn_pairs
    return ((gain_zero, gain_one, gain_two), pairs, grad_encoder_input)


def apply_update(weight, moment, average, gradient, factor):
    clipped = gradient * factor
    moment_new = MOMENTUM * moment + clipped
    step_size = -LEARN_RATE * (clipped + MOMENTUM * moment_new)
    weight_new = weight + step_size
    return (
        weight_new,
        moment_new,
        AVERAGE_DECAY * average + (1.0 - AVERAGE_DECAY) * weight_new,
        step_size,
    )


def body(
    prompt_ids,
    prompt_lengths,
    response_ids,
    response_lengths,
    sequence_pair,
    chosen_flag,
    pair_microbatch,
    policy_embed,
    policy_layers,
    policy_gains,
    momentum_embed,
    momentum_layers,
    momentum_gains,
    average_embed,
    average_layers,
    average_gains,
    frozen_embed,
    frozen_layers,
    frozen_gains,
):
    n_dev = lax.axis_size(AXES)
    me = lax.axis_index(AXES)
    rows_here = policy_embed.shape[0]
    pairs_here = prompt_ids.shape[0]
    seat_count = response_ids.shape[0]
    decoder_input = jnp.concatenate(
        [jnp.zeros((seat_count, 1), jnp.int32), response_ids[:, :-1]], axis=1
    )
    pair_local = sequence_pair - me * pairs_here
    select_float = (pair_local[:, None] == jnp.arange(pairs_here)[None, :]).astype(jnp.float32)
    prompt_pos = jnp.arange(P_MAX)
    reply_pos = jnp.arange(R_MAX)
    prompt_keys = prompt_pos[None, :] < prompt_lengths[:, None]
    valid = reply_pos[None, :] < response_lengths[:, None]
    enc_allowed = jnp.broadcast_to(prompt_keys[:, None, :], (pairs_here, P_MAX, P_MAX))
    self_allowed = (reply_pos[:, None] >= reply_pos[None, :])[None] & valid[:, None, :]
    seat_keys = jnp.einsum("sp,pk->sk", select_float, prompt_keys.astype(jnp.float32)) > 0.5
    cross_allowed = jnp.broadcast_to(seat_keys[:, None, :], (seat_count, R_MAX, P_MAX))
    batch_data = (
        prompt_ids,
        decoder_input,
        response_ids,
        enc_allowed,
        self_allowed,
        cross_allowed,
        pair_local,
        valid,
    )
    token_ids = jnp.concatenate([prompt_ids.reshape(-1), decoder_input.reshape(-1)])
    token_live = jnp.concatenate([prompt_keys.reshape(-1), valid.reshape(-1)])
    plan = lookup_plan(token_ids, token_live, rows_here)
    packed = jnp.concatenate(
        [
            round_requests(plan, 0, n_dev),
            response_ids.reshape(-1),
            response_lengths,
            pair_local,
            chosen_flag,
            pair_microbatch,
            plan[5][None],
        ]
    )
    packed = jnp.pad(packed, (0, -packed.shape[0] % 1024)).reshape(8, -1)
    *policy_enc, notes = tree_gather(
        to_low(policy_layers), ENC_BLOCKS, D, 1, 115, extra=packed
    )
    notes = notes.reshape(n_dev, -1)
    asked = mine_of(notes)
    at = n_dev * SLOTS
    cuts = []
    for width in (seat_count * R_MAX, seat_count, seat_count, seat_count, pairs_here, 1):
        cuts.append(notes[:, at : at + width])
        at += width
    targets, all_lengths, all_pair, all_flag, all_micro, all_rounds = cuts
    targets = targets.reshape(-1)
    rounds = jnp.max(all_rounds)
    all_select = (all_pair[:, :, None] == jnp.arange(pairs_here)).astype(jnp.float32)
    pair_micro = (all_micro[:, :, None] == jnp.arange(MICRO)).astype(jnp.float32)
    seat_micro = jnp.sum(all_select[:, :, :, None] * pair_micro[:, None], axis=2)
    chosen_float = all_flag.astype(jnp.float32)
    pair_total = jnp.sum(pair_micro, axis=(0, 1))
    token_total = jnp.sum(
        seat_micro * (chosen_float * all_lengths.astype(jnp.float32))[:, :, None], axis=(0, 1)
    )
    micro_counts = jnp.stack([pair_total, token_total])
    pair_divisor = jnp.sum(pair_micro * pair_total, axis=2)
    sequence_divisor = jnp.sum(seat_micro * token_total, axis=2)
    all_valid = reply_pos < all_lengths[:, :, None]

    policy_table = to_low(policy_embed)
    policy_low = to_low(after(policy_layers, policy_enc[0]))
    policy_dec = gather_offloaded(policy_low, DEC_BLOCKS)
    answers = answer(asked, (policy_table, frozen_embed))
    policy_tokens, frozen_tokens = fetch_rows(plan, answers, rounds, (policy_table, frozen_embed), n_dev)
    policy_layer_enc = by_column(ENC_BLOCKS, policy_enc)
    policy_layer_dec = split_blocks(policy_dec, DEC_BLOCKS)
    policy_layer_full = policy_layer_enc | policy_layer_dec
    def policy_after(memory):
        return policy_layer_dec

    def logp_of(token_logp):
        return jnp.sum(jnp.where(all_valid, token_logp.reshape(all_valid.shape), 0.0), axis=2)

    policy_rows, stored = forward(
        policy_tokens, policy_layer_enc, policy_after, policy_gains, batch_data
    )
    frozen_enc = gather_offloaded(after(frozen_layers, stored[5]), ENC_BLOCKS)
    frozen_dec = gather_offloaded(after(frozen_layers, policy_rows), DEC_BLOCKS)
    frozen_layer_enc = split_blocks(frozen_enc, ENC_BLOCKS)

    def frozen_after(memory):
        return split_blocks(after(frozen_dec, memory), DEC_BLOCKS)

    token_logp, log_own, logits, hot, all_rows = shard_stats(
        policy_rows, policy_table, targets, (3, 4)
    )
    policy_logp = logp_of(token_logp)
    row_slope = jnp.where(
        all_valid.reshape(-1)[:, None], hot.astype(jnp.float32) - jnp.exp(logits - log_own[:, None]), 0.0
    )
    row_slope = with_layout_constraint(to_low(row_slope), Layout(major_to_minor=(0, 1)))
    grad_final = scatter_final(row_slope, policy_table, 10)
    dec_gains, dec_pairs, grad_memory, grad_zero = decoder_backward(
        policy_layer_full, policy_gains, batch_data, stored, grad_final
    )
    frozen_inputs = after(frozen_tokens, grad_zero)
    frozen_rows, unused = forward(
        frozen_inputs, frozen_layer_enc, frozen_after, frozen_gains, batch_data, True
    )
    frozen_logp = logp_of(shard_stats(frozen_rows, frozen_embed, targets, (5, 6))[0])
    frozen_mean = lax.dynamic_index_in_dim(
        frozen_logp / all_lengths.astype(jnp.float32), me, 0, keepdims=False
    )

    sign_value = 2.0 * chosen_float - 1.0
    margin = PREFERENCE_BETA * jnp.sum(
        all_select * (sign_value * (policy_logp - frozen_logp))[:, :, None], axis=1
    )
    loss = (
        jnp.sum(jax.nn.softplus(-margin) / pair_divisor)
        - CHOSEN_WEIGHT * jnp.sum(chosen_float * policy_logp / sequence_divisor)
    ) / MICRO
    pair_slope = -PREFERENCE_BETA * jax.nn.sigmoid(-margin) / pair_divisor
    sequence_slope = (
        sign_value * jnp.sum(all_select * pair_slope[:, None, :], axis=2)
        - CHOSEN_WEIGHT * chosen_float / sequence_divisor
    ) / MICRO
    slope_here = lax.dynamic_index_in_dim(sequence_slope, me, 0, keepdims=False)
    slope_rows = jnp.repeat(slope_here, R_MAX)[:, None]
    memory_slope = (select_float * slope_here[:, None])[:, :, None, None, None]
    memory_low = jnp.concatenate(
        [
            join_heads(to_low(jnp.sum(memory_slope * part[:, None], axis=0))).reshape(-1, D)
            for part in grad_memory
        ],
        axis=1,
    )
    enc_gains, enc_pairs, grad_encoder_input = encoder_backward(
        policy_layer_full, policy_gains, batch_data, stored, memory_low
    )
    gain_grads = jnp.stack(
        [jnp.sum(rows, axis=0) for rows in enc_gains]
        + [jnp.sum(slope_rows * rows, axis=0) for rows in dec_gains]
    )
    token_gradient = jnp.concatenate([grad_encoder_input, slope_rows * grad_zero], axis=0)
    enc_pairs = [(to_low(left), to_low(right)) for left, right in enc_pairs]
    scaled_pairs = []
    for left, right in dec_pairs:
        if left.dtype == jnp.float32:
            scaled_pairs.append((to_low(slope_rows * left), right))
        else:
            scaled_pairs.append((left, to_low(slope_rows * right)))
    token_gradient = to_low(token_gradient)
    first_sums = row_sums(picking(plan, 0, n_dev), token_gradient)
    late_slope = after(sequence_slope, first_sums)
    table_grad = jnp.einsum(
        "rc,rd->cd",
        row_slope,
        to_low(jnp.repeat(late_slope.reshape(-1), R_MAX)[:, None] * all_rows),
        preferred_element_type=jnp.float32,
    )
    table_grad = after(table_grad, first_sums)
    enc_pairs[0] = (after(enc_pairs[0][0], first_sums, table_grad), enc_pairs[0][1])
    embed_grad = return_rows(plan, asked, rounds, first_sums, token_gradient, table_grad, n_dev)
    layer_grad = scatter_layers(scaled_pairs, enc_pairs, policy_layers.shape[0], 8)
    squares_local = jnp.sum(embed_grad * embed_grad) + jnp.sum(layer_grad * layer_grad)
    shared = total_of(jnp.concatenate([gain_grads, jnp.full((1, D), squares_local)], axis=0), 9)
    gain_total, squares_total = (shared[:7], shared[7, 0])
    grad_norm = jnp.sqrt(squares_total + jnp.sum(gain_total * gain_total))
    factor = jnp.minimum(1.0, CLIP_NORM / grad_norm)
    embed_new = apply_update(policy_embed, momentum_embed, average_embed, embed_grad, factor)
    layers_new = apply_update(policy_layers, momentum_layers, average_layers, layer_grad, factor)
    gains_new = apply_update(policy_gains, momentum_gains, average_gains, gain_total, factor)
    return (
        loss,
        grad_norm,
        micro_counts,
        frozen_mean,
        embed_new[3],
        layers_new[0],
        gains_new[0],
        embed_new[1],
        layers_new[1],
        gains_new[1],
        embed_new[2],
        layers_new[2],
        gains_new[2],
    )


def solution(mesh):
    placed = (
        P(("dp", "fsdp"), None),
        P(("dp", "fsdp")),
        P(("dp", "fsdp"), None),
        P(("dp", "fsdp")),
        P(("dp", "fsdp")),
        P(("dp", "fsdp")),
        P(("dp", "fsdp")),
        P(("dp", "fsdp"), None),
        P(("dp", "fsdp"), None),
        P(),
        P(("dp", "fsdp"), None),
        P(("dp", "fsdp"), None),
        P(),
        P(("dp", "fsdp"), None),
        P(("dp", "fsdp"), None),
        P(),
        P(("dp", "fsdp"), None),
        P(("dp", "fsdp"), None),
        P(),
    )
    return jax.shard_map(
        body,
        mesh=mesh,
        in_specs=placed,
        out_specs=(
            P(),
            P(),
            P(),
            P(("dp", "fsdp")),
            P(("dp", "fsdp"), None),
            P(("dp", "fsdp"), None),
            P(),
            P(("dp", "fsdp"), None),
            P(("dp", "fsdp"), None),
            P(),
            P(("dp", "fsdp"), None),
            P(("dp", "fsdp"), None),
            P(),
        ),
        check_vma=False,
    )
```
